32 devices in a mesh: img: 4 (over x, core), vol: 8 (over z, y).
Axes of the slice: x: 2, y: 2, z: 4, core: 2. Of those that a mesh axis runs over, the one named last changes fastest.
Arguments:
- images: bfloat16 [2, 1536, 256, 128], P(None, 'img', 'vol'), may hold values from -6 to 6
- defocus: float32 [1536], P('img'), may hold values from 20 to 200
- candidates: int32 [1536, 8], P('img'), may hold values from 0 to 63, all different within a row
- counts: int32 [1536], P('img'), may hold values from 1 to 8
- noise_weight: float32 [256, 128], P('vol'), may hold values from 0.002 to 0.02
- volume: float32 [2, 256, 256, 128], P(None, 'vol'), may hold values from -6 to 6
- row_plane: int32 [64, 256], replicated, may hold values from 0 to 255
- row_line: int32 [64, 256], replicated, may hold values from 0 to 254
- row_weight: float32 [64, 256], replicated, may hold values from 0 to 1
- regularizer: float32 [256, 256, 128], P('vol', 'img'), may hold values from 0.05 to 0.5
Outputs:
- new_volume: float32 [2, 256, 256, 128], P(None, 'vol', 'img')
The draws below stay inside these ranges and needn't reach their ends.
Inputs may be any that keep to these rules, and one draw needn't show every extreme that they name: The entries of one row of candidates are distinct; only the first counts entries are used.
All inputs are finite; a program needn't handle non-finite values.
Results may differ from the reference program's by a relative error of at most 0.0066.
Values may be sent and summed in bfloat16 or wider, within the bound.
No kernel may reach another device: no remote copies, remote signals or barrier semaphores. Data moves between devices by JAX's collectives and lax.ppermute only.
A program may use at most 128 MiB of HBM per device.

```python
import math
import jax
import jax.numpy as jnp
from jax import lax

ROWS = 256
COLS = 128
K = 64
LMAX = 8
TRANS = 4
IMG_DEV = 384
IMAGES = 1536
N_IMG = 4


def draw_row_plane(key, part):
    slope = jax.random.randint(key, (K, 1), -(ROWS - 1), ROWS)
    row_ids = jnp.arange(ROWS).astype(jnp.int32)[None, :]
    return (ROWS // 2 + (row_ids - ROWS // 2) * slope // ROWS).astype(jnp.int32)


def place_ends(values, own_key, least, largest):
    spot = [jax.random.randint(jax.random.fold_in(own_key, axis), (), 0, length) for axis, length in enumerate(values.shape)]
    main_axis = values.shape.index(max(values.shape))
    neighbour = spot[:main_axis] + [(spot[main_axis] + 1) % values.shape[main_axis]] + spot[main_axis + 1:]
    return values.at[tuple(spot)].set(least).at[tuple(neighbour)].set(largest)


def levels(rng, extent, split, low, top_value):
    factor_of = 1.0
    for axis_at, shards_of in split:
        draws = jax.random.uniform(jax.random.fold_in(jax.random.fold_in(rng, 6), axis_at), (shards_of,), jnp.float32, low / len(split), top_value / len(split))
        factor_of = factor_of * jnp.repeat(jnp.exp(draws), extent[axis_at] // shards_of).reshape((-1,) + (1,) * (len(extent) - 1 - axis_at))
    return factor_of


def distinct(rng, rows, count, top, lift):
    ranking = jax.random.permutation(jax.random.fold_in(rng, 1), count)
    pull = ranking
    for power in range(3):
        pull = pull * pull // count
    pull = pull * lift // count
    chance = jax.random.randint(jax.random.fold_in(rng, 2), (rows, count), 0, 4096) + pull
    holders = jax.random.permutation(jax.random.fold_in(rng, 3), rows)[jnp.arange(count) % rows]
    chance = jnp.where(jnp.arange(rows)[:, None] == holders[None, :], 1 << 14, chance)
    score = chance * count + jnp.arange(count)
    return lax.top_k(score.astype(jnp.int32), top)[1].astype(jnp.int32)


def noise(rng, extent, spread, most, pieces=(), held_as=jnp.bfloat16):
    loudness = levels(rng, extent, pieces, -0.22, 0.18) if pieces else 1.0
    result = jax.random.normal(rng, extent, jnp.float32) * spread * loudness
    return jnp.minimum(jnp.maximum(result, -most), most).astype(held_as)


def setup_inputs(seed: int = 0) -> dict:
    key_list = jax.random.split(jax.random.key(seed), 11)
    images = noise(key_list[0], (2, IMAGES, ROWS, COLS), 1.0, 6.0, ((1, 4), (2, 8)))
    defocus = jnp.clip(20.0 + 180.0 * jax.random.uniform(key_list[1], (IMAGES,), jnp.float32) ** levels(key_list[1], (IMAGES,), ((0, 4),), -0.2, 0.2), 20.0, 200.0)
    candidates = distinct(key_list[2], IMAGES, K, LMAX, 2048)
    counts = place_ends(jax.random.randint(key_list[3], (IMAGES,), 1, LMAX + 1), jax.random.fold_in(key_list[3], 1), 1, LMAX).astype(jnp.int32)
    noise_weight = jnp.clip(jnp.exp(math.log(0.02) - 2.30258502 * jax.random.uniform(key_list[4], (ROWS, COLS), jnp.float32) ** levels(key_list[4], (ROWS, COLS), ((0, 8),), -0.2, 0.2)), 0.002, 0.02)
    volume = noise(key_list[5], (2, ROWS, ROWS, COLS), 1.0, 6.0, ((1, 8),), jnp.float32)
    row_plane = draw_row_plane(jax.random.fold_in(key_list[10], 71), 0)
    row_line = place_ends(jax.random.randint(key_list[7], (K, ROWS), 0, ROWS - 1), jax.random.fold_in(key_list[7], 1), 0, (ROWS - 1) - 1).astype(jnp.int32)
    row_weight = jnp.clip(jax.random.uniform(key_list[8], (K, ROWS), jnp.float32, 0.0, 1.0), 0.0, 1.0)
    regularizer = jnp.clip(jnp.exp(math.log(0.5) - 2.3025851 * jax.random.uniform(key_list[9], (ROWS, ROWS, COLS), jnp.float32) ** levels(key_list[9], (ROWS, ROWS, COLS), ((0, 8), (1, 4)), -0.2, 0.2)), 0.05, 0.5)
    return dict(images=images, defocus=defocus, candidates=candidates, counts=counts, noise_weight=noise_weight, volume=volume, row_plane=row_plane, row_line=row_line, row_weight=row_weight, regularizer=regularizer)


AMPLITUDE = 0.1

def contrast_of(defocus, row_freq, col_freq):
    radius_sq = row_freq[:, None] * row_freq[:, None] + col_freq[None, :] * col_freq[None, :]
    angle = defocus[:, None, None] * radius_sq[None]
    return -(math.sqrt(1.0 - AMPLITUDE * AMPLITUDE) * jnp.sin(angle) + AMPLITUDE * jnp.cos(angle))

def shift_phases(row_freq, col_freq, number):
    shift_ids = jnp.arange(number)
    shift_x = (shift_ids % 2).astype(jnp.float32) - 0.5
    shift_y = (shift_ids // 2).astype(jnp.float32) - 0.5
    angle = -2.0 * math.pi * (shift_x[:, None, None] * col_freq[None, None, :] + shift_y[:, None, None] * row_freq[None, :, None])
    return (jnp.cos(angle), jnp.sin(angle))

def make_references(slices, cosine, sine):
    real_part = slices[0].astype(jnp.float32)
    imag_part = slices[1].astype(jnp.float32)
    shift_re = cosine[:, None] * real_part[None] - sine[:, None] * imag_part[None]
    shift_im = sine[:, None] * real_part[None] + cosine[:, None] * imag_part[None]
    shifted = jnp.stack([shift_re, shift_im], axis=2).astype(jnp.bfloat16)
    power = (real_part * real_part + imag_part * imag_part).astype(jnp.bfloat16)
    return (shifted, power)

def posterior_of(logits, candidates, counts):
    orientation = jnp.arange(logits.shape[2]).astype(jnp.int32)
    in_list = jnp.arange(candidates.shape[1]).astype(jnp.int32)[None, :] < counts[:, None]
    listed = jnp.any((candidates[:, :, None] == orientation[None, None, :]) & in_list[:, :, None], axis=1)
    allowed = listed[:, None, :]
    masked = jnp.where(allowed, logits, -1e+30)
    highest = lax.optimization_barrier(jnp.max(masked, axis=(1, 2), keepdims=True))
    exponent = jnp.where(allowed, jnp.exp(masked - highest), 0.0)
    return (exponent / lax.optimization_barrier(jnp.sum(exponent, axis=(1, 2), keepdims=True))).astype(jnp.bfloat16)

def reference(images, defocus, candidates, counts, noise_weight, volume, row_plane, row_line, row_weight, regularizer):
    row_freq = (jnp.arange(ROWS).astype(jnp.float32) - ROWS // 2) / ROWS
    col_freq = jnp.arange(COLS).astype(jnp.float32) / (2 * COLS)
    flat = volume.reshape(2, ROWS * ROWS, COLS)
    line_index = row_plane * ROWS + row_line
    lower = jnp.take(flat, line_index, axis=1)
    upper = jnp.take(flat, line_index + 1, axis=1)
    weight = row_weight[None, :, :, None]
    slices = (weight * lower + (1.0 - weight) * upper).astype(jnp.bfloat16)
    cosine, sine = shift_phases(row_freq, col_freq, TRANS)
    shifted, power = make_references(slices, cosine, sine)
    shifted_f = shifted.astype(jnp.float32)
    power_f = power.astype(jnp.float32)

    def block_step(carry, block_id):
        begin = (block_id * IMG_DEV).astype(jnp.int32)
        image_block = lax.dynamic_slice_in_dim(images, begin, IMG_DEV, 1)
        defocus_block = lax.dynamic_slice_in_dim(defocus, begin, IMG_DEV, 0)
        cand_block = lax.dynamic_slice_in_dim(candidates, begin, IMG_DEV, 0)
        count_block = lax.dynamic_slice_in_dim(counts, begin, IMG_DEV, 0)
        contrast = contrast_of(defocus_block, row_freq, col_freq)
        weighted = ((contrast * noise_weight)[None] * image_block).astype(jnp.bfloat16)
        squared = (contrast * contrast * noise_weight).astype(jnp.bfloat16)
        weighted_f = weighted.astype(jnp.float32)
        squared_f = squared.astype(jnp.float32)
        cross = jnp.einsum('jbrc,tkjrc->btk', weighted_f, shifted_f)
        quadratic = jnp.einsum('brc,krc->bk', squared_f, power_f)
        weights = posterior_of(cross - 0.5 * quadratic[:, None, :], cand_block, count_block).astype(jnp.float32)
        y_sum = carry[0] + jnp.einsum('btk,jbrc->tkrjc', weights, weighted_f)
        d_sum = carry[1] + jnp.einsum('btk,brc->tkrc', weights, squared_f)
        return ((y_sum, d_sum), None)
    start = (jnp.zeros((TRANS, K, ROWS, 2, COLS), jnp.float32), jnp.zeros((TRANS, K, ROWS, COLS), jnp.float32))
    (y_sum, d_sum), unused = lax.scan(block_step, start, jnp.arange(N_IMG).astype(jnp.int32))
    num_re = lax.optimization_barrier(jnp.sum(cosine[:, None] * y_sum[:, :, :, 0] + sine[:, None] * y_sum[:, :, :, 1], axis=0))
    num_im = lax.optimization_barrier(jnp.sum(cosine[:, None] * y_sum[:, :, :, 1] - sine[:, None] * y_sum[:, :, :, 0], axis=0))
    den = lax.optimization_barrier(jnp.sum(d_sum, axis=0))
    values = jnp.stack([num_re, num_im, den], axis=2).reshape(K * ROWS, 3 * COLS)
    flat_index = line_index.reshape(-1)
    flat_weight = row_weight.reshape(-1, 1)
    accum = jnp.zeros((ROWS * ROWS, 3 * COLS), jnp.float32)
    accum = accum.at[flat_index].add(flat_weight * values)
    accum = accum.at[flat_index + 1].add((1.0 - flat_weight) * values)
    accum = accum.reshape(ROWS, ROWS, 3, COLS)
    denom = accum[:, :, 2] + regularizer
    return jnp.stack([accum[:, :, 0] / denom, accum[:, :, 1] / denom], axis=0)
```

```python
import math
from functools import partial

import jax
import jax.numpy as jnp
from jax import lax
from jax.experimental import pallas as pl
from jax.experimental.pallas import tpu as pltpu
from jax.sharding import PartitionSpec as P

ROWS = 256
COLS = 128
K = 64
TRANS = 4
LMAX = 8
AMPLITUDE = 0.1
VMEM_LIMIT = 56 * 1024 * 1024
BF16 = jnp.bfloat16
F32 = jnp.float32


def params(steps):
    return pltpu.CompilerParams(
        dimension_semantics=("arbitrary",) * steps, vmem_limit_bytes=VMEM_LIMIT
    )


def smem():
    return pl.BlockSpec(memory_space=pltpu.SMEM)


def vmem():
    return pl.BlockSpec(memory_space=pltpu.VMEM)


def shift_phases(row_freq, col_freq, number):
    shift_ids = jnp.arange(number)
    shift_x = (shift_ids % 2).astype(F32) - 0.5
    shift_y = (shift_ids // 2).astype(F32) - 0.5
    angle = (
        -2.0
        * math.pi
        * (
            shift_x[:, None, None] * col_freq[None, None, :]
            + shift_y[:, None, None] * row_freq[None, :, None]
        )
    )
    return (jnp.cos(angle), jnp.sin(angle))


def extract_kernel(idx_s, flag_s, vol_ref, w_ref, out_ref, pair):
    blocks = out_ref.shape[0]
    groups = out_ref.shape[2] // 16

    def block_step(blk, carry):
        def group_step(g, inner):
            at = blk * groups + g
            base = pl.multiple_of(g * 16, 16)

            @pl.when(flag_s[at] > 0)
            def _():
                for u in range(16):
                    i = idx_s[at * 16 + u]
                    pair[0, 2 * u : 2 * u + 2, :] = vol_ref[0, pl.ds(i, 2), :]
                    pair[1, 2 * u : 2 * u + 2, :] = vol_ref[1, pl.ds(i, 2), :]
                w = jnp.broadcast_to(w_ref[pl.ds(pl.multiple_of(at * 16, 16), 16), :], (16, COLS))
                for j in range(2):
                    lower = pair[j, pl.ds(0, 16, stride=2), :]
                    upper = pair[j, pl.ds(1, 16, stride=2), :]
                    value = jnp.where(w >= 0.0, w * lower + (1.0 - w) * upper, 0.0)
                    out_ref[blk, j, pl.ds(base, 16), :] = value.astype(BF16)

            @pl.when(flag_s[at] == 0)
            def _():
                for j in range(2):
                    out_ref[blk, j, pl.ds(base, 16), :] = jnp.zeros((16, COLS), BF16)

            return inner

        return lax.fori_loop(0, groups, group_step, carry)

    lax.fori_loop(0, blocks, block_step, 0)


def extract(volume, planes, lines, weights, slab_id, n_vol):
    share = planes.shape[0]
    planes_here = volume.shape[1]
    rows = ROWS // n_vol

    def order(x):
        return x.reshape(share, n_vol, rows).transpose(1, 0, 2).reshape(-1)

    local = order(planes) - slab_id * planes_here
    owned = (local >= 0) & (local < planes_here)
    idx = jnp.where(owned, local, 0) * ROWS + order(lines)
    w = jnp.where(owned, order(weights), -1.0)[:, None]
    flag = jnp.any(owned.reshape(-1, 16), axis=1).astype(jnp.int32)
    return pl.pallas_call(
        extract_kernel,
        out_shape=jax.ShapeDtypeStruct((n_vol, 2, share * rows, COLS), BF16),
        in_specs=[smem(), smem(), vmem(), vmem()],
        out_specs=vmem(),
        scratch_shapes=[pltpu.VMEM((2, 32, COLS), F32)],
        compiler_params=pltpu.CompilerParams(vmem_limit_bytes=VMEM_LIMIT),
        name="extract",
    )(idx, flag, volume.reshape(2, planes_here * ROWS, COLS), w)


def weigh_kernel(img_ref, sa_ref, ca_ref, sx_ref, cx_ref, nw_ref, wt_ref, sq_ref, buf):
    count = img_ref.shape[1]
    rows = img_ref.shape[2]
    for j in range(2):
        buf[j] = img_ref[j].astype(F32).reshape(count * rows, COLS)
    sx = sx_ref[...]
    cx = cx_ref[...]
    for r in range(rows):
        contrast = -(sa_ref[:, r : r + 1] * cx + ca_ref[:, r : r + 1] * sx)
        noise = nw_ref[r : r + 1, :]
        scale = contrast * noise
        for j in range(2):
            x = buf[j, pl.ds(r, count, stride=rows), :]
            wt_ref[r, :, j * COLS : (j + 1) * COLS] = (scale * x).astype(BF16)
        sq_ref[r] = (contrast * contrast * noise).astype(BF16)


def weigh(images, defocus, noise_weight, row_freq, col_freq):
    count = images.shape[1]
    rows = images.shape[2]
    step = 64
    angle_r = defocus[:, None] * (row_freq * row_freq)[None, :] + math.asin(AMPLITUDE)
    angle_c = defocus[:, None] * (col_freq * col_freq)[None, :]
    return pl.pallas_call(
        weigh_kernel,
        grid=(count // step,),
        out_shape=[
            jax.ShapeDtypeStruct((rows, count, 2 * COLS), BF16),
            jax.ShapeDtypeStruct((rows, count, COLS), BF16),
        ],
        in_specs=[
            pl.BlockSpec((2, step, rows, COLS), lambda b: (0, b, 0, 0)),
            pl.BlockSpec((step, rows), lambda b: (b, 0)),
            pl.BlockSpec((step, rows), lambda b: (b, 0)),
            pl.BlockSpec((step, COLS), lambda b: (b, 0)),
            pl.BlockSpec((step, COLS), lambda b: (b, 0)),
            pl.BlockSpec((rows, COLS), lambda b: (0, 0)),
        ],
        out_specs=[
            pl.BlockSpec((rows, step, 2 * COLS), lambda b: (0, b, 0)),
            pl.BlockSpec((rows, step, COLS), lambda b: (0, b, 0)),
        ],
        scratch_shapes=[pltpu.VMEM((2, step * rows, COLS), F32)],
        compiler_params=params(1),
        name="weigh",
    )(
        images,
        jnp.sin(angle_r),
        jnp.cos(angle_r),
        jnp.sin(angle_c),
        jnp.cos(angle_c),
        noise_weight,
    )


def logits_kernel(sl_ref, wt_ref, sq_ref, cos_ref, sin_ref, cand_ref, out_ref, part, acc, quad):
    step = pl.program_id(0)
    groups = sl_ref.shape[0]
    span = sl_ref.shape[2]
    rows = groups * span // K
    inner = wt_ref.shape[0]

    @pl.when(step == 0)
    def _():
        for i in range(groups):
            for j in range(2):
                part[j, i * span : (i + 1) * span, :] = sl_ref[i, j].astype(F32)
        acc[...] = jnp.zeros_like(acc)
        quad[...] = jnp.zeros_like(quad)

    dims = (((1,), (1,)), ((), ()))
    total = acc[...]
    total_q = quad[...]
    for u in range(inner):
        re = part[0, pl.ds(step * inner + u, K, stride=rows), :]
        im = part[1, pl.ds(step * inner + u, K, stride=rows), :]
        shifted = []
        for t in range(TRANS):
            c = cos_ref[t, u : u + 1, :]
            s = sin_ref[t, u : u + 1, :]
            shifted.append(
                jnp.concatenate(
                    [(c * re - s * im).astype(BF16), (s * re + c * im).astype(BF16)], axis=1
                )
            )
        left = jnp.concatenate(shifted, axis=0)
        power = (re * re + im * im).astype(BF16)
        total = total + lax.dot_general(left, wt_ref[u], dims, preferred_element_type=F32)
        total_q = total_q + lax.dot_general(power, sq_ref[u], dims, preferred_element_type=F32)
    acc[...] = total
    quad[...] = total_q

    @pl.when(step == pl.num_programs(0) - 1)
    def _():
        ids = lax.broadcasted_iota(jnp.int32, quad.shape, 0)
        half = 0.5 * quad[...]
        for t in range(TRANS):
            value = acc[t * K : (t + 1) * K, :] - half
            for l in range(LMAX):
                pick = jnp.where(ids == cand_ref[l : l + 1, :], value, 0.0)
                out_ref[t * LMAX + l : t * LMAX + l + 1, :] = jnp.sum(pick, axis=0, keepdims=True)


def candidate_logits(slices, weighted, squared, cosine, sine, cand):
    rows, count = squared.shape[:2]
    inner = 8
    return pl.pallas_call(
        logits_kernel,
        grid=(rows // inner,),
        out_shape=jax.ShapeDtypeStruct((TRANS * LMAX, count), F32),
        in_specs=[
            pl.BlockSpec(slices.shape, lambda s: (0, 0, 0, 0)),
            pl.BlockSpec((inner, count, 2 * COLS), lambda s: (s, 0, 0)),
            pl.BlockSpec((inner, count, COLS), lambda s: (s, 0, 0)),
            pl.BlockSpec((TRANS, inner, COLS), lambda s: (0, s, 0)),
            pl.BlockSpec((TRANS, inner, COLS), lambda s: (0, s, 0)),
            pl.BlockSpec((LMAX, count), lambda s: (0, 0)),
        ],
        out_specs=pl.BlockSpec((TRANS * LMAX, count), lambda s: (0, 0)),
        scratch_shapes=[
            pltpu.VMEM((2, K * rows, COLS), F32),
            pltpu.VMEM((TRANS * K, count), F32),
            pltpu.VMEM((K, count), F32),
        ],
        compiler_params=params(1),
        name="logits",
    )(slices, weighted, squared, cosine, sine, cand)


def posterior_rows(logits, counts):
    place = lax.broadcasted_iota(jnp.int32, logits.shape, 0) % LMAX
    allowed = place < counts
    masked = jnp.where(allowed, logits, -1e30)
    highest = jnp.max(masked, axis=0, keepdims=True)
    exponent = jnp.where(allowed, jnp.exp(masked - highest), 0.0)
    return (exponent / jnp.sum(exponent, axis=0, keepdims=True)).astype(BF16).astype(F32)


def project_kernel(
    src_s, len_s, lg_ref, cand_ref, cnt_ref, wt_ref, sq_ref, cos_ref, sin_ref,
    out_ref, post, post_sum, num, pick,
):
    step = pl.program_id(0)
    inner = wt_ref.shape[0]
    parts = out_ref.shape[0]
    cap = out_ref.shape[2]

    @pl.when(step == 0)
    def _():
        prob = posterior_rows(lg_ref[...], cnt_ref[...])
        ids = lax.broadcasted_iota(jnp.int32, (K, prob.shape[1]), 0)
        total = jnp.zeros((K, prob.shape[1]), F32)
        for t in range(TRANS):
            dense = jnp.zeros((K, prob.shape[1]), F32)
            for l in range(LMAX):
                at = t * LMAX + l
                dense = jnp.where(ids == cand_ref[l : l + 1, :], dense + prob[at : at + 1, :], dense)
            post[t * K : (t + 1) * K, :] = dense.astype(BF16)
            total = total + dense
        high = total.astype(BF16)
        post_sum[:K, :] = high
        post_sum[K:, :] = (total - high.astype(F32)).astype(BF16)

    for u in range(inner):
        y = jnp.dot(post[...], wt_ref[u], preferred_element_type=F32)
        d = jnp.dot(post_sum[...], sq_ref[u], preferred_element_type=F32)
        re = jnp.zeros((K, COLS), F32)
        im = jnp.zeros((K, COLS), F32)
        for t in range(TRANS):
            c = cos_ref[t, u : u + 1, :]
            s = sin_ref[t, u : u + 1, :]
            y_re = y[t * K : (t + 1) * K, :COLS]
            y_im = y[t * K : (t + 1) * K, COLS:]
            re = re + (c * y_re + s * y_im)
            im = im + (c * y_im - s * y_re)
        base = pl.multiple_of((step * inner + u) * K, K)
        num[0, pl.ds(base, K), :] = re
        num[1, pl.ds(base, K), :] = im
        num[2, pl.ds(base, K), :] = d[:K] + d[K:]

    @pl.when(step == pl.num_programs(0) - 1)
    def _():
        for q in range(parts):

            def group_step(g, carry):
                base = pl.multiple_of(g * 16, 16)
                for u in range(16):
                    s = src_s[q * cap + base + u]
                    for c in range(3):
                        pick[c, u : u + 1, :] = num[c, pl.ds(s, 1), :]
                for c in range(3):
                    out_ref[q, c, pl.ds(base, 16), :] = pick[c].astype(BF16)
                return carry

            lax.fori_loop(0, (len_s[q] + 15) // 16, group_step, 0)


def project(src, lengths, logits, cand, counts, weighted, squared, cosine, sine, parts, cap):
    rows, count = squared.shape[:2]
    inner = 8
    return pl.pallas_call(
        project_kernel,
        grid=(rows // inner,),
        out_shape=jax.ShapeDtypeStruct((parts, 3, cap, COLS), BF16),
        in_specs=[
            smem(),
            smem(),
            pl.BlockSpec((TRANS * LMAX, count), lambda s: (0, 0)),
            pl.BlockSpec((LMAX, count), lambda s: (0, 0)),
            pl.BlockSpec((1, count), lambda s: (0, 0)),
            pl.BlockSpec((inner, count, 2 * COLS), lambda s: (s, 0, 0)),
            pl.BlockSpec((inner, count, COLS), lambda s: (s, 0, 0)),
            pl.BlockSpec((TRANS, inner, COLS), lambda s: (0, s, 0)),
            pl.BlockSpec((TRANS, inner, COLS), lambda s: (0, s, 0)),
        ],
        out_specs=pl.BlockSpec((parts, 3, cap, COLS), lambda s: (0, 0, 0, 0)),
        scratch_shapes=[
            pltpu.VMEM((TRANS * K, count), BF16),
            pltpu.VMEM((2 * K, count), BF16),
            pltpu.VMEM((3, rows * K, COLS), F32),
            pltpu.VMEM((3, 16, COLS), F32),
        ],
        compiler_params=params(1),
        name="project",
    )(src, lengths, logits, cand, counts, weighted, squared, cosine, sine)


HEAD = 8


def line_stride(lines_here):
    return lines_here + 2 * HEAD


def insert_kernel(len_s, pos_s, at_s, wgt_s, rows_ref, reg_ref, out_ref, acc, buf):
    step = pl.program_id(0)
    cap = rows_ref.shape[2]
    planes, lines_here = reg_ref.shape[:2]
    stride = line_stride(lines_here)

    @pl.when(step == 0)
    def _():
        acc[...] = jnp.zeros_like(acc)

    for c in range(3):
        buf[c] = rows_ref[0, c].astype(F32)
    first = lax.broadcasted_iota(jnp.int32, (2, COLS), 0) == 0

    def group_step(g, carry):
        for u in range(4):
            e = step * cap + g * 4 + u
            s = pos_s[e]
            to = at_s[e]
            w = wgt_s[e]
            both = jnp.where(first, w, 1.0 - w)
            for c in range(3):
                row = jnp.broadcast_to(buf[c, pl.ds(s, 1), :], (2, COLS))
                acc[c, pl.ds(to, 2), :] = acc[c, pl.ds(to, 2), :] + both * row
        return carry

    lax.fori_loop(0, (len_s[step] + 3) // 4, group_step, 0)

    @pl.when(step == pl.num_programs(0) - 1)
    def _():
        def plane_step(p, carry):
            base = pl.multiple_of(p * stride + HEAD, 8)
            inv = 1.0 / (acc[2, pl.ds(base, lines_here), :] + reg_ref[p])
            out_ref[0, p] = acc[0, pl.ds(base, lines_here), :] * inv
            out_ref[1, p] = acc[1, pl.ds(base, lines_here), :] * inv
            return carry

        lax.fori_loop(0, planes, plane_step, 0)


def insert(lengths, positions, targets, weights, received, regularizer):
    blocks, _, cap, _ = received.shape
    planes, lines_here = regularizer.shape[:2]
    return pl.pallas_call(
        insert_kernel,
        grid=(blocks,),
        out_shape=jax.ShapeDtypeStruct((2, planes, lines_here, COLS), F32),
        in_specs=[
            smem(),
            smem(),
            smem(),
            smem(),
            pl.BlockSpec((1, 3, cap, COLS), lambda s: (s, 0, 0, 0)),
            pl.BlockSpec((planes, lines_here, COLS), lambda s: (0, 0, 0)),
        ],
        out_specs=pl.BlockSpec((2, planes, lines_here, COLS), lambda s: (0, 0, 0, 0)),
        scratch_shapes=[
            pltpu.VMEM((3, planes * line_stride(lines_here), COLS), F32),
            pltpu.VMEM((3, cap, COLS), F32),
        ],
        compiler_params=params(1),
        name="insert",
    )(lengths, positions, targets, weights, received, regularizer)


def ranks(member, rows):
    x = member.reshape(-1, rows, K).astype(F32)
    before_k = (jnp.arange(K)[:, None] < jnp.arange(K)[None, :]).astype(F32)
    before_r = (jnp.arange(rows)[:, None] < jnp.arange(rows)[None, :]).astype(F32)
    inner = jnp.einsum("xrk,kl->xrl", x, before_k, preferred_element_type=F32)
    outer = jnp.einsum("xr,rs->xs", jnp.sum(x, axis=2), before_r, preferred_element_type=F32)
    return (inner + outer[:, :, None]).reshape(member.shape).astype(jnp.int32)


def compact(member, rank, values, cap):
    high = jnp.where(member, rank // 32, -1)
    low = rank % 32
    left = (high[:, :, None] == jnp.arange(cap // 32)).astype(F32)
    hot = low[:, None, None, :] == jnp.arange(32)[None, None, :, None]
    right = jnp.where(hot, values[:, :, None, :], 0.0)
    out = jnp.einsum("xnh,xvln->xvhl", left, right, precision=lax.Precision.HIGHEST)
    return out.reshape(values.shape[0], values.shape[1], cap)


def insert_into(carry, piece, planes_all, lines_all, weights_all, slab_id, planes_here):
    local_plane = planes_all - slab_id * planes_here
    in_slab = (local_plane >= 0) & (local_plane < planes_here)
    dump_row = planes_here * ROWS
    lower_index = jnp.where(in_slab, local_plane * ROWS + lines_all, dump_row).reshape(-1)
    upper_index = jnp.where(in_slab, lower_index.reshape(in_slab.shape) + 1, dump_row).reshape(-1)
    values = piece.reshape(-1, 3 * COLS)
    weight = weights_all.reshape(-1, 1)
    carry = carry.at[lower_index].add(weight * values)
    return carry.at[upper_index].add((1.0 - weight) * values)


def dense_path(
    logits, cand, counts, weighted, squared, cosine, sine,
    plane_share, line_share, weight_share, regularizer, slab_id,
):
    prob = posterior_rows(logits, counts).reshape(TRANS, LMAX, -1)
    hot = (cand[:, None, :] == jnp.arange(K)[None, :, None]).astype(F32)
    post = jnp.einsum("tlb,lkb->tkb", prob, hot).astype(BF16)
    y = jnp.einsum("tkb,rbz->tkrz", post, weighted, preferred_element_type=F32)
    d = jnp.einsum("tkb,rbc->krc", post, squared, preferred_element_type=F32)
    y_re = y[..., :COLS]
    y_im = y[..., COLS:]
    num_re = jnp.sum(cosine[:, None] * y_re + sine[:, None] * y_im, axis=0)
    num_im = jnp.sum(cosine[:, None] * y_im - sine[:, None] * y_re, axis=0)
    partial_value = lax.psum_scatter(
        jnp.stack([num_re, num_im, d], axis=2), "img", scatter_dimension=0, tiled=True
    )
    planes_here = regularizer.shape[0]
    inserted = insert_into(
        jnp.zeros((planes_here * ROWS + 1, 3 * COLS), F32),
        lax.all_gather(partial_value, "vol", axis=1, tiled=True),
        plane_share,
        line_share,
        weight_share,
        slab_id,
        planes_here,
    )
    slab = inserted[: planes_here * ROWS].reshape(planes_here, ROWS, 3, COLS)
    summed = lax.psum_scatter(slab, "img", scatter_dimension=1, tiled=True)
    denom = summed[:, :, 2] + regularizer
    return jnp.stack([summed[:, :, 0] / denom, summed[:, :, 1] / denom], axis=0)


def body(
    images, defocus, candidates, counts, noise_weight, volume,
    row_plane, row_line, row_weight, regularizer,
):
    rows = noise_weight.shape[0]
    planes_here = volume.shape[1]
    lines_here = regularizer.shape[1]
    slab_id = lax.axis_index("vol")
    group_id = lax.axis_index("img")
    n_vol = lax.axis_size("vol")
    n_img = lax.axis_size("img")
    global_rows = slab_id * rows + jnp.arange(rows)
    row_freq = (global_rows.astype(F32) - ROWS // 2) / ROWS
    col_freq = jnp.arange(COLS).astype(F32) / (2 * COLS)
    share = K // n_img
    first = group_id * share
    plane_share = lax.dynamic_slice_in_dim(row_plane, first, share, 0)
    line_share = lax.dynamic_slice_in_dim(row_line, first, share, 0)
    weight_share = lax.dynamic_slice_in_dim(row_weight, first, share, 0)

    masked = extract(volume, plane_share, line_share, weight_share, slab_id, n_vol)
    own = lax.psum_scatter(masked, "vol", scatter_dimension=0, tiled=False)
    slices = lax.all_gather(own, "img", axis=0, tiled=False)

    cosine, sine = shift_phases(row_freq, col_freq, TRANS)
    weighted, squared = weigh(images, defocus, noise_weight, row_freq, col_freq)
    cand = candidates.T
    count_row = counts[None, :]
    partial_logits = candidate_logits(slices, weighted, squared, cosine, sine, cand)
    logits = lax.psum(partial_logits, "vol")

    mean = rows * K // n_img
    cap = -(-int(mean + 5.0 * math.sqrt(mean)) // 32) * 32
    line_b = row_line.T.reshape(n_vol, rows * K)
    plane_b = row_plane.T.reshape(n_vol, rows * K)
    weight_b = row_weight.T.reshape(n_vol, rows * K)
    low_part = line_b // lines_here
    high_part = (line_b + 1) // lines_here
    part_ids = jnp.arange(n_img)[:, None, None]
    members = (low_part == part_ids) | (high_part == part_ids)
    lengths = jnp.sum(members.astype(jnp.int32), axis=2)
    fits = jnp.max(lengths) <= cap

    send_member = lax.dynamic_index_in_dim(members, slab_id, 1, keepdims=False)
    row_ids = jnp.arange(rows * K).astype(F32)
    send_src = compact(
        send_member,
        ranks(send_member, rows),
        jnp.broadcast_to(row_ids, (n_img, 1, rows * K)),
        cap,
    ).astype(jnp.int32)
    send_len = lax.dynamic_index_in_dim(lengths, slab_id, 1, keepdims=False)

    recv_member = lax.dynamic_index_in_dim(members, group_id, 0, keepdims=False)
    recv_rank = ranks(recv_member, rows)
    local_plane = plane_b - slab_id * planes_here
    here = recv_member & (local_plane >= 0) & (local_plane < planes_here)
    target = local_plane * line_stride(lines_here) + line_b - group_id * lines_here + HEAD
    entry = compact(
        here,
        ranks(here, rows),
        jnp.stack([recv_rank.astype(F32), target.astype(F32), weight_b], axis=1),
        cap,
    )
    entry_len = jnp.sum(here.astype(jnp.int32), axis=1)
    entry_pos = entry[:, 0].astype(jnp.int32).reshape(-1)
    entry_at = entry[:, 1].astype(jnp.int32).reshape(-1)
    entry_w = entry[:, 2].reshape(-1)

    def listed_path():
        listed = project(
            send_src.reshape(-1), send_len, logits, cand, count_row, weighted, squared,
            cosine, sine, n_img, cap,
        )
        summed = lax.psum_scatter(listed, "img", scatter_dimension=0, tiled=False)
        received = lax.all_gather(summed, "vol", axis=0, tiled=False)
        return insert(entry_len, entry_pos, entry_at, entry_w, received, regularizer)

    def other_path():
        return dense_path(
            logits, cand, count_row, weighted, squared, cosine, sine,
            plane_share, line_share, weight_share, regularizer, slab_id,
        )

    return lax.cond(fits, listed_path, other_path)


def solution(mesh):
    return jax.shard_map(
        body,
        mesh=mesh,
        in_specs=(
            P(None, "img", "vol", None),
            P("img"),
            P("img", None),
            P("img"),
            P("vol", None),
            P(None, "vol", None, None),
            P(),
            P(),
            P(),
            P("vol", "img", None),
        ),
        out_specs=P(None, "vol", "img", None),
        check_vma=False,
    )
```

```python
import math

import jax
import jax.numpy as jnp
import numpy as np
from jax import lax
from jax.experimental import pallas as pl
from jax.experimental.pallas import tpu as pltpu
from jax.sharding import PartitionSpec as P

ROWS = 256
COLS = 128
K = 64
TRANS = 4
LMAX = 8
AMPLITUDE = 0.1
VMEM_LIMIT = 56 * 1024 * 1024
BF16 = jnp.bfloat16
F32 = jnp.float32


def params(steps):
    return pltpu.CompilerParams(
        dimension_semantics=("arbitrary",) * steps, vmem_limit_bytes=VMEM_LIMIT
    )


def smem():
    return pl.BlockSpec(memory_space=pltpu.SMEM)


def vmem():
    return pl.BlockSpec(memory_space=pltpu.VMEM)


def shift_phases(row_freq, col_freq, number):
    shift_ids = jnp.arange(number)
    shift_x = (shift_ids % 2).astype(F32) - 0.5
    shift_y = (shift_ids // 2).astype(F32) - 0.5
    angle = (
        -2.0
        * math.pi
        * (
            shift_x[:, None, None] * col_freq[None, None, :]
            + shift_y[:, None, None] * row_freq[None, :, None]
        )
    )
    return (jnp.cos(angle), jnp.sin(angle))


def along_z(n_vol, shift):
    count = n_vol // 2
    return [(v, (v // 2 + shift) % count * 2 + v % 2) for v in range(n_vol)]


def flip(number, mask):
    return [(v, v ^ mask) for v in range(number)]


def ring_of(n_vol):
    return list(range(0, n_vol, 2)) + list(range(n_vol - 1, 0, -2))


def ring_order(n_vol):
    ring = ring_of(n_vol)
    table = np.zeros((n_vol, n_vol), np.int32)
    for p, v in enumerate(ring):
        order = [v]
        for d in range(1, n_vol // 2):
            order += [ring[p - d], ring[(p + d) % n_vol]]
        table[v] = order + [ring[p - n_vol // 2]]
    return table


def extract_kernel(idx_s, wl_s, wu_s, flag_s, blk_s, vol_ref, keep_a, send_a, *rest):
    pair = rest[-1]
    parts_b = rest[:-1]
    count_z = keep_a.shape[0]
    groups_a = keep_a.shape[2] // 16
    groups_b = parts_b[0].shape[2] // 16
    first = lax.broadcasted_iota(jnp.int32, (2, COLS), 0) == 0

    def fill(out, lead, block, skip, groups):
        def group_step(g, carry):
            at = block * (groups_a + groups_b) + skip + g
            base = pl.multiple_of(g * 16, 16)

            @pl.when(flag_s[at] > 0)
            def _():
                for u in range(16):
                    i = idx_s[at * 16 + u]
                    w = jnp.where(first, wl_s[at * 16 + u], wu_s[at * 16 + u])
                    for j in range(2):
                        pair[j, 2 * u : 2 * u + 2, :] = w * vol_ref[j, pl.ds(i, 2), :]
                for j in range(2):
                    value = pair[j, pl.ds(0, 16, stride=2), :] + pair[j, pl.ds(1, 16, stride=2), :]
                    out[lead, j, pl.ds(base, 16), :] = value.astype(BF16)

            @pl.when(flag_s[at] == 0)
            def _():
                for j in range(2):
                    out[lead, j, pl.ds(base, 16), :] = jnp.zeros((16, COLS), BF16)

            return carry

        lax.fori_loop(0, groups, group_step, 0)

    for dz in range(count_z):
        for dy in range(2):
            block = blk_s[dz * 2 + dy]
            fill((keep_a, send_a)[dy], dz, block, 0, groups_a)
            fill(parts_b[dz], dy, block, groups_a, groups_b)


def extract(volume, planes, lines, weights, slab_id, n_vol, share_a):
    share = planes.shape[0]
    planes_here = volume.shape[1]
    rows = ROWS // n_vol
    count_z = n_vol // 2

    def order(x):
        return x.reshape(share, n_vol, rows).transpose(1, 0, 2).reshape(-1)

    local = order(planes) - slab_id * planes_here
    owned = (local >= 0) & (local < planes_here)
    idx = jnp.where(owned, local, 0) * ROWS + order(lines)
    weight = order(weights)
    lower = jnp.where(owned, weight, 0.0)
    upper = jnp.where(owned, 1.0 - weight, 0.0)
    flag = jnp.any(owned.reshape(-1, 16), axis=1).astype(jnp.int32)
    rel = jnp.arange(n_vol)
    blocks = (slab_id // 2 + rel // 2) % count_z * 2 + (slab_id % 2 + rel) % 2
    shape_a = jax.ShapeDtypeStruct((count_z, 2, share_a * rows, COLS), BF16)
    shape_b = jax.ShapeDtypeStruct((2, 2, (share - share_a) * rows, COLS), BF16)
    return pl.pallas_call(
        extract_kernel,
        out_shape=[shape_a, shape_a] + [shape_b] * count_z,
        in_specs=[smem()] * 5 + [vmem()],
        out_specs=[vmem()] * (2 + count_z),
        scratch_shapes=[pltpu.VMEM((2, 32, COLS), F32)],
        compiler_params=pltpu.CompilerParams(vmem_limit_bytes=VMEM_LIMIT),
        name="extract",
    )(idx, lower, upper, flag, blocks, volume.reshape(2, planes_here * ROWS, COLS))


def to_pixel_rows(messages, n_vol):
    keep_a, send_a, keep_b = messages[:3]
    got_b = [lax.ppermute(m, "vol", along_z(n_vol, d + 1)) for d, m in enumerate(messages[3:])]
    got_a = lax.ppermute(send_a, "vol", flip(n_vol, 1))
    sum_b = sum(got_b, keep_b)
    out_b = sum_b[0] + lax.ppermute(sum_b[1], "vol", flip(n_vol, 1))
    sums_a = [keep_a[d] + got_a[d] for d in range(n_vol // 2)]
    moved = [lax.ppermute(sums_a[d], "vol", along_z(n_vol, d)) for d in range(1, n_vol // 2)]
    return sum(moved, sums_a[0]), out_b


def from_partners(x, n_img):
    return [x] + [lax.ppermute(x, "img", flip(n_img, m)) for m in range(1, n_img)]


def ring_gather(x, n_vol):
    ring = ring_of(n_vol)
    ahead = [(ring[p], ring[(p + 1) % n_vol]) for p in range(n_vol)]
    back = [(b, a) for a, b in ahead]
    pieces = [x]
    one = two = x
    for _ in range(1, n_vol // 2):
        one = lax.ppermute(one, "vol", ahead)
        two = lax.ppermute(two, "vol", back)
        pieces += [one, two]
    half = x.shape[1] // 2
    return pieces + [
        lax.ppermute(one[:, :half], "vol", ahead),
        lax.ppermute(two[:, half:], "vol", back),
    ]


def weigh_kernel(img_ref, sa_ref, ca_ref, sx_ref, cx_ref, nw_ref, wt_ref, sq_ref, buf):
    count = img_ref.shape[1]
    rows = img_ref.shape[2]
    for j in range(2):
        buf[j] = img_ref[j].astype(F32).reshape(count * rows, COLS)
    sx = sx_ref[...]
    cx = cx_ref[...]
    for r in range(rows):
        contrast = -(sa_ref[:, r : r + 1] * cx + ca_ref[:, r : r + 1] * sx)
        noise = nw_ref[r : r + 1, :]
        scale = contrast * noise
        for j in range(2):
            x = buf[j, pl.ds(r, count, stride=rows), :]
            wt_ref[r, :, j * COLS : (j + 1) * COLS] = (scale * x).astype(BF16)
        sq_ref[r] = (contrast * contrast * noise).astype(BF16)


def weigh(images, defocus, noise_weight, row_freq, col_freq):
    count = images.shape[1]
    rows = images.shape[2]
    step = 64
    angle_r = defocus[:, None] * (row_freq * row_freq)[None, :] + math.asin(AMPLITUDE)
    angle_c = defocus[:, None] * (col_freq * col_freq)[None, :]
    return pl.pallas_call(
        weigh_kernel,
        grid=(count // step,),
        out_shape=[
            jax.ShapeDtypeStruct((rows, count, 2 * COLS), BF16),
            jax.ShapeDtypeStruct((rows, count, COLS), BF16),
        ],
        in_specs=[
            pl.BlockSpec((2, step, rows, COLS), lambda b: (0, b, 0, 0)),
            pl.BlockSpec((step, rows), lambda b: (b, 0)),
            pl.BlockSpec((step, rows), lambda b: (b, 0)),
            pl.BlockSpec((step, COLS), lambda b: (b, 0)),
            pl.BlockSpec((step, COLS), lambda b: (b, 0)),
            pl.BlockSpec((rows, COLS), lambda b: (0, 0)),
        ],
        out_specs=[
            pl.BlockSpec((rows, step, 2 * COLS), lambda b: (0, b, 0)),
            pl.BlockSpec((rows, step, COLS), lambda b: (0, b, 0)),
        ],
        scratch_shapes=[pltpu.VMEM((2, step * rows, COLS), F32)],
        compiler_params=params(1),
        name="weigh",
    )(
        images,
        jnp.sin(angle_r),
        jnp.cos(angle_r),
        jnp.sin(angle_c),
        jnp.cos(angle_c),
        noise_weight,
    )


def logits_kernel(group_s, wt_ref, sq_ref, cos_ref, sin_ref, cand_ref, *rest):
    sl_refs = rest[:-4]
    out_ref, part, acc, quad = rest[-4:]
    step = pl.program_id(0)
    groups = len(sl_refs) // 2
    rows = part.shape[1] // K
    span = part.shape[1] // groups
    inner = wt_ref.shape[0]

    @pl.when(step == 0)
    def _():
        for m in range(groups):
            base = group_s[m] * span
            for ref in sl_refs[2 * m : 2 * m + 2]:
                size = ref.shape[1]
                for j in range(2):
                    part[j, pl.ds(pl.multiple_of(base, 8), size), :] = ref[j].astype(F32)
                base = base + size
        acc[...] = jnp.zeros_like(acc)
        quad[...] = jnp.zeros_like(quad)

    dims = (((1,), (1,)), ((), ()))
    total = acc[...]
    total_q = quad[...]
    for u in range(inner):
        re = part[0, pl.ds(step * inner + u, K, stride=rows), :]
        im = part[1, pl.ds(step * inner + u, K, stride=rows), :]
        shifted = []
        for t in range(TRANS):
            c = cos_ref[t, u : u + 1, :]
            s = sin_ref[t, u : u + 1, :]
            shifted.append(
                jnp.concatenate(
                    [(c * re - s * im).astype(BF16), (s * re + c * im).astype(BF16)], axis=1
                )
            )
        left = jnp.concatenate(shifted, axis=0)
        power = (re * re + im * im).astype(BF16)
        total = total + lax.dot_general(left, wt_ref[u], dims, preferred_element_type=F32)
        total_q = total_q + lax.dot_general(power, sq_ref[u], dims, preferred_element_type=F32)
    acc[...] = total
    quad[...] = total_q

    @pl.when(step == pl.num_programs(0) - 1)
    def _():
        ids = lax.broadcasted_iota(jnp.int32, quad.shape, 0)
        half = 0.5 * quad[...]
        for t in range(TRANS):
            value = acc[t * K : (t + 1) * K, :] - half
            for l in range(LMAX):
                pick = jnp.where(ids == cand_ref[l : l + 1, :], value, 0.0)
                out_ref[t * LMAX + l : t * LMAX + l + 1, :] = jnp.sum(pick, axis=0, keepdims=True)


def candidate_logits(group_ids, slices, weighted, squared, cosine, sine, cand):
    rows, count = squared.shape[:2]
    inner = 8
    return pl.pallas_call(
        logits_kernel,
        grid=(rows // inner,),
        out_shape=jax.ShapeDtypeStruct((TRANS * LMAX, count), F32),
        in_specs=[
            smem(),
            pl.BlockSpec((inner, count, 2 * COLS), lambda s: (s, 0, 0)),
            pl.BlockSpec((inner, count, COLS), lambda s: (s, 0, 0)),
            pl.BlockSpec((TRANS, inner, COLS), lambda s: (0, s, 0)),
            pl.BlockSpec((TRANS, inner, COLS), lambda s: (0, s, 0)),
            pl.BlockSpec((LMAX, count), lambda s: (0, 0)),
        ]
        + [pl.BlockSpec(x.shape, lambda s: (0, 0, 0)) for x in slices],
        out_specs=pl.BlockSpec((TRANS * LMAX, count), lambda s: (0, 0)),
        scratch_shapes=[
            pltpu.VMEM((2, K * rows, COLS), F32),
            pltpu.VMEM((TRANS * K, count), F32),
            pltpu.VMEM((K, count), F32),
        ],
        compiler_params=params(1),
        name="logits",
    )(group_ids, weighted, squared, cosine, sine, cand, *slices)


def posterior_rows(logits, counts):
    place = lax.broadcasted_iota(jnp.int32, logits.shape, 0) % LMAX
    allowed = place < counts
    masked = jnp.where(allowed, logits, -1e30)
    highest = jnp.max(masked, axis=0, keepdims=True)
    exponent = jnp.where(allowed, jnp.exp(masked - highest), 0.0)
    return (exponent / jnp.sum(exponent, axis=0, keepdims=True)).astype(BF16).astype(F32)


def project_kernel(
    src_s, len_s, group_s, cand_ref, cnt_ref, wt_ref, sq_ref, cos_ref, sin_ref, *rest
):
    lg_refs = rest[:-6]
    keep_ref, send_ref, post, post_sum, num, pick = rest[-6:]
    step = pl.program_id(0)
    inner = wt_ref.shape[0]
    parts = 2 * keep_ref.shape[0]
    cap = keep_ref.shape[2]

    @pl.when(step == 0)
    def _():
        prob = posterior_rows(sum([ref[...] for ref in lg_refs[1:]], lg_refs[0][...]), cnt_ref[...])
        ids = lax.broadcasted_iota(jnp.int32, (K, prob.shape[1]), 0)
        total = jnp.zeros((K, prob.shape[1]), F32)
        for t in range(TRANS):
            dense = jnp.zeros((K, prob.shape[1]), F32)
            for l in range(LMAX):
                at = t * LMAX + l
                dense = jnp.where(ids == cand_ref[l : l + 1, :], dense + prob[at : at + 1, :], dense)
            post[t * K : (t + 1) * K, :] = dense.astype(BF16)
            total = total + dense
        high = total.astype(BF16)
        post_sum[:K, :] = high
        post_sum[K:, :] = (total - high.astype(F32)).astype(BF16)

    for u in range(inner):
        y = jnp.dot(post[...], wt_ref[u], preferred_element_type=F32)
        d = jnp.dot(post_sum[...], sq_ref[u], preferred_element_type=F32)
        re = jnp.zeros((K, COLS), F32)
        im = jnp.zeros((K, COLS), F32)
        for t in range(TRANS):
            c = cos_ref[t, u : u + 1, :]
            s = sin_ref[t, u : u + 1, :]
            y_re = y[t * K : (t + 1) * K, :COLS]
            y_im = y[t * K : (t + 1) * K, COLS:]
            re = re + (c * y_re + s * y_im)
            im = im + (c * y_im - s * y_re)
        base = pl.multiple_of((step * inner + u) * K, K)
        num[0, pl.ds(base, K), :] = re
        num[1, pl.ds(base, K), :] = im
        num[2, pl.ds(base, K), :] = d[:K] + d[K:]

    @pl.when(step == pl.num_programs(0) - 1)
    def _():
        for m in range(parts):
            q = group_s[m]
            out_ref = (keep_ref, send_ref)[m % 2]

            def group_step(g, carry, q=q, m=m, out_ref=out_ref):
                base = pl.multiple_of(g * 16, 16)
                for u in range(16):
                    s = src_s[q * cap + base + u]
                    for c in range(3):
                        pick[c, u : u + 1, :] = num[c, pl.ds(s, 1), :]
                for c in range(3):
                    out_ref[m // 2, c, pl.ds(base, 16), :] = pick[c].astype(BF16)
                return carry

            lax.fori_loop(0, (jnp.minimum(len_s[q], cap) + 15) // 16, group_step, 0)


def project(src, lengths, group_ids, logits, cand, counts, weighted, squared, cosine, sine, cap):
    rows, count = squared.shape[:2]
    inner = 8
    shape = (group_ids.shape[0] // 2, 3, cap, COLS)
    return pl.pallas_call(
        project_kernel,
        grid=(rows // inner,),
        out_shape=[jax.ShapeDtypeStruct(shape, BF16)] * 2,
        in_specs=[
            smem(),
            smem(),
            smem(),
            pl.BlockSpec((LMAX, count), lambda s: (0, 0)),
            pl.BlockSpec((1, count), lambda s: (0, 0)),
            pl.BlockSpec((inner, count, 2 * COLS), lambda s: (s, 0, 0)),
            pl.BlockSpec((inner, count, COLS), lambda s: (s, 0, 0)),
            pl.BlockSpec((TRANS, inner, COLS), lambda s: (0, s, 0)),
            pl.BlockSpec((TRANS, inner, COLS), lambda s: (0, s, 0)),
        ]
        + [pl.BlockSpec((TRANS * LMAX, count), lambda s: (0, 0)) for _ in logits],
        out_specs=[pl.BlockSpec(shape, lambda s: (0, 0, 0, 0))] * 2,
        scratch_shapes=[
            pltpu.VMEM((TRANS * K, count), BF16),
            pltpu.VMEM((2 * K, count), BF16),
            pltpu.VMEM((3, rows * K, COLS), F32),
            pltpu.VMEM((3, 16, COLS), F32),
        ],
        compiler_params=params(1),
        name="project",
    )(src, lengths, group_ids, cand, counts, weighted, squared, cosine, sine, *logits)


HEAD = 8


def line_stride(lines_here):
    return lines_here + 2 * HEAD


def insert_kernel(len_s, pos_s, at_s, wgt_s, order_s, reg_ref, *rest):
    pieces = rest[:-3]
    out_ref, acc, buf = rest[-3:]
    cap = pieces[0].shape[1]
    planes, lines_here = reg_ref.shape[:2]
    stride = line_stride(lines_here)
    acc[...] = jnp.zeros_like(acc)
    first = lax.broadcasted_iota(jnp.int32, (2, COLS), 0) == 0
    for m in range(len(pieces) - 1):
        for c in range(3):
            if m < len(pieces) - 2:
                buf[c] = pieces[m][c].astype(F32)
            else:
                buf[c, : cap // 2, :] = pieces[m][c].astype(F32)
                buf[c, cap // 2 :, :] = pieces[m + 1][c].astype(F32)
        block = order_s[m]

        def group_step(g, carry, block=block):
            for u in range(4):
                e = block * cap + g * 4 + u
                s = pos_s[e]
                to = at_s[e]
                w = wgt_s[e]
                both = jnp.where(first, w, 1.0 - w)
                for c in range(3):
                    row = jnp.broadcast_to(buf[c, pl.ds(s, 1), :], (2, COLS))
                    acc[c, pl.ds(to, 2), :] = acc[c, pl.ds(to, 2), :] + both * row
            return carry

        lax.fori_loop(0, (jnp.minimum(len_s[block], cap) + 3) // 4, group_step, 0)

    def plane_step(p, carry):
        base = pl.multiple_of(p * stride + HEAD, 8)
        inv = 1.0 / (acc[2, pl.ds(base, lines_here), :] + reg_ref[p])
        out_ref[0, p] = acc[0, pl.ds(base, lines_here), :] * inv
        out_ref[1, p] = acc[1, pl.ds(base, lines_here), :] * inv
        return carry

    lax.fori_loop(0, planes, plane_step, 0)


def insert(lengths, positions, targets, weights, order, pieces, regularizer):
    cap = pieces[0].shape[1]
    planes, lines_here = regularizer.shape[:2]
    return pl.pallas_call(
        insert_kernel,
        out_shape=jax.ShapeDtypeStruct((2, planes, lines_here, COLS), F32),
        in_specs=[smem()] * 5 + [vmem()] * (1 + len(pieces)),
        out_specs=vmem(),
        scratch_shapes=[
            pltpu.VMEM((3, planes * line_stride(lines_here), COLS), F32),
            pltpu.VMEM((3, cap, COLS), F32),
        ],
        compiler_params=pltpu.CompilerParams(vmem_limit_bytes=VMEM_LIMIT),
        name="insert",
    )(lengths, positions, targets, weights, order, regularizer, *pieces)


def ranks(member, rows):
    x = member.reshape(-1, rows, K).astype(F32)
    before_k = (jnp.arange(K)[:, None] < jnp.arange(K)[None, :]).astype(F32)
    before_r = (jnp.arange(rows)[:, None] < jnp.arange(rows)[None, :]).astype(F32)
    inner = jnp.einsum("xrk,kl->xrl", x, before_k, preferred_element_type=F32)
    outer = jnp.einsum("xr,rs->xs", jnp.sum(x, axis=2), before_r, preferred_element_type=F32)
    return (inner + outer[:, :, None]).reshape(member.shape).astype(jnp.int32)


def compact(member, rank, values, cap):
    high = jnp.where(member, rank // 32, -1)
    low = rank % 32
    left = (high[:, :, None] == jnp.arange(cap // 32)).astype(F32)
    hot = low[:, None, None, :] == jnp.arange(32)[None, None, :, None]
    right = jnp.where(hot, values[:, :, None, :], 0.0)
    out = jnp.einsum("xnh,xvln->xvhl", left, right, precision=lax.Precision.HIGHEST)
    return out.reshape(values.shape[0], values.shape[1], cap)


def insert_into(carry, piece, planes_all, lines_all, weights_all, slab_id, planes_here):
    local_plane = planes_all - slab_id * planes_here
    in_slab = (local_plane >= 0) & (local_plane < planes_here)
    dump_row = planes_here * ROWS
    lower_index = jnp.where(in_slab, local_plane * ROWS + lines_all, dump_row).reshape(-1)
    upper_index = jnp.where(in_slab, lower_index.reshape(in_slab.shape) + 1, dump_row).reshape(-1)
    values = piece.reshape(-1, 3 * COLS)
    weight = weights_all.reshape(-1, 1)
    carry = carry.at[lower_index].add(weight * values)
    return carry.at[upper_index].add((1.0 - weight) * values)


def dense_path(
    logits, cand, counts, weighted, squared, cosine, sine,
    plane_share, line_share, weight_share, regularizer, slab_id,
):
    prob = posterior_rows(logits, counts).reshape(TRANS, LMAX, -1)
    hot = (cand[:, None, :] == jnp.arange(K)[None, :, None]).astype(F32)
    post = jnp.einsum("tlb,lkb->tkb", prob, hot).astype(BF16)
    y = jnp.einsum("tkb,rbz->tkrz", post, weighted, preferred_element_type=F32)
    d = jnp.einsum("tkb,rbc->krc", post, squared, preferred_element_type=F32)
    y_re = y[..., :COLS]
    y_im = y[..., COLS:]
    num_re = jnp.sum(cosine[:, None] * y_re + sine[:, None] * y_im, axis=0)
    num_im = jnp.sum(cosine[:, None] * y_im - sine[:, None] * y_re, axis=0)
    partial_value = lax.psum_scatter(
        jnp.stack([num_re, num_im, d], axis=2), "img", scatter_dimension=0, tiled=True
    )
    planes_here = regularizer.shape[0]
    inserted = insert_into(
        jnp.zeros((planes_here * ROWS + 1, 3 * COLS), F32),
        lax.all_gather(partial_value, "vol", axis=1, tiled=True),
        plane_share,
        line_share,
        weight_share,
        slab_id,
        planes_here,
    )
    slab = inserted[: planes_here * ROWS].reshape(planes_here, ROWS, 3, COLS)
    summed = lax.psum_scatter(slab, "img", scatter_dimension=1, tiled=True)
    denom = summed[:, :, 2] + regularizer
    return jnp.stack([summed[:, :, 0] / denom, summed[:, :, 1] / denom], axis=0)


def body(
    images, defocus, candidates, counts, noise_weight, volume,
    row_plane, row_line, row_weight, regularizer,
):
    rows = noise_weight.shape[0]
    planes_here = volume.shape[1]
    lines_here = regularizer.shape[1]
    slab_id = lax.axis_index("vol")
    group_id = lax.axis_index("img")
    n_vol = lax.axis_size("vol")
    n_img = lax.axis_size("img")
    global_rows = slab_id * rows + jnp.arange(rows)
    row_freq = (global_rows.astype(F32) - ROWS // 2) / ROWS
    col_freq = jnp.arange(COLS).astype(F32) / (2 * COLS)
    share = K // n_img
    first = group_id * share
    plane_share = lax.dynamic_slice_in_dim(row_plane, first, share, 0)
    line_share = lax.dynamic_slice_in_dim(row_line, first, share, 0)
    weight_share = lax.dynamic_slice_in_dim(row_weight, first, share, 0)

    aligned = max(1, 16 // rows)
    share_a = share * 11 // 16 // aligned * aligned
    messages = extract(volume, plane_share, line_share, weight_share, slab_id, n_vol, share_a)
    own_a, own_b = to_pixel_rows(messages, n_vol)
    slices_b = from_partners(own_b, n_img)
    slices_a = from_partners(own_a, n_img)
    slices = [x for both in zip(slices_a, slices_b) for x in both]
    group_ids = group_id ^ jnp.arange(n_img)

    cosine, sine = shift_phases(row_freq, col_freq, TRANS)
    weighted, squared = weigh(images, defocus, noise_weight, row_freq, col_freq)
    cand = candidates.T
    count_row = counts[None, :]
    partial_logits = candidate_logits(group_ids, slices, weighted, squared, cosine, sine, cand)
    pair_logits = partial_logits + lax.ppermute(partial_logits, "vol", flip(n_vol, 1))
    logits = [pair_logits] + [
        lax.ppermute(pair_logits, "vol", along_z(n_vol, d)) for d in range(1, n_vol // 2)
    ]

    mean = rows * K // n_img
    cap = -(-int(mean + 5.0 * math.sqrt(mean)) // 32) * 32
    line_b = row_line.T.reshape(n_vol, rows * K)
    plane_b = row_plane.T.reshape(n_vol, rows * K)
    weight_b = row_weight.T.reshape(n_vol, rows * K)
    low_part = line_b // lines_here
    high_part = (line_b + 1) // lines_here
    part_ids = jnp.arange(n_img)[:, None, None]
    members = (low_part == part_ids) | (high_part == part_ids)
    lengths = jnp.sum(members.astype(jnp.int32), axis=2)
    fits = jnp.max(lengths) <= cap

    send_member = lax.dynamic_index_in_dim(members, slab_id, 1, keepdims=False)
    row_ids = jnp.arange(rows * K).astype(F32)
    send_src = compact(
        send_member,
        ranks(send_member, rows),
        jnp.broadcast_to(row_ids, (n_img, 1, rows * K)),
        cap,
    ).astype(jnp.int32)
    send_len = lax.dynamic_index_in_dim(lengths, slab_id, 1, keepdims=False)

    recv_member = lax.dynamic_index_in_dim(members, group_id, 0, keepdims=False)
    recv_rank = ranks(recv_member, rows)
    local_plane = plane_b - slab_id * planes_here
    here = recv_member & (local_plane >= 0) & (local_plane < planes_here)
    target = local_plane * line_stride(lines_here) + line_b - group_id * lines_here + HEAD
    entry = compact(
        here,
        ranks(here, rows),
        jnp.stack([recv_rank.astype(F32), target.astype(F32), weight_b], axis=1),
        cap,
    )
    entry_len = jnp.sum(here.astype(jnp.int32), axis=1)
    entry_pos = entry[:, 0].astype(jnp.int32).reshape(-1)
    entry_at = entry[:, 1].astype(jnp.int32).reshape(-1)
    entry_w = entry[:, 2].reshape(-1)

    keep, send = project(
        send_src.reshape(-1), send_len, group_ids, logits, cand, count_row, weighted, squared,
        cosine, sine, cap,
    )
    got = lax.ppermute(send, "img", flip(n_img, 1))
    summed = [(keep[m].astype(F32) + got[m].astype(F32)).astype(BF16) for m in range(n_img // 2)]
    moved = [lax.ppermute(summed[m], "img", flip(n_img, 2 * m)) for m in range(1, n_img // 2)]
    own_rows = sum([x.astype(F32) for x in moved], summed[0].astype(F32)).astype(BF16)
    pieces = ring_gather(own_rows, n_vol)
    order = jnp.asarray(ring_order(n_vol))[slab_id]

    def listed_path():
        return insert(entry_len, entry_pos, entry_at, entry_w, order, pieces, regularizer)

    def other_path():
        return dense_path(
            sum(logits[1:], logits[0]), cand, count_row, weighted, squared, cosine, sine,
            plane_share, line_share, weight_share, regularizer, slab_id,
        )

    return lax.cond(fits, listed_path, other_path)


def solution(mesh):
    return jax.shard_map(
        body,
        mesh=mesh,
        in_specs=(
            P(None, "img", "vol", None),
            P("img"),
            P("img", None),
            P("img"),
            P("vol", None),
            P(None, "vol", None, None),
            P(),
            P(),
            P(),
            P("vol", "img", None),
        ),
        out_specs=P(None, "vol", "img", None),
        check_vma=False,
    )
```

```python
import math
from functools import partial

import jax
import jax.numpy as jnp
import numpy as np
from jax import lax
from jax.experimental import pallas as pl
from jax.experimental.pallas import tpu as pltpu
from jax.sharding import PartitionSpec as P

ROWS = 256
COLS = 128
K = 64
TRANS = 4
LMAX = 8
AMPLITUDE = 0.1
VMEM_LIMIT = 56 * 1024 * 1024
BF16 = jnp.bfloat16
F32 = jnp.float32


def params(steps):
    return pltpu.CompilerParams(
        dimension_semantics=("arbitrary",) * steps, vmem_limit_bytes=VMEM_LIMIT
    )


def smem():
    return pl.BlockSpec(memory_space=pltpu.SMEM)


def vmem():
    return pl.BlockSpec(memory_space=pltpu.VMEM)


def hbm():
    return pl.BlockSpec(memory_space=pl.ANY)


def shift_phases(row_freq, col_freq, number):
    shift_ids = jnp.arange(number)
    shift_x = (shift_ids % 2).astype(F32) - 0.5
    shift_y = (shift_ids // 2).astype(F32) - 0.5
    angle = (
        -2.0
        * math.pi
        * (
            shift_x[:, None, None] * col_freq[None, None, :]
            + shift_y[:, None, None] * row_freq[None, :, None]
        )
    )
    return (jnp.cos(angle), jnp.sin(angle))


def along_z(n_vol, shift):
    count = n_vol // 2
    return [(v, (v // 2 + shift) % count * 2 + v % 2) for v in range(n_vol)]


def flip(number, mask):
    return [(v, v ^ mask) for v in range(number)]


def ring_of(n_vol):
    return list(range(0, n_vol, 2)) + list(range(n_vol - 1, 0, -2))


def ring_order(n_vol):
    ring = ring_of(n_vol)
    table = np.zeros((n_vol, n_vol), np.int32)
    for p, v in enumerate(ring):
        order = [v]
        for d in range(1, n_vol // 2):
            order += [ring[p - d], ring[(p + d) % n_vol]]
        table[v] = order + [ring[p - n_vol // 2]]
    return table


def extract_kernel(idx_s, wl_s, wu_s, flag_s, blk_s, vol_hbm, keep_a, send_a, *rest):
    vol_ref, pair, sem = rest[-3:]
    parts_b = rest[:-3]
    load = pltpu.make_async_copy(vol_hbm, vol_ref, sem)
    load.start()
    for ref in (keep_a, send_a) + parts_b:
        ref[...] = jnp.zeros_like(ref)
    load.wait()
    count_z = keep_a.shape[0]
    groups_a = keep_a.shape[2] // 16
    groups_b = parts_b[0].shape[2] // 16
    first = lax.broadcasted_iota(jnp.int32, (2, COLS), 0) == 0

    def fill(out, lead, block, skip, groups):
        def group_step(g, carry):
            at = block * (groups_a + groups_b) + skip + g
            base = pl.multiple_of(g * 16, 16)

            @pl.when(flag_s[at] > 0)
            def _():
                for u in range(16):
                    i = idx_s[at * 16 + u]
                    w = jnp.where(first, wl_s[at * 16 + u], wu_s[at * 16 + u])
                    for j in range(2):
                        pair[j, 2 * u : 2 * u + 2, :] = w * vol_ref[j, pl.ds(i, 2), :]
                for j in range(2):
                    value = pair[j, pl.ds(0, 16, stride=2), :] + pair[j, pl.ds(1, 16, stride=2), :]
                    out[lead, j, pl.ds(base, 16), :] = value.astype(BF16)

            return carry

        lax.fori_loop(0, groups, group_step, 0)

    for dz in range(count_z):
        for dy in range(2):
            block = blk_s[dz * 2 + dy]
            fill((keep_a, send_a)[dy], dz, block, 0, groups_a)
            fill(parts_b[dz], dy, block, groups_a, groups_b)


def extract(volume, planes, lines, weights, slab_id, n_vol, share_a):
    share = planes.shape[0]
    planes_here = volume.shape[1]
    rows = ROWS // n_vol
    count_z = n_vol // 2

    def order(x):
        return x.reshape(share, n_vol, rows).transpose(1, 0, 2).reshape(-1)

    local = order(planes) - slab_id * planes_here
    owned = (local >= 0) & (local < planes_here)
    idx = jnp.where(owned, local, 0) * ROWS + order(lines)
    weight = order(weights)
    lower = jnp.where(owned, weight, 0.0)
    upper = jnp.where(owned, 1.0 - weight, 0.0)
    flag = jnp.any(owned.reshape(-1, 16), axis=1).astype(jnp.int32)
    rel = jnp.arange(n_vol)
    blocks = (slab_id // 2 + rel // 2) % count_z * 2 + (slab_id % 2 + rel) % 2
    shape_a = jax.ShapeDtypeStruct((count_z, 2, share_a * rows, COLS), BF16)
    shape_b = jax.ShapeDtypeStruct((2, 2, (share - share_a) * rows, COLS), BF16)
    return pl.pallas_call(
        extract_kernel,
        out_shape=[shape_a, shape_a] + [shape_b] * count_z,
        in_specs=[smem()] * 5 + [hbm()],
        out_specs=[vmem()] * (2 + count_z),
        scratch_shapes=[
            pltpu.VMEM((2, planes_here * ROWS, COLS), F32),
            pltpu.VMEM((2, 32, COLS), F32),
            pltpu.SemaphoreType.DMA,
        ],
        compiler_params=pltpu.CompilerParams(vmem_limit_bytes=VMEM_LIMIT),
        name="extract",
    )(idx, lower, upper, flag, blocks, volume.reshape(2, planes_here * ROWS, COLS))


def combine_first_kernel(keep_a, got_a, keep_b, *rest):
    count_z = keep_a.shape[0]
    got_b = rest[: count_z - 1]
    out_a = rest[count_z : 2 * count_z]
    out_b = rest[2 * count_z :]
    for d in range(count_z):
        out_a[d][...] = keep_a[d] + got_a[d]
    for d in range(2):
        total = keep_b[d]
        for ref in got_b:
            total = total + ref[d]
        out_b[d][...] = total


def combine_last_kernel(*refs):
    total = refs[0][...]
    for ref in refs[1:-2]:
        total = total + ref[...]
    refs[-1][...] = total


def to_pixel_rows(messages, n_vol, first_with, last_with):
    keep_a, send_a, keep_b = messages[:3]
    count_z = n_vol // 2
    got_b = [lax.ppermute(m, "vol", along_z(n_vol, d + 1)) for d, m in enumerate(messages[3:])]
    got_a = lax.ppermute(send_a, "vol", flip(n_vol, 1))
    shape_a = jax.ShapeDtypeStruct(keep_a.shape[1:], BF16)
    shape_b = jax.ShapeDtypeStruct(keep_b.shape[1:], BF16)
    sums = pl.pallas_call(
        combine_first_kernel,
        out_shape=[shape_a] * count_z + [shape_b] * 2,
        in_specs=[vmem()] * (2 + count_z) + [hbm()],
        out_specs=[vmem()] * (count_z + 2),
        compiler_params=pltpu.CompilerParams(vmem_limit_bytes=VMEM_LIMIT),
        name="combine_first",
    )(keep_a, got_a, keep_b, *got_b, first_with)
    sums_a, sums_b = sums[:count_z], sums[count_z:]
    moved_b = lax.ppermute(sums_b[1], "vol", flip(n_vol, 1))
    moved = [lax.ppermute(sums_a[d], "vol", along_z(n_vol, d)) for d in range(1, count_z)]
    out_b = sums_b[0] + moved_b
    out_a = pl.pallas_call(
        combine_last_kernel,
        out_shape=shape_a,
        in_specs=[vmem()] * count_z + [hbm()],
        out_specs=vmem(),
        compiler_params=pltpu.CompilerParams(vmem_limit_bytes=VMEM_LIMIT),
        name="combine_last",
    )(sums_a[0], *moved, last_with)
    return out_a, out_b


def from_partners(x, n_img):
    return [x] + [lax.ppermute(x, "img", flip(n_img, m)) for m in range(1, n_img)]


def ring_gather(x, n_vol):
    ring = ring_of(n_vol)
    ahead = [(ring[p], ring[(p + 1) % n_vol]) for p in range(n_vol)]
    back = [(b, a) for a, b in ahead]
    pieces = [x]
    one = two = x
    for _ in range(1, n_vol // 2):
        one = lax.ppermute(one, "vol", ahead)
        two = lax.ppermute(two, "vol", back)
        pieces += [one, two]
    half = x.shape[1] // 2
    return pieces + [
        lax.ppermute(one[:, :half], "vol", ahead),
        lax.ppermute(two[:, half:], "vol", back),
    ]


def weigh_kernel(img_ref, sa_ref, ca_ref, sx_ref, cx_ref, nw_ref, wt_ref, sq_ref, buf):
    count = img_ref.shape[1]
    rows = img_ref.shape[2]
    for j in range(2):
        buf[j] = img_ref[j].astype(F32).reshape(count * rows, COLS)
    sx = sx_ref[...]
    cx = cx_ref[...]
    for r in range(rows):
        contrast = -(sa_ref[:, r : r + 1] * cx + ca_ref[:, r : r + 1] * sx)
        noise = nw_ref[r : r + 1, :]
        scale = contrast * noise
        for j in range(2):
            x = buf[j, pl.ds(r, count, stride=rows), :]
            wt_ref[r, :, j * COLS : (j + 1) * COLS] = (scale * x).astype(BF16)
        sq_ref[r] = (contrast * contrast * noise).astype(BF16)


def weigh(images, defocus, noise_weight, row_freq, col_freq):
    count = images.shape[1]
    rows = images.shape[2]
    step = 64
    angle_r = defocus[:, None] * (row_freq * row_freq)[None, :] + math.asin(AMPLITUDE)
    angle_c = defocus[:, None] * (col_freq * col_freq)[None, :]
    return pl.pallas_call(
        weigh_kernel,
        grid=(count // step,),
        out_shape=[
            jax.ShapeDtypeStruct((rows, count, 2 * COLS), BF16),
            jax.ShapeDtypeStruct((rows, count, COLS), BF16),
        ],
        in_specs=[
            pl.BlockSpec((2, step, rows, COLS), lambda b: (0, b, 0, 0)),
            pl.BlockSpec((step, rows), lambda b: (b, 0)),
            pl.BlockSpec((step, rows), lambda b: (b, 0)),
            pl.BlockSpec((step, COLS), lambda b: (b, 0)),
            pl.BlockSpec((step, COLS), lambda b: (b, 0)),
            pl.BlockSpec((rows, COLS), lambda b: (0, 0)),
        ],
        out_specs=[
            pl.BlockSpec((rows, step, 2 * COLS), lambda b: (0, b, 0)),
            pl.BlockSpec((rows, step, COLS), lambda b: (0, b, 0)),
        ],
        scratch_shapes=[pltpu.VMEM((2, step * rows, COLS), F32)],
        compiler_params=params(1),
        name="weigh",
    )(
        images,
        jnp.sin(angle_r),
        jnp.cos(angle_r),
        jnp.sin(angle_c),
        jnp.cos(angle_c),
        noise_weight,
    )


def logits_kernel(group_s, wt_ref, sq_ref, cos_ref, sin_ref, cand_ref, *rest):
    sl_refs = rest[:-4]
    out_ref, part, acc, quad = rest[-4:]
    step = pl.program_id(0)
    groups = len(sl_refs) // 2
    rows = part.shape[1] // K
    span = part.shape[1] // groups
    inner = wt_ref.shape[0]

    @pl.when(step == 0)
    def _():
        for m in range(groups):
            base = group_s[m] * span
            for ref in sl_refs[2 * m : 2 * m + 2]:
                size = ref.shape[1]
                for j in range(2):
                    part[j, pl.ds(pl.multiple_of(base, 8), size), :] = ref[j].astype(F32)
                base = base + size
        acc[...] = jnp.zeros_like(acc)
        quad[...] = jnp.zeros_like(quad)

    dims = (((1,), (1,)), ((), ()))
    total = acc[...]
    total_q = quad[...]
    for u in range(inner):
        re = part[0, pl.ds(step * inner + u, K, stride=rows), :]
        im = part[1, pl.ds(step * inner + u, K, stride=rows), :]
        shifted = []
        for t in range(TRANS):
            c = cos_ref[t, u : u + 1, :]
            s = sin_ref[t, u : u + 1, :]
            shifted.append(
                jnp.concatenate(
                    [(c * re - s * im).astype(BF16), (s * re + c * im).astype(BF16)], axis=1
                )
            )
        left = jnp.concatenate(shifted, axis=0)
        power = (re * re + im * im).astype(BF16)
        total = total + lax.dot_general(left, wt_ref[u], dims, preferred_element_type=F32)
        total_q = total_q + lax.dot_general(power, sq_ref[u], dims, preferred_element_type=F32)
    acc[...] = total
    quad[...] = total_q

    @pl.when(step == pl.num_programs(0) - 1)
    def _():
        ids = lax.broadcasted_iota(jnp.int32, quad.shape, 0)
        half = 0.5 * quad[...]
        for t in range(TRANS):
            value = acc[t * K : (t + 1) * K, :] - half
            for l in range(LMAX):
                pick = jnp.where(ids == cand_ref[l : l + 1, :], value, 0.0)
                out_ref[t * LMAX + l : t * LMAX + l + 1, :] = jnp.sum(pick, axis=0, keepdims=True)


def candidate_logits(group_ids, slices, weighted, squared, cosine, sine, cand):
    rows, count = squared.shape[:2]
    inner = 8
    return pl.pallas_call(
        logits_kernel,
        grid=(rows // inner,),
        out_shape=jax.ShapeDtypeStruct((TRANS * LMAX, count), F32),
        in_specs=[
            smem(),
            pl.BlockSpec((inner, count, 2 * COLS), lambda s: (s, 0, 0)),
            pl.BlockSpec((inner, count, COLS), lambda s: (s, 0, 0)),
            pl.BlockSpec((TRANS, inner, COLS), lambda s: (0, s, 0)),
            pl.BlockSpec((TRANS, inner, COLS), lambda s: (0, s, 0)),
            pl.BlockSpec((LMAX, count), lambda s: (0, 0)),
        ]
        + [pl.BlockSpec(x.shape, lambda s: (0, 0, 0)) for x in slices],
        out_specs=pl.BlockSpec((TRANS * LMAX, count), lambda s: (0, 0)),
        scratch_shapes=[
            pltpu.VMEM((2, K * rows, COLS), F32),
            pltpu.VMEM((TRANS * K, count), F32),
            pltpu.VMEM((K, count), F32),
        ],
        compiler_params=params(1),
        name="logits",
    )(group_ids, weighted, squared, cosine, sine, cand, *slices)


def posterior_rows(logits, counts):
    place = lax.broadcasted_iota(jnp.int32, logits.shape, 0) % LMAX
    allowed = place < counts
    masked = jnp.where(allowed, logits, -1e30)
    highest = jnp.max(masked, axis=0, keepdims=True)
    exponent = jnp.where(allowed, jnp.exp(masked - highest), 0.0)
    return (exponent / jnp.sum(exponent, axis=0, keepdims=True)).astype(BF16).astype(F32)


def list_rows(num, src_s, len_s, group_s, outs, pick):
    parts = 2 * outs[0].shape[0]
    cap = outs[0].shape[2]
    comps = num.shape[0]
    lead = src_s.shape[0] // parts
    for m in range(parts):
        q = group_s[m]

        def group_step(g, carry, q=q, m=m):
            base = pl.multiple_of(g * 16, 16)
            at = q * lead + g // 2
            off = g % 2 * 16
            for u in range(16):
                s = src_s[at, off + u]
                for c in range(comps):
                    pick[c, u : u + 1, :] = num[c, pl.ds(s, 1), :]
            for c in range(comps):
                outs[m % 2][m // 2, c, pl.ds(base, 16), :] = pick[c].astype(BF16)
            return carry

        lax.fori_loop(0, (jnp.minimum(len_s[q, 0], cap) + 15) // 16, group_step, 0)


def spread_kernel(src_s, len_s, group_s, cand_ref, cnt_ref, sq_ref, *rest):
    lg_refs = rest[:-6]
    keep_ref, send_ref, post, post_sum, num, pick = rest[-6:]
    step = pl.program_id(0)
    inner = sq_ref.shape[0]

    @pl.when(step == 0)
    def _():
        prob = posterior_rows(sum([ref[...] for ref in lg_refs[1:]], lg_refs[0][...]), cnt_ref[...])
        ids = lax.broadcasted_iota(jnp.int32, (K, prob.shape[1]), 0)
        total = jnp.zeros((K, prob.shape[1]), F32)
        for t in range(TRANS):
            dense = jnp.zeros((K, prob.shape[1]), F32)
            for l in range(LMAX):
                at = t * LMAX + l
                dense = jnp.where(ids == cand_ref[l : l + 1, :], dense + prob[at : at + 1, :], dense)
            post[t * K : (t + 1) * K, :] = dense.astype(BF16)
            total = total + dense
        high = total.astype(BF16)
        post_sum[:K, :] = high
        post_sum[K:, :] = (total - high.astype(F32)).astype(BF16)

    for u in range(inner):
        d = jnp.dot(post_sum[...], sq_ref[u], preferred_element_type=F32)
        base = pl.multiple_of((step * inner + u) * K, K)
        num[0, pl.ds(base, K), :] = d[:K] + d[K:]

    @pl.when(step == pl.num_programs(0) - 1)
    def _():
        list_rows(num, src_s, len_s, group_s, (keep_ref, send_ref), pick)


def project_kernel(
    src_s, len_s, group_s, post, wt_ref, cos_ref, sin_ref, keep_ref, send_ref, num, pick
):
    step = pl.program_id(0)
    inner = wt_ref.shape[0]
    for u in range(inner):
        y = jnp.dot(post[...], wt_ref[u], preferred_element_type=F32)
        re = jnp.zeros((K, COLS), F32)
        im = jnp.zeros((K, COLS), F32)
        for t in range(TRANS):
            c = cos_ref[t, u : u + 1, :]
            s = sin_ref[t, u : u + 1, :]
            y_re = y[t * K : (t + 1) * K, :COLS]
            y_im = y[t * K : (t + 1) * K, COLS:]
            re = re + (c * y_re + s * y_im)
            im = im + (c * y_im - s * y_re)
        base = pl.multiple_of((step * inner + u) * K, K)
        num[0, pl.ds(base, K), :] = re
        num[1, pl.ds(base, K), :] = im

    @pl.when(step == pl.num_programs(0) - 1)
    def _():
        list_rows(num, src_s, len_s, group_s, (keep_ref, send_ref), pick)


def spread(src, lengths, group_ids, logits, cand, counts, squared, cap):
    rows, count = squared.shape[:2]
    inner = 8
    shape = (group_ids.shape[0] // 2, 1, cap, COLS)
    return pl.pallas_call(
        spread_kernel,
        grid=(rows // inner,),
        out_shape=[jax.ShapeDtypeStruct(shape, BF16)] * 2
        + [jax.ShapeDtypeStruct((TRANS * K, count), BF16)],
        in_specs=[
            smem(),
            smem(),
            smem(),
            pl.BlockSpec((LMAX, count), lambda s: (0, 0)),
            pl.BlockSpec((1, count), lambda s: (0, 0)),
            pl.BlockSpec((inner, count, COLS), lambda s: (s, 0, 0)),
        ]
        + [pl.BlockSpec((TRANS * LMAX, count), lambda s: (0, 0)) for _ in logits],
        out_specs=[pl.BlockSpec(shape, lambda s: (0, 0, 0, 0))] * 2
        + [pl.BlockSpec((TRANS * K, count), lambda s: (0, 0))],
        scratch_shapes=[
            pltpu.VMEM((2 * K, count), BF16),
            pltpu.VMEM((1, rows * K, COLS), F32),
            pltpu.VMEM((1, 16, COLS), F32),
        ],
        compiler_params=params(1),
        name="spread",
    )(src, lengths, group_ids, cand, counts, squared, *logits)


def project(src, lengths, group_ids, post, weighted, cosine, sine, cap):
    rows, count = weighted.shape[:2]
    inner = 8
    shape = (group_ids.shape[0] // 2, 2, cap, COLS)
    return pl.pallas_call(
        project_kernel,
        grid=(rows // inner,),
        out_shape=[jax.ShapeDtypeStruct(shape, BF16)] * 2,
        in_specs=[
            smem(),
            smem(),
            smem(),
            pl.BlockSpec((TRANS * K, count), lambda s: (0, 0)),
            pl.BlockSpec((inner, count, 2 * COLS), lambda s: (s, 0, 0)),
            pl.BlockSpec((TRANS, inner, COLS), lambda s: (0, s, 0)),
            pl.BlockSpec((TRANS, inner, COLS), lambda s: (0, s, 0)),
        ],
        out_specs=[pl.BlockSpec(shape, lambda s: (0, 0, 0, 0))] * 2,
        scratch_shapes=[
            pltpu.VMEM((2, rows * K, COLS), F32),
            pltpu.VMEM((2, 16, COLS), F32),
        ],
        compiler_params=params(1),
        name="project",
    )(src, lengths, group_ids, post, weighted, cosine, sine)


def to_member(keep, send, n_img):
    got = lax.ppermute(send, "img", flip(n_img, 1))
    summed = [(keep[m].astype(F32) + got[m].astype(F32)).astype(BF16) for m in range(n_img // 2)]
    moved = [lax.ppermute(summed[m], "img", flip(n_img, 2 * m)) for m in range(1, n_img // 2)]
    return sum([x.astype(F32) for x in moved], summed[0].astype(F32)).astype(BF16)


HEAD = 8


def line_stride(lines_here):
    return lines_here + 2 * HEAD


def insert_kernel(start, count, has_acc, mode, len_s, pos_s, at_s, wgt_s, order_s, *rest):
    pieces = rest[:count]
    rest = rest[count:]
    out_ref, acc, buf = rest[-3:]
    extra = rest[:-3]
    comps, cap = buf.shape[:2]
    lead = pos_s.shape[0] // order_s.shape[0]
    if has_acc:
        pltpu.sync_copy(extra[-1], acc)
    else:
        acc[...] = jnp.zeros_like(acc)
    first = lax.broadcasted_iota(jnp.int32, (2, COLS), 0) == 0
    index = 0
    while index < count:
        m = start + index
        whole = pieces[index].shape[1] == cap
        for c in range(comps):
            if whole:
                buf[c] = pieces[index][c].astype(F32)
            else:
                buf[c, : cap // 2, :] = pieces[index][c].astype(F32)
                buf[c, cap // 2 :, :] = pieces[index + 1][c].astype(F32)
        if whole:
            index += 1
        else:
            index += 2
        block = order_s[m]

        def group_step(g, carry, block=block):
            at = block * lead + g // 8
            off = g % 8 * 4
            for u in range(4):
                s = pos_s[at, off + u]
                to = at_s[at, off + u]
                w = wgt_s[at, off + u]
                both = jnp.where(first, w, 1.0 - w)
                for c in range(comps):
                    row = jnp.broadcast_to(buf[c, pl.ds(s, 1), :], (2, COLS))
                    acc[c, pl.ds(to, 2), :] = acc[c, pl.ds(to, 2), :] + both * row
            return carry

        lax.fori_loop(0, (jnp.minimum(len_s[block, 0], cap) + 3) // 4, group_step, 0)

    if mode == "sum":
        pltpu.sync_copy(acc, out_ref)
        return
    planes, lines_here = extra[0].shape[:2]
    stride = line_stride(lines_here)

    def plane_step(p, carry):
        base = pl.multiple_of(p * stride + HEAD, 8)
        if mode == "inverse":
            out_ref[p] = 1.0 / (acc[0, pl.ds(base, lines_here), :] + extra[0][p])
        else:
            for c in range(comps):
                out_ref[c, p] = acc[c, pl.ds(base, lines_here), :] * extra[0][p]
        return carry

    lax.fori_loop(0, planes, plane_step, 0)


def insert(tables, order, start, pieces, cap, block, mode, extra=(), acc=None):
    comps = pieces[0].shape[0]
    planes, lines_here = block
    acc_shape = (comps, planes * line_stride(lines_here), COLS)
    out = {
        "sum": acc_shape,
        "inverse": (planes, lines_here, COLS),
        "result": (comps, planes, lines_here, COLS),
    }[mode]
    more = list(extra) + ([] if acc is None else [acc])
    return pl.pallas_call(
        partial(insert_kernel, start, len(pieces), acc is not None, mode),
        out_shape=jax.ShapeDtypeStruct(out, F32),
        in_specs=[smem()] * 5
        + [vmem()] * (len(pieces) + len(extra))
        + [hbm()] * (acc is not None),
        out_specs=hbm() if mode == "sum" else vmem(),
        scratch_shapes=[pltpu.VMEM(acc_shape, F32), pltpu.VMEM((comps, cap, COLS), F32)],
        compiler_params=pltpu.CompilerParams(vmem_limit_bytes=VMEM_LIMIT),
        name="insert_" + mode,
    )(*tables, order, *pieces, *more)


def running(x):
    lanes = lax.broadcasted_iota(jnp.int32, x.shape, 1)
    step = 1
    while step < x.shape[1]:
        x = x + jnp.where(lanes >= step, pltpu.roll(x, step, 1), 0)
        step *= 2
    return x


def split_index(x):
    return [(x >> 5).astype(F32), (x & 31).astype(F32)]


def split_weight(w):
    a = w.astype(BF16).astype(F32)
    b = (w - a).astype(BF16).astype(F32)
    return [a, b, w - a - b]


def compacted(member, rank, values, lead):
    high = jnp.where(member, rank >> 5, -1)
    low = rank & 31
    left = lax.broadcasted_iota(jnp.int32, (lead, rank.shape[1]), 0) == high
    hot = lax.broadcasted_iota(jnp.int32, (32, rank.shape[1]), 0) == low
    right = jnp.concatenate([jnp.where(hot, v, 0.0).astype(BF16) for v in values], axis=0)
    return lax.dot_general(
        left.astype(F32).astype(BF16), right, (((1,), (1,)), ((), ())), preferred_element_type=F32
    )


def lists_kernel(
    n_img, planes_here, lines_here, cap,
    plane_ref, line_ref, wgt_ref,
    src_ref, pos_ref, at_ref, w_ref, send_len, recv_len, longest, own,
):
    slab = lax.axis_index("vol")
    group = lax.axis_index("img")
    blocks, number = line_ref.shape
    lead = src_ref.shape[0] // n_img
    lines = line_ref[...]

    def in_part(x, part):
        return (x >= part * lines_here - 1) & (x < (part + 1) * lines_here)

    top = jnp.zeros((blocks, COLS), jnp.int32)
    for q in range(n_img):
        size = jnp.sum(in_part(lines, q).astype(F32), axis=1, keepdims=True).astype(jnp.int32)
        top = jnp.maximum(top, jnp.broadcast_to(size, (blocks, COLS)))
    longest[...] = jnp.broadcast_to(jnp.max(top.astype(F32)), (8, COLS)).astype(jnp.int32)

    own[...] = jnp.broadcast_to(line_ref[pl.ds(slab, 1), :], own.shape)
    sent = in_part(own[...], lax.broadcasted_iota(jnp.int32, own.shape, 0))
    total = running(sent.astype(jnp.int32))
    send_len[...] = jnp.broadcast_to(total[:, number - 1 :], send_len.shape)
    rank = total - sent.astype(jnp.int32)
    row_ids = split_index(lax.broadcasted_iota(jnp.int32, (1, number), 1))
    for q in range(n_img):
        out = compacted(sent[q : q + 1], rank[q : q + 1], row_ids, lead)
        src_ref[q * lead : (q + 1) * lead, :] = (32.0 * out[:, :32] + out[:, 32:64]).astype(jnp.int32)

    member = in_part(lines, group)
    place = running(member.astype(jnp.int32)) - member.astype(jnp.int32)
    local = plane_ref[...] - slab * planes_here
    here = member & (local >= 0) & (local < planes_here)
    total = running(here.astype(jnp.int32))
    recv_len[...] = jnp.broadcast_to(total[:, number - 1 :], recv_len.shape)
    rank = total - here.astype(jnp.int32)
    target = local * line_stride(lines_here) + lines - group * lines_here + HEAD
    target = jnp.where(here, target, 0)
    for v in range(blocks):
        row = slice(v, v + 1)
        values = split_index(place[row]) + split_index(target[row]) + split_weight(wgt_ref[row, :])
        out = compacted(here[row], rank[row], values, lead)
        at = slice(v * lead, (v + 1) * lead)
        pos_ref[at, :] = (32.0 * out[:, :32] + out[:, 32:64]).astype(jnp.int32)
        at_ref[at, :] = (32.0 * out[:, 64:96] + out[:, 96:128]).astype(jnp.int32)
        w_ref[at, :] = out[:, 128:160] + out[:, 160:192] + out[:, 192:224]


def lists(row_plane, row_line, row_weight, n_vol, n_img, planes_here, lines_here, cap):
    lead = -(-(cap // 32) // 8) * 8
    number = ROWS // n_vol * K

    def order(x):
        return x.T.reshape(n_vol, number)

    def table(blocks, dtype=jnp.int32):
        return jax.ShapeDtypeStruct((blocks * lead, 32), dtype)

    return pl.pallas_call(
        partial(lists_kernel, n_img, planes_here, lines_here, cap),
        out_shape=[
            table(n_img),
            table(n_vol),
            table(n_vol),
            table(n_vol, F32),
            jax.ShapeDtypeStruct((8, COLS), jnp.int32),
            jax.ShapeDtypeStruct((n_vol, COLS), jnp.int32),
            jax.ShapeDtypeStruct((8, COLS), jnp.int32),
        ],
        in_specs=[vmem()] * 3,
        out_specs=[vmem()] * 7,
        scratch_shapes=[pltpu.VMEM((8, number), jnp.int32)],
        compiler_params=pltpu.CompilerParams(vmem_limit_bytes=VMEM_LIMIT),
        name="lists",
    )(order(row_plane), order(row_line), order(row_weight))


def insert_into(carry, piece, planes_all, lines_all, weights_all, slab_id, planes_here):
    local_plane = planes_all - slab_id * planes_here
    in_slab = (local_plane >= 0) & (local_plane < planes_here)
    dump_row = planes_here * ROWS
    lower_index = jnp.where(in_slab, local_plane * ROWS + lines_all, dump_row).reshape(-1)
    upper_index = jnp.where(in_slab, lower_index.reshape(in_slab.shape) + 1, dump_row).reshape(-1)
    values = piece.reshape(-1, 3 * COLS)
    weight = weights_all.reshape(-1, 1)
    carry = carry.at[lower_index].add(weight * values)
    return carry.at[upper_index].add((1.0 - weight) * values)


def dense_path(
    logits, cand, counts, weighted, squared, cosine, sine,
    plane_share, line_share, weight_share, regularizer, slab_id,
):
    prob = posterior_rows(logits, counts).reshape(TRANS, LMAX, -1)
    hot = (cand[:, None, :] == jnp.arange(K)[None, :, None]).astype(F32)
    post = jnp.einsum("tlb,lkb->tkb", prob, hot).astype(BF16)
    y = jnp.einsum("tkb,rbz->tkrz", post, weighted, preferred_element_type=F32)
    d = jnp.einsum("tkb,rbc->krc", post, squared, preferred_element_type=F32)
    y_re = y[..., :COLS]
    y_im = y[..., COLS:]
    num_re = jnp.sum(cosine[:, None] * y_re + sine[:, None] * y_im, axis=0)
    num_im = jnp.sum(cosine[:, None] * y_im - sine[:, None] * y_re, axis=0)
    partial_value = lax.psum_scatter(
        jnp.stack([num_re, num_im, d], axis=2), "img", scatter_dimension=0, tiled=True
    )
    planes_here = regularizer.shape[0]
    inserted = insert_into(
        jnp.zeros((planes_here * ROWS + 1, 3 * COLS), F32),
        lax.all_gather(partial_value, "vol", axis=1, tiled=True),
        plane_share,
        line_share,
        weight_share,
        slab_id,
        planes_here,
    )
    slab = inserted[: planes_here * ROWS].reshape(planes_here, ROWS, 3, COLS)
    summed = lax.psum_scatter(slab, "img", scatter_dimension=1, tiled=True)
    denom = summed[:, :, 2] + regularizer
    return jnp.stack([summed[:, :, 0] / denom, summed[:, :, 1] / denom], axis=0)


def body(
    images, defocus, candidates, counts, noise_weight, volume,
    row_plane, row_line, row_weight, regularizer,
):
    rows = noise_weight.shape[0]
    planes_here = volume.shape[1]
    lines_here = regularizer.shape[1]
    slab_id = lax.axis_index("vol")
    group_id = lax.axis_index("img")
    n_vol = lax.axis_size("vol")
    n_img = lax.axis_size("img")
    global_rows = slab_id * rows + jnp.arange(rows)
    row_freq = (global_rows.astype(F32) - ROWS // 2) / ROWS
    col_freq = jnp.arange(COLS).astype(F32) / (2 * COLS)
    share = K // n_img
    first = group_id * share
    plane_share = lax.dynamic_slice_in_dim(row_plane, first, share, 0)
    line_share = lax.dynamic_slice_in_dim(row_line, first, share, 0)
    weight_share = lax.dynamic_slice_in_dim(row_weight, first, share, 0)

    aligned = max(1, 16 // rows)
    share_a = share * 11 // 16 // aligned * aligned
    messages = extract(volume, plane_share, line_share, weight_share, slab_id, n_vol, share_a)
    cosine, sine = shift_phases(row_freq, col_freq, TRANS)
    weighted, squared = weigh(images, defocus, noise_weight, row_freq, col_freq)
    mean = rows * K // n_img
    cap = -(-int(mean + 4.2 * math.sqrt(mean)) // 32) * 32
    src, pos, at, wgt, send_len, recv_len, longest = lists(
        row_plane, row_line, row_weight, n_vol, n_img, planes_here, lines_here, cap
    )
    own_a, own_b = to_pixel_rows(messages, n_vol, weighted, pos)
    slices_b = from_partners(own_b, n_img)
    slices_a = from_partners(own_a, n_img)
    slices = [x for both in zip(slices_a, slices_b) for x in both]
    group_ids = group_id ^ jnp.arange(n_img)

    cand = candidates.T
    count_row = counts[None, :]
    partial_logits = candidate_logits(group_ids, slices, weighted, squared, cosine, sine, cand)
    pair_logits = partial_logits + lax.ppermute(partial_logits, "vol", flip(n_vol, 1))
    logits = [pair_logits] + [
        lax.ppermute(pair_logits, "vol", along_z(n_vol, d)) for d in range(1, n_vol // 2)
    ]

    keep_d, send_d, post = spread(
        src, send_len, group_ids, logits, cand, count_row, squared, cap
    )
    keep_n, send_n = project(src, send_len, group_ids, post, weighted, cosine, sine, cap)
    pieces_d = ring_gather(to_member(keep_d, send_d, n_img), n_vol)
    pieces_n = ring_gather(to_member(keep_n, send_n, n_img), n_vol)
    order = jnp.asarray(ring_order(n_vol))[slab_id]
    tables = (recv_len, pos, at, wgt)
    block = (planes_here, lines_here)
    early = n_vol // 2 + 1
    inverse = insert(tables, order, 0, pieces_d, cap, block, "inverse", [regularizer])
    part_sum = insert(tables, order, 0, pieces_n[:early], cap, block, "sum")
    result = insert(
        tables, order, early, pieces_n[early:], cap, block, "result", [inverse], part_sum
    )

    def dense(state):
        return False, dense_path(
            sum(logits[1:], logits[0]), cand, count_row, weighted, squared, cosine, sine,
            plane_share, line_share, weight_share, regularizer, slab_id,
        )

    return lax.while_loop(lambda state: state[0], dense, (longest[0, 0] > cap, result))[1]


def solution(mesh):
    return jax.shard_map(
        body,
        mesh=mesh,
        in_specs=(
            P(None, "img", "vol", None),
            P("img"),
            P("img", None),
            P("img"),
            P("vol", None),
            P(None, "vol", None, None),
            P(),
            P(),
            P(),
            P("vol", "img", None),
        ),
        out_specs=P(None, "vol", "img", None),
        check_vma=False,
    )
```

```python
import math
from functools import partial

import jax
import jax.numpy as jnp
from jax import lax
from jax.experimental import pallas as pl
from jax.experimental.pallas import tpu as pltpu
from jax.sharding import PartitionSpec as P

ROWS = 256
COLS = 128
K = 64
TRANS = 4
LMAX = 8
AMPLITUDE = 0.1
VMEM_LIMIT = 56 * 1024 * 1024
BF16 = jnp.bfloat16
F32 = jnp.float32


def params(steps):
    return pltpu.CompilerParams(
        dimension_semantics=("arbitrary",) * steps, vmem_limit_bytes=VMEM_LIMIT
    )


def smem():
    return pl.BlockSpec(memory_space=pltpu.SMEM)


def vmem():
    return pl.BlockSpec(memory_space=pltpu.VMEM)


def cost(us):
    return pl.CostEstimate(flops=0, transcendentals=0, bytes_accessed=int(us * 3.69e6))


def hbm():
    return pl.BlockSpec(memory_space=pl.ANY)


def shift_phases(row_freq, col_freq, number):
    shift_ids = jnp.arange(number)
    shift_x = (shift_ids % 2).astype(F32) - 0.5
    shift_y = (shift_ids // 2).astype(F32) - 0.5
    angle = (
        -2.0
        * math.pi
        * (
            shift_x[:, None, None] * col_freq[None, None, :]
            + shift_y[:, None, None] * row_freq[None, :, None]
        )
    )
    return (jnp.cos(angle), jnp.sin(angle))


def along_z(n_vol, shift):
    count = n_vol // 2
    return [(v, (v // 2 + shift) % count * 2 + v % 2) for v in range(n_vol)]


def flip(number, mask):
    return [(v, v ^ mask) for v in range(number)]


def ring_of(n_vol):
    return list(range(0, n_vol, 2)) + list(range(n_vol - 1, 0, -2))


def extract_kernel(rows, planes_here, *refs):
    plane_ref, line_ref, weight_hbm, vol_hbm, keep_a, send_a = refs[:6]
    vol, pair, idx_v, flag_v, idx_s, flag_s, w_s, sem = refs[-8:]
    parts_b = refs[6:-8]
    slab = lax.axis_index("vol")
    share = idx_v.shape[0]
    first = lax.axis_index("img") * share
    height = planes_here * ROWS
    count_z = keep_a.shape[0]
    groups_a = keep_a.shape[2] // 16
    groups_b = parts_b[0].shape[2] // 16
    load = pltpu.make_async_copy(vol_hbm, vol.at[:, :height, :], sem.at[0])
    load.start()
    load_w = pltpu.make_async_copy(weight_hbm.at[pl.ds(first, share), :], w_s, sem.at[1])
    load_w.start()
    local = plane_ref[pl.ds(first, share), :] - slab * planes_here
    owned = (local >= 0) & (local < planes_here)
    idx_v[...] = jnp.where(owned, local * ROWS + line_ref[pl.ds(first, share), :], height)
    eights = (
        lax.broadcasted_iota(jnp.int32, (ROWS, COLS), 0) >> 3
        == lax.broadcasted_iota(jnp.int32, (ROWS, COLS), 1)
    )
    flag_v[...] = jnp.dot(
        owned.astype(F32).astype(BF16), eights.astype(F32).astype(BF16), preferred_element_type=F32
    ).astype(jnp.int32)
    to_idx = pltpu.make_async_copy(idx_v, idx_s, sem.at[2])
    to_flag = pltpu.make_async_copy(flag_v, flag_s, sem.at[3])
    to_idx.start()
    to_flag.start()
    vol[:, height : height + 8, :] = jnp.zeros((2, 8, COLS), F32)
    for ref in (keep_a, send_a) + parts_b:
        ref[...] = jnp.zeros_like(ref)
    to_idx.wait()
    to_flag.wait()
    load_w.wait()
    load.wait()
    lower_row = lax.broadcasted_iota(jnp.int32, (2, COLS), 0) == 0
    shift = rows.bit_length() - 1

    def fill(out, lead, block, skip, groups):
        def group_step(g, carry):
            base = pl.multiple_of(g * 16, 16)
            at = []
            for h in range(2):
                n = (skip + g) * 16 + 8 * h
                at.append((n >> shift, block * rows + (n & (rows - 1))))
            hits = flag_s[at[0][0], at[0][1] >> 3] + flag_s[at[1][0], at[1][1] >> 3]

            @pl.when(hits > 0)
            def _():
                for u in range(16):
                    k, r = at[u // 8]
                    i = idx_s[k, r + u % 8]
                    w = w_s[k, r + u % 8]
                    both = jnp.where(lower_row, w, 1.0 - w)
                    for j in range(2):
                        pair[j, 2 * u : 2 * u + 2, :] = both * vol[j, pl.ds(i, 2), :]
                for j in range(2):
                    value = pair[j, pl.ds(0, 16, stride=2), :] + pair[j, pl.ds(1, 16, stride=2), :]
                    out[lead, j, pl.ds(base, 16), :] = value.astype(BF16)

            return carry

        lax.fori_loop(0, groups, group_step, 0)

    for dz in range(count_z):
        for dy in range(2):
            z = (slab >> 1) + dz
            block = jnp.where(z >= count_z, z - count_z, z) * 2 + ((slab + dy) & 1)
            fill((keep_a, send_a)[dy], dz, block, 0, groups_a)
            fill(parts_b[dz], dy, block, groups_a, groups_b)


def extract(volume, row_plane, row_line, row_weight, n_vol, share, share_a):
    planes_here = volume.shape[1]
    rows = ROWS // n_vol
    count_z = n_vol // 2
    shape_a = jax.ShapeDtypeStruct((count_z, 2, share_a * rows, COLS), BF16)
    shape_b = jax.ShapeDtypeStruct((2, 2, (share - share_a) * rows, COLS), BF16)
    return pl.pallas_call(
        partial(extract_kernel, rows, planes_here),
        out_shape=[shape_a, shape_a] + [shape_b] * count_z,
        in_specs=[vmem(), vmem(), hbm(), hbm()],
        out_specs=[vmem()] * (2 + count_z),
        scratch_shapes=[
            pltpu.VMEM((2, planes_here * ROWS + 8, COLS), F32),
            pltpu.VMEM((2, 32, COLS), F32),
            pltpu.VMEM((share, ROWS), jnp.int32),
            pltpu.VMEM((share, COLS), jnp.int32),
            pltpu.SMEM((share, ROWS), jnp.int32),
            pltpu.SMEM((share, COLS), jnp.int32),
            pltpu.SMEM((share, ROWS), F32),
            pltpu.SemaphoreType.DMA((4,)),
        ],
        compiler_params=pltpu.CompilerParams(vmem_limit_bytes=VMEM_LIMIT),
        cost_estimate=cost(11),
        name="extract",
    )(row_plane, row_line, row_weight, volume.reshape(2, planes_here * ROWS, COLS))


def combine_first_kernel(keep_a, got_a, keep_b, *rest):
    count_z = keep_a.shape[0]
    got_b = rest[: count_z - 1]
    out_a = rest[count_z : 2 * count_z]
    out_b = rest[2 * count_z :]
    for d in range(count_z):
        out_a[d][...] = keep_a[d] + got_a[d]
    for d in range(2):
        total = keep_b[d]
        for ref in got_b:
            total = total + ref[d]
        out_b[d][...] = total


def to_pixel_rows(messages, n_vol, first_with):
    keep_a, send_a, keep_b = messages[:3]
    count_z = n_vol // 2
    got_b = [lax.ppermute(m, "vol", along_z(n_vol, d + 1)) for d, m in enumerate(messages[3:])]
    got_a = lax.ppermute(send_a, "vol", flip(n_vol, 1))
    shape_a = jax.ShapeDtypeStruct(keep_a.shape[1:], BF16)
    shape_b = jax.ShapeDtypeStruct(keep_b.shape[1:], BF16)
    sums = pl.pallas_call(
        combine_first_kernel,
        out_shape=[shape_a] * count_z + [shape_b] * 2,
        in_specs=[vmem()] * (2 + count_z) + [hbm()],
        out_specs=[vmem()] * (count_z + 2),
        compiler_params=pltpu.CompilerParams(vmem_limit_bytes=VMEM_LIMIT),
        cost_estimate=cost(3),
        name="combine_first",
    )(keep_a, got_a, keep_b, *got_b, first_with)
    sums_a, sums_b = sums[:count_z], sums[count_z:]
    moved_b = lax.ppermute(sums_b[1], "vol", flip(n_vol, 1))
    moved = [lax.ppermute(sums_a[d], "vol", along_z(n_vol, d)) for d in range(1, count_z)]
    out_b = sums_b[0] + moved_b
    out_a = sum(moved, sums_a[0])
    return out_a, out_b


def from_partners(x, n_img):
    return [x] + [lax.ppermute(x, "img", flip(n_img, m)) for m in range(1, n_img)]


def ring_gather(x, n_vol):
    ring = ring_of(n_vol)
    ahead = [(ring[p], ring[(p + 1) % n_vol]) for p in range(n_vol)]
    back = [(b, a) for a, b in ahead]
    pieces = [x]
    one = two = x
    for _ in range(1, n_vol // 2):
        one = lax.ppermute(one, "vol", ahead)
        two = lax.ppermute(two, "vol", back)
        pieces += [one, two]
    half = x.shape[1] // 2
    return pieces + [
        lax.ppermute(one[:, :half], "vol", ahead),
        lax.ppermute(two[:, half:], "vol", back),
    ]


def weigh_kernel(img_ref, sa_ref, ca_ref, sx_ref, cx_ref, nw_ref, wt_ref, sq_ref, buf):
    count = img_ref.shape[1]
    rows = img_ref.shape[2]
    pitch = rows + 1
    for j in range(2):
        for b in range(count):
            buf[j, b * pitch : b * pitch + rows, :] = img_ref[j, b].astype(F32)
    sx = sx_ref[...]
    cx = cx_ref[...]
    for r in range(rows):
        contrast = -(sa_ref[:, r : r + 1] * cx + ca_ref[:, r : r + 1] * sx)
        noise = nw_ref[r : r + 1, :]
        scale = contrast * noise
        for j in range(2):
            x = buf[j, pl.ds(r, count, stride=pitch), :]
            wt_ref[r, :, j * COLS : (j + 1) * COLS] = (scale * x).astype(BF16)
        sq_ref[r] = (contrast * contrast * noise).astype(BF16)


def weigh(images, defocus, noise_weight, row_freq, col_freq):
    count = images.shape[1]
    rows = images.shape[2]
    step = 64
    angle_r = defocus[:, None] * (row_freq * row_freq)[None, :] + math.asin(AMPLITUDE)
    angle_c = defocus[:, None] * (col_freq * col_freq)[None, :]
    return pl.pallas_call(
        weigh_kernel,
        grid=(count // step,),
        out_shape=[
            jax.ShapeDtypeStruct((rows, count, 2 * COLS), BF16),
            jax.ShapeDtypeStruct((rows, count, COLS), BF16),
        ],
        in_specs=[
            pl.BlockSpec((2, step, rows, COLS), lambda b: (0, b, 0, 0)),
            pl.BlockSpec((step, rows), lambda b: (b, 0)),
            pl.BlockSpec((step, rows), lambda b: (b, 0)),
            pl.BlockSpec((step, COLS), lambda b: (b, 0)),
            pl.BlockSpec((step, COLS), lambda b: (b, 0)),
            pl.BlockSpec((rows, COLS), lambda b: (0, 0)),
        ],
        out_specs=[
            pl.BlockSpec((rows, step, 2 * COLS), lambda b: (0, b, 0)),
            pl.BlockSpec((rows, step, COLS), lambda b: (0, b, 0)),
        ],
        scratch_shapes=[pltpu.VMEM((2, step * (rows + 1), COLS), F32)],
        compiler_params=params(1),
        cost_estimate=cost(12),
        name="weigh",
    )(
        images,
        jnp.sin(angle_r),
        jnp.cos(angle_r),
        jnp.sin(angle_c),
        jnp.cos(angle_c),
        noise_weight,
    )


def logits_kernel(wt_ref, sq_ref, cos_ref, sin_ref, cand_ref, *rest):
    sl_refs = rest[:-4]
    out_ref, part, acc, quad = rest[-4:]
    step = pl.program_id(0)
    groups = len(sl_refs) // 2
    rows = part.shape[1] // K - 1
    share = K // groups
    pitch = rows + 1
    inner = wt_ref.shape[0]

    @pl.when(step == 0)
    def _():
        for m in range(groups):
            at = m * share
            for ref in sl_refs[2 * m : 2 * m + 2]:
                for j in range(2):
                    for k in range(ref.shape[1] // rows):
                        row = (at + k) * pitch
                        part[j, row : row + rows, :] = ref[j, k * rows : (k + 1) * rows].astype(F32)
                at += ref.shape[1] // rows
        acc[...] = jnp.zeros_like(acc)
        quad[...] = jnp.zeros_like(quad)

    dims = (((1,), (1,)), ((), ()))
    total = acc[...]
    total_q = quad[...]
    for u in range(inner):
        re = part[0, pl.ds(step * inner + u, K, stride=pitch), :]
        im = part[1, pl.ds(step * inner + u, K, stride=pitch), :]
        shifted = []
        for t in range(TRANS):
            c = cos_ref[t, u : u + 1, :]
            s = sin_ref[t, u : u + 1, :]
            shifted.append(
                jnp.concatenate(
                    [(c * re - s * im).astype(BF16), (s * re + c * im).astype(BF16)], axis=1
                )
            )
        left = jnp.concatenate(shifted, axis=0)
        power = (re * re + im * im).astype(BF16)
        total = total + lax.dot_general(left, wt_ref[u], dims, preferred_element_type=F32)
        total_q = total_q + lax.dot_general(power, sq_ref[u], dims, preferred_element_type=F32)
    acc[...] = total
    quad[...] = total_q

    @pl.when(step == pl.num_programs(0) - 1)
    def _():
        ids = lax.broadcasted_iota(jnp.int32, quad.shape, 0) ^ (lax.axis_index("img") * share)
        half = 0.5 * quad[...]
        for t in range(TRANS):
            value = acc[t * K : (t + 1) * K, :] - half
            for l in range(LMAX):
                pick = jnp.where(ids == cand_ref[l : l + 1, :], value, 0.0)
                out_ref[t * LMAX + l : t * LMAX + l + 1, :] = jnp.sum(pick, axis=0, keepdims=True)


def candidate_logits(slices, weighted, squared, cosine, sine, cand):
    rows, count = squared.shape[:2]
    inner = 8
    return pl.pallas_call(
        logits_kernel,
        grid=(rows // inner,),
        out_shape=jax.ShapeDtypeStruct((TRANS * LMAX, count), F32),
        in_specs=[
            pl.BlockSpec((inner, count, 2 * COLS), lambda s: (s, 0, 0)),
            pl.BlockSpec((inner, count, COLS), lambda s: (s, 0, 0)),
            pl.BlockSpec((TRANS, inner, COLS), lambda s: (0, s, 0)),
            pl.BlockSpec((TRANS, inner, COLS), lambda s: (0, s, 0)),
            pl.BlockSpec((LMAX, count), lambda s: (0, 0)),
        ]
        + [pl.BlockSpec(x.shape, lambda s: (0, 0, 0)) for x in slices],
        out_specs=pl.BlockSpec((TRANS * LMAX, count), lambda s: (0, 0)),
        scratch_shapes=[
            pltpu.VMEM((2, K * (rows + 1), COLS), F32),
            pltpu.VMEM((TRANS * K, count), F32),
            pltpu.VMEM((K, count), F32),
        ],
        compiler_params=params(1),
        cost_estimate=cost(8),
        name="logits",
    )(weighted, squared, cosine, sine, cand, *slices)


def posterior_rows(logits, counts):
    place = lax.broadcasted_iota(jnp.int32, logits.shape, 0) % LMAX
    allowed = place < counts
    masked = jnp.where(allowed, logits, -1e30)
    highest = jnp.max(masked, axis=0, keepdims=True)
    exponent = jnp.where(allowed, jnp.exp(masked - highest), 0.0)
    return (exponent / jnp.sum(exponent, axis=0, keepdims=True)).astype(BF16).astype(F32)


def list_rows(num, src_s, len_s, outs, pick):
    parts = 2 * outs[0].shape[0]
    cap = outs[0].shape[2]
    comps = num.shape[0]
    lead = src_s.shape[0] // parts
    group = lax.axis_index("img")
    for m in range(parts):
        q = group ^ m

        def turn(g, carry, q=q, m=m):
            base = pl.multiple_of(g * 32, 32)
            at = q * lead + base
            for u in range(32):
                s = src_s[at + u]
                for c in range(comps):
                    pick[c, u : u + 1, :] = num[c, pl.ds(s, 1), :]
            for c in range(comps):
                outs[m % 2][m // 2, c, pl.ds(base, 32), :] = pick[c].astype(BF16)
            return carry

        lax.fori_loop(0, (jnp.minimum(len_s[q, 0], cap) + 31) // 32, turn, 0)


def spread_kernel(src_s, len_s, cand_ref, cnt_ref, sq_ref, *rest):
    lg_refs = rest[:-6]
    keep_ref, send_ref, post, post_sum, num, pick = rest[-6:]
    step = pl.program_id(0)
    inner = sq_ref.shape[0]

    @pl.when(step == 0)
    def _():
        prob = posterior_rows(sum([ref[...] for ref in lg_refs[1:]], lg_refs[0][...]), cnt_ref[...])
        ids = lax.broadcasted_iota(jnp.int32, (K, prob.shape[1]), 0)
        total = jnp.zeros((K, prob.shape[1]), F32)
        for t in range(TRANS):
            dense = jnp.zeros((K, prob.shape[1]), F32)
            for l in range(LMAX):
                at = t * LMAX + l
                dense = jnp.where(ids == cand_ref[l : l + 1, :], dense + prob[at : at + 1, :], dense)
            post[t * K : (t + 1) * K, :] = dense.astype(BF16)
            total = total + dense
        high = total.astype(BF16)
        post_sum[:K, :] = high
        post_sum[K:, :] = (total - high.astype(F32)).astype(BF16)

    for u in range(inner):
        d = jnp.dot(post_sum[...], sq_ref[u], preferred_element_type=F32)
        base = pl.multiple_of((step * inner + u) * K, K)
        num[0, pl.ds(base, K), :] = d[:K] + d[K:]

    @pl.when(step == pl.num_programs(0) - 1)
    def _():
        list_rows(num, src_s, len_s, (keep_ref, send_ref), pick)


def project_kernel(
    src_s, len_s, post, wt_ref, cos_ref, sin_ref, after, keep_ref, send_ref, num, pick
):
    step = pl.program_id(0)
    inner = wt_ref.shape[0]
    for u in range(inner):
        y = jnp.dot(post[...], wt_ref[u], preferred_element_type=F32)
        re = jnp.zeros((K, COLS), F32)
        im = jnp.zeros((K, COLS), F32)
        for t in range(TRANS):
            c = cos_ref[t, u : u + 1, :]
            s = sin_ref[t, u : u + 1, :]
            y_re = y[t * K : (t + 1) * K, :COLS]
            y_im = y[t * K : (t + 1) * K, COLS:]
            re = re + (c * y_re + s * y_im)
            im = im + (c * y_im - s * y_re)
        base = pl.multiple_of((step * inner + u) * K, K)
        num[0, pl.ds(base, K), :] = re
        num[1, pl.ds(base, K), :] = im

    @pl.when(step == pl.num_programs(0) - 1)
    def _():
        list_rows(num, src_s, len_s, (keep_ref, send_ref), pick)


def spread(src, lengths, n_img, logits, cand, counts, squared, cap):
    rows, count = squared.shape[:2]
    inner = 8
    shape = (n_img // 2, 1, cap, COLS)
    return pl.pallas_call(
        spread_kernel,
        grid=(rows // inner,),
        out_shape=[jax.ShapeDtypeStruct(shape, BF16)] * 2
        + [jax.ShapeDtypeStruct((TRANS * K, count), BF16)],
        in_specs=[
            smem(),
            smem(),
            pl.BlockSpec((LMAX, count), lambda s: (0, 0)),
            pl.BlockSpec((1, count), lambda s: (0, 0)),
            pl.BlockSpec((inner, count, COLS), lambda s: (s, 0, 0)),
        ]
        + [pl.BlockSpec((TRANS * LMAX, count), lambda s: (0, 0)) for _ in logits],
        out_specs=[pl.BlockSpec(shape, lambda s: (0, 0, 0, 0))] * 2
        + [pl.BlockSpec((TRANS * K, count), lambda s: (0, 0))],
        scratch_shapes=[
            pltpu.VMEM((2 * K, count), BF16),
            pltpu.VMEM((1, rows * K, COLS), F32),
            pltpu.VMEM((1, 32, COLS), F32),
        ],
        compiler_params=params(1),
        cost_estimate=cost(8),
        name="spread",
    )(src, lengths, cand, counts, squared, *logits)


def project(src, lengths, n_img, post, weighted, cosine, sine, after, cap):
    rows, count = weighted.shape[:2]
    inner = 8
    shape = (n_img // 2, 2, cap, COLS)
    return pl.pallas_call(
        project_kernel,
        grid=(rows // inner,),
        out_shape=[jax.ShapeDtypeStruct(shape, BF16)] * 2,
        in_specs=[
            smem(),
            smem(),
            pl.BlockSpec((TRANS * K, count), lambda s: (0, 0)),
            pl.BlockSpec((inner, count, 2 * COLS), lambda s: (s, 0, 0)),
            pl.BlockSpec((TRANS, inner, COLS), lambda s: (0, s, 0)),
            pl.BlockSpec((TRANS, inner, COLS), lambda s: (0, s, 0)),
            hbm(),
        ],
        out_specs=[pl.BlockSpec(shape, lambda s: (0, 0, 0, 0))] * 2,
        scratch_shapes=[
            pltpu.VMEM((2, rows * K, COLS), F32),
            pltpu.VMEM((2, 32, COLS), F32),
        ],
        compiler_params=params(1),
        cost_estimate=cost(9),
        name="project",
    )(src, lengths, post, weighted, cosine, sine, after)


def add_cores(keep, send, n_img):
    got = lax.ppermute(send, "img", flip(n_img, 1))
    return [(keep[m].astype(F32) + got[m].astype(F32)).astype(BF16) for m in range(n_img // 2)]


def add_chips(summed, n_img):
    moved = [lax.ppermute(summed[m], "img", flip(n_img, 2 * m)) for m in range(1, n_img // 2)]
    return sum([x.astype(F32) for x in moved], summed[0].astype(F32)).astype(BF16)


HEAD = 8


def line_stride(lines_here):
    return lines_here + 2 * HEAD


def insert_kernel(start, count, has_acc, mode, len_s, code_s, wgt_s, *rest):
    pieces = rest[:count]
    rest = rest[count:]
    out_ref, acc, buf = rest[-3:]
    extra = rest[:-3]
    comps, cap = buf.shape[:2]
    blocks = len_s.shape[0]
    lead = code_s.shape[0] // blocks
    slab = lax.axis_index("vol")
    place = jnp.where(slab & 1, blocks - 1 - (slab >> 1), slab >> 1)
    if has_acc:
        pltpu.sync_copy(extra[-1], acc.at[0])
    else:
        acc[0] = jnp.zeros(acc.shape[1:], F32)
    acc[1] = jnp.zeros(acc.shape[1:], F32)
    first = lax.broadcasted_iota(jnp.int32, (2, COLS), 0) == 0
    index = 0
    while index < count:
        m = start + index
        whole = pieces[index].shape[1] == cap
        for c in range(comps):
            if whole:
                buf[c] = pieces[index][c].astype(F32)
            else:
                buf[c, : cap // 2, :] = pieces[index][c].astype(F32)
                buf[c, cap // 2 :, :] = pieces[index + 1][c].astype(F32)
        if whole:
            index += 1
        else:
            index += 2
        from_place = place + ((m + 1) // 2) * (-1 if m % 2 else 1)
        from_place = from_place & (blocks - 1)
        block = jnp.where(
            from_place >= blocks // 2, 2 * (blocks - 1 - from_place) + 1, 2 * from_place
        )

        def group_step(g, carry, block=block):
            at = block * lead + g * 4
            for u in range(4):
                code = code_s[at + u]
                s = code & 1023
                to = code >> 10
                w = wgt_s[at + u]
                both = jnp.where(first, w, 1.0 - w)
                for c in range(comps):
                    row = jnp.broadcast_to(buf[c, pl.ds(s, 1), :], (2, COLS))
                    acc[u % 2, c, pl.ds(to, 2), :] = acc[u % 2, c, pl.ds(to, 2), :] + both * row
            return carry

        lax.fori_loop(0, (jnp.minimum(len_s[block, 0], cap) + 3) // 4, group_step, 0)

    if mode == "sum":
        acc[0] = acc[0] + acc[1]
        pltpu.sync_copy(acc.at[0], out_ref)
        return
    planes, lines_here = extra[0].shape[:2]
    stride = line_stride(lines_here)

    def plane_step(p, carry):
        base = pl.multiple_of(p * stride + HEAD, 8)
        for c in range(comps):
            total = acc[0, c, pl.ds(base, lines_here), :] + acc[1, c, pl.ds(base, lines_here), :]
            if mode == "inverse":
                out_ref[p] = 1.0 / (total + extra[0][p])
            else:
                out_ref[c, p] = total * extra[0][p]
        return carry

    lax.fori_loop(0, planes, plane_step, 0)


def insert(tables, start, pieces, cap, block, mode, extra=(), acc=None):
    comps = pieces[0].shape[0]
    planes, lines_here = block
    acc_shape = (comps, planes * line_stride(lines_here), COLS)
    out = {
        "sum": acc_shape,
        "inverse": (planes, lines_here, COLS),
        "result": (comps, planes, lines_here, COLS),
    }[mode]
    more = list(extra) + ([] if acc is None else [acc])
    return pl.pallas_call(
        partial(insert_kernel, start, len(pieces), acc is not None, mode),
        out_shape=jax.ShapeDtypeStruct(out, F32),
        in_specs=[smem()] * 3
        + [vmem()] * (len(pieces) + len(extra))
        + [hbm()] * (acc is not None),
        out_specs=hbm() if mode == "sum" else vmem(),
        scratch_shapes=[pltpu.VMEM((2,) + acc_shape, F32), pltpu.VMEM((comps, cap, COLS), F32)],
        compiler_params=pltpu.CompilerParams(vmem_limit_bytes=VMEM_LIMIT),
        cost_estimate=cost(6),
        name="insert_" + mode,
    )(*tables, *pieces, *more)


def running(x):
    lanes = lax.broadcasted_iota(jnp.int32, x.shape, 1)
    step = 1
    while step < x.shape[1]:
        x = x + jnp.where(lanes >= step, pltpu.roll(x, step, 1), 0)
        step *= 2
    return x


def split_index(x):
    return [(x >> 5).astype(F32), (x & 31).astype(F32)]


def split_weight(w):
    a = w.astype(BF16).astype(F32)
    b = (w - a).astype(BF16).astype(F32)
    return [a, b, w - a - b]


def compacted(member, rank, values, lead):
    high = jnp.where(member, rank >> 5, -1)
    low = rank & 31
    spot = lax.broadcasted_iota(jnp.int32, (4 * lead, rank.shape[1]), 0)
    shift = lead.bit_length() - 1
    left = ((spot & (lead - 1)) * 4 + (spot >> shift)) == high
    hot = lax.broadcasted_iota(jnp.int32, (32, rank.shape[1]), 0) == low
    right = jnp.concatenate([jnp.where(hot, v, 0.0).astype(BF16) for v in values], axis=0)
    out = lax.dot_general(
        left.astype(F32).astype(BF16), right, (((1,), (1,)), ((), ())), preferred_element_type=F32
    )
    return [
        jnp.concatenate(
            [out[h * lead : (h + 1) * lead, 32 * i : 32 * (i + 1)] for h in range(4)], axis=1
        )
        for i in range(len(values))
    ]


def lists_kernel(
    n_img, planes_here, lines_here, cap,
    plane_ref, line_ref, wgt_ref,
    src_ref, code_ref, w_ref, send_len, recv_len, longest, own,
):
    slab = lax.axis_index("vol")
    group = lax.axis_index("img")
    blocks, number = line_ref.shape
    lead = src_ref.shape[0] // n_img
    lines = line_ref[...]

    def in_part(x, part):
        return (x >= part * lines_here - 1) & (x < (part + 1) * lines_here)

    top = jnp.zeros((blocks, COLS), jnp.int32)
    for q in range(n_img):
        size = jnp.sum(in_part(lines, q).astype(F32), axis=1, keepdims=True).astype(jnp.int32)
        top = jnp.maximum(top, jnp.broadcast_to(size, (blocks, COLS)))
    longest[...] = jnp.broadcast_to(jnp.max(top.astype(F32)), (8, COLS)).astype(jnp.int32)

    own[...] = jnp.broadcast_to(line_ref[pl.ds(slab, 1), :], own.shape)
    sent = in_part(own[...], lax.broadcasted_iota(jnp.int32, own.shape, 0))
    total = running(sent.astype(jnp.int32))
    send_len[...] = jnp.broadcast_to(total[:, number - 1 :], send_len.shape)
    rank = total - sent.astype(jnp.int32)
    row_ids = split_index(lax.broadcasted_iota(jnp.int32, (1, number), 1))
    for q in range(n_img):
        out = compacted(sent[q : q + 1], rank[q : q + 1], row_ids, lead)
        src_ref[q * lead : (q + 1) * lead, :] = (32.0 * out[0] + out[1]).astype(jnp.int32)

    member = in_part(lines, group)
    place = running(member.astype(jnp.int32)) - member.astype(jnp.int32)
    place = jnp.minimum(place, cap - 1)
    local = plane_ref[...] - slab * planes_here
    here = member & (local >= 0) & (local < planes_here)
    total = running(here.astype(jnp.int32))
    recv_len[...] = jnp.broadcast_to(total[:, number - 1 :], recv_len.shape)
    rank = total - here.astype(jnp.int32)
    target = local * line_stride(lines_here) + lines - group * lines_here + HEAD
    target = jnp.where(here, target, 0)
    for v in range(blocks):
        row = slice(v, v + 1)
        values = split_index(place[row]) + split_index(target[row]) + split_weight(wgt_ref[row, :])
        out = compacted(here[row], rank[row], values, lead)
        at = slice(v * lead, (v + 1) * lead)
        code_ref[at, :] = (
            32768.0 * out[2] + 1024.0 * out[3] + 32.0 * out[0] + out[1]
        ).astype(jnp.int32)
        w_ref[at, :] = out[4] + out[5] + out[6]


def lists(row_plane, row_line, row_weight, n_vol, n_img, planes_here, lines_here, cap):
    lead = 8
    assert cap <= lead * COLS
    number = ROWS // n_vol * K

    def order(x):
        return x.T.reshape(n_vol, number)

    def table(blocks, dtype=jnp.int32):
        return jax.ShapeDtypeStruct((blocks * lead, COLS), dtype)

    return pl.pallas_call(
        partial(lists_kernel, n_img, planes_here, lines_here, cap),
        out_shape=[
            table(n_img),
            table(n_vol),
            table(n_vol, F32),
            jax.ShapeDtypeStruct((8, COLS), jnp.int32),
            jax.ShapeDtypeStruct((n_vol, COLS), jnp.int32),
            jax.ShapeDtypeStruct((8, COLS), jnp.int32),
        ],
        in_specs=[vmem()] * 3,
        out_specs=[vmem()] * 6,
        scratch_shapes=[pltpu.VMEM((8, number), jnp.int32)],
        compiler_params=pltpu.CompilerParams(vmem_limit_bytes=VMEM_LIMIT),
        cost_estimate=cost(6),
        name="lists",
    )(order(row_plane), order(row_line), order(row_weight))


def insert_into(carry, piece, planes_all, lines_all, weights_all, slab_id, planes_here):
    local_plane = planes_all - slab_id * planes_here
    in_slab = (local_plane >= 0) & (local_plane < planes_here)
    dump_row = planes_here * ROWS
    lower_index = jnp.where(in_slab, local_plane * ROWS + lines_all, dump_row).reshape(-1)
    upper_index = jnp.where(in_slab, lower_index.reshape(in_slab.shape) + 1, dump_row).reshape(-1)
    values = piece.reshape(-1, 3 * COLS)
    weight = weights_all.reshape(-1, 1)
    carry = carry.at[lower_index].add(weight * values)
    return carry.at[upper_index].add((1.0 - weight) * values)


def dense_path(
    logits, cand, counts, weighted, squared, cosine, sine,
    plane_share, line_share, weight_share, regularizer, slab_id,
):
    prob = posterior_rows(logits, counts).reshape(TRANS, LMAX, -1)
    hot = (cand[:, None, :] == jnp.arange(K)[None, :, None]).astype(F32)
    post = jnp.einsum("tlb,lkb->tkb", prob, hot).astype(BF16)
    y = jnp.einsum("tkb,rbz->tkrz", post, weighted, preferred_element_type=F32)
    d = jnp.einsum("tkb,rbc->krc", post, squared, preferred_element_type=F32)
    y_re = y[..., :COLS]
    y_im = y[..., COLS:]
    num_re = jnp.sum(cosine[:, None] * y_re + sine[:, None] * y_im, axis=0)
    num_im = jnp.sum(cosine[:, None] * y_im - sine[:, None] * y_re, axis=0)
    partial_value = lax.psum_scatter(
        jnp.stack([num_re, num_im, d], axis=2), "img", scatter_dimension=0, tiled=True
    )
    planes_here = regularizer.shape[0]
    inserted = insert_into(
        jnp.zeros((planes_here * ROWS + 1, 3 * COLS), F32),
        lax.all_gather(partial_value, "vol", axis=1, tiled=True),
        plane_share,
        line_share,
        weight_share,
        slab_id,
        planes_here,
    )
    slab = inserted[: planes_here * ROWS].reshape(planes_here, ROWS, 3, COLS)
    summed = lax.psum_scatter(slab, "img", scatter_dimension=1, tiled=True)
    denom = summed[:, :, 2] + regularizer
    return jnp.stack([summed[:, :, 0] / denom, summed[:, :, 1] / denom], axis=0)


def body(
    images, defocus, candidates, counts, noise_weight, volume,
    row_plane, row_line, row_weight, regularizer,
):
    rows = noise_weight.shape[0]
    planes_here = volume.shape[1]
    lines_here = regularizer.shape[1]
    slab_id = lax.axis_index("vol")
    group_id = lax.axis_index("img")
    n_vol = lax.axis_size("vol")
    n_img = lax.axis_size("img")
    global_rows = slab_id * rows + jnp.arange(rows)
    row_freq = (global_rows.astype(F32) - ROWS // 2) / ROWS
    col_freq = jnp.arange(COLS).astype(F32) / (2 * COLS)
    share = K // n_img
    first = group_id * share
    plane_share = lax.dynamic_slice_in_dim(row_plane, first, share, 0)
    line_share = lax.dynamic_slice_in_dim(row_line, first, share, 0)
    weight_share = lax.dynamic_slice_in_dim(row_weight, first, share, 0)

    aligned = max(1, 16 // rows)
    share_a = share * 11 // 16 // aligned * aligned
    messages = extract(volume, row_plane, row_line, row_weight, n_vol, share, share_a)
    cosine, sine = shift_phases(row_freq, col_freq, TRANS)
    weighted, squared = weigh(images, defocus, noise_weight, row_freq, col_freq)
    mean = rows * K // n_img
    cap = -(-int(mean + 4.2 * math.sqrt(mean)) // 32) * 32
    src, code, wgt, send_len, recv_len, longest = lists(
        row_plane, row_line, row_weight, n_vol, n_img, planes_here, lines_here, cap
    )
    own_a, own_b = to_pixel_rows(messages, n_vol, weighted)
    slices_b = from_partners(own_b, n_img)
    slices_a = from_partners(own_a, n_img)
    slices = [x for both in zip(slices_a, slices_b) for x in both]
    cand = candidates.T
    count_row = counts[None, :]
    partial_logits = candidate_logits(slices, weighted, squared, cosine, sine, cand)
    pair_logits = partial_logits + lax.ppermute(partial_logits, "vol", flip(n_vol, 1))
    logits = [pair_logits] + [
        lax.ppermute(pair_logits, "vol", along_z(n_vol, d)) for d in range(1, n_vol // 2)
    ]

    src = src.reshape(-1)
    keep_d, send_d, post = spread(src, send_len, n_img, logits, cand, count_row, squared, cap)
    summed_d = add_cores(keep_d, send_d, n_img)
    keep_n, send_n = project(
        src, send_len, n_img, post, weighted, cosine, sine, summed_d[-1], cap
    )
    pieces_d = ring_gather(add_chips(summed_d, n_img), n_vol)
    pieces_n = ring_gather(add_chips(add_cores(keep_n, send_n, n_img), n_img), n_vol)
    tables = (recv_len, code.reshape(-1), wgt.reshape(-1))
    block = (planes_here, lines_here)
    early = n_vol // 2 + 1
    inverse = insert(tables, 0, pieces_d, cap, block, "inverse", [regularizer])
    part_sum = insert(tables, 0, pieces_n[:early], cap, block, "sum")

    def listed():
        return insert(tables, early, pieces_n[early:], cap, block, "result", [inverse], part_sum)

    def dense():
        return dense_path(
            sum(logits[1:], logits[0]), cand, count_row, weighted, squared, cosine, sine,
            plane_share, line_share, weight_share, regularizer, slab_id,
        )

    return lax.cond(longest[0, 0] <= cap, listed, dense)


def solution(mesh):
    return jax.shard_map(
        body,
        mesh=mesh,
        in_specs=(
            P(None, "img", "vol", None),
            P("img"),
            P("img", None),
            P("img"),
            P("vol", None),
            P(None, "vol", None, None),
            P(),
            P(),
            P(),
            P("vol", "img", None),
        ),
        out_specs=P(None, "vol", "img", None),
        check_vma=False,
    )
```

```python
import math
from functools import partial

import jax
import jax.numpy as jnp
from jax import lax
from jax.experimental import pallas as pl
from jax.experimental.pallas import tpu as pltpu
from jax.sharding import PartitionSpec as P

ROWS = 256
COLS = 128
K = 64
TRANS = 4
LMAX = 8
AMPLITUDE = 0.1
VMEM_LIMIT = 56 * 1024 * 1024
BF16 = jnp.bfloat16
F32 = jnp.float32


def params(steps):
    return pltpu.CompilerParams(
        dimension_semantics=("arbitrary",) * steps, vmem_limit_bytes=VMEM_LIMIT
    )


def smem():
    return pl.BlockSpec(memory_space=pltpu.SMEM)


def vmem():
    return pl.BlockSpec(memory_space=pltpu.VMEM)


def cost(us):
    return pl.CostEstimate(flops=0, transcendentals=0, bytes_accessed=int(us * 3.69e6))


def hbm():
    return pl.BlockSpec(memory_space=pl.ANY)


def shift_phases(row_freq, col_freq, number):
    shift_ids = jnp.arange(number)
    shift_x = (shift_ids % 2).astype(F32) - 0.5
    shift_y = (shift_ids // 2).astype(F32) - 0.5
    angle = (
        -2.0
        * math.pi
        * (
            shift_x[:, None, None] * col_freq[None, None, :]
            + shift_y[:, None, None] * row_freq[None, :, None]
        )
    )
    return (jnp.cos(angle), jnp.sin(angle))


def along_z(n_vol, shift):
    count = n_vol // 2
    return [(v, (v // 2 + shift) % count * 2 + v % 2) for v in range(n_vol)]


def flip(number, mask):
    return [(v, v ^ mask) for v in range(number)]


def ring_of(n_vol):
    return list(range(0, n_vol, 2)) + list(range(n_vol - 1, 0, -2))


def extract_kernel(rows, planes_here, *refs):
    plane_ref, line_ref, weight_hbm, vol_hbm, keep_a, send_a = refs[:6]
    vol, pair, idx_v, flag_v, idx_s, flag_s, w_s, sem = refs[-8:]
    parts_b = refs[6:-8]
    slab = lax.axis_index("vol")
    share = idx_v.shape[0] // 2
    first = lax.axis_index("img") * share
    height = planes_here * ROWS
    count_z = keep_a.shape[0]
    groups_a = keep_a.shape[2] // 16
    groups_b = parts_b[0].shape[2] // 16
    load = pltpu.make_async_copy(vol_hbm, vol.at[:, :height, :], sem.at[0])
    load.start()
    loads_w = [
        pltpu.make_async_copy(
            weight_hbm.at[pl.ds(first, share), pl.ds(h * COLS, COLS)],
            w_s.at[pl.ds(h * share, share), :],
            sem.at[4 + h],
        )
        for h in range(2)
    ]
    for copy in loads_w:
        copy.start()
    local = plane_ref[pl.ds(first, share), :] - slab * planes_here
    owned = (local >= 0) & (local < planes_here)
    idx = jnp.where(owned, local * ROWS + line_ref[pl.ds(first, share), :], height)
    for h in range(2):
        idx_v[h * share : (h + 1) * share, :] = idx[:, h * COLS : (h + 1) * COLS]
    eights = (
        lax.broadcasted_iota(jnp.int32, (ROWS, COLS), 0) >> 3
        == lax.broadcasted_iota(jnp.int32, (ROWS, COLS), 1)
    )
    flag_v[...] = jnp.dot(
        owned.astype(F32).astype(BF16), eights.astype(F32).astype(BF16), preferred_element_type=F32
    ).astype(jnp.int32)
    to_idx = pltpu.make_async_copy(idx_v, idx_s, sem.at[2])
    to_flag = pltpu.make_async_copy(flag_v, flag_s, sem.at[3])
    to_idx.start()
    to_flag.start()
    vol[:, height : height + 8, :] = jnp.zeros((2, 8, COLS), F32)
    for ref in (keep_a, send_a) + parts_b:
        ref[...] = jnp.zeros_like(ref)
    to_idx.wait()
    to_flag.wait()
    for copy in loads_w:
        copy.wait()
    load.wait()
    lower_row = lax.broadcasted_iota(jnp.int32, (2, COLS), 0) == 0
    shift = rows.bit_length() - 1

    def fill(out, lead, block, skip, groups):
        def group_step(g, carry):
            base = pl.multiple_of(g * 16, 16)
            at = []
            for h in range(2):
                n = (skip + g) * 16 + 8 * h
                at.append((n >> shift, block * rows + (n & (rows - 1))))
            hits = flag_s[at[0][0], at[0][1] >> 3] + flag_s[at[1][0], at[1][1] >> 3]

            @pl.when(hits > 0)
            def _():
                spot = [(k + share * (r >> 7), r & (COLS - 1)) for k, r in at]
                for u in range(16):
                    line, lane = spot[u // 8]
                    i = idx_s[line, lane + u % 8]
                    w = w_s[line, lane + u % 8]
                    both = jnp.where(lower_row, w, 1.0 - w)
                    for j in range(2):
                        pair[j, 2 * u : 2 * u + 2, :] = both * vol[j, pl.ds(i, 2), :]
                for j in range(2):
                    value = pair[j, pl.ds(0, 16, stride=2), :] + pair[j, pl.ds(1, 16, stride=2), :]
                    out[lead, j, pl.ds(base, 16), :] = value.astype(BF16)

            return carry

        lax.fori_loop(0, groups, group_step, 0)

    for dz in range(count_z):
        for dy in range(2):
            z = (slab >> 1) + dz
            block = jnp.where(z >= count_z, z - count_z, z) * 2 + ((slab + dy) & 1)
            fill((keep_a, send_a)[dy], dz, block, 0, groups_a)
            fill(parts_b[dz], dy, block, groups_a, groups_b)


def extract(volume, row_plane, row_line, row_weight, n_vol, share, share_a):
    planes_here = volume.shape[1]
    rows = ROWS // n_vol
    count_z = n_vol // 2
    shape_a = jax.ShapeDtypeStruct((count_z, 2, share_a * rows, COLS), BF16)
    shape_b = jax.ShapeDtypeStruct((2, 2, (share - share_a) * rows, COLS), BF16)
    return pl.pallas_call(
        partial(extract_kernel, rows, planes_here),
        out_shape=[shape_a, shape_a] + [shape_b] * count_z,
        in_specs=[vmem(), vmem(), hbm(), hbm()],
        out_specs=[vmem()] * (2 + count_z),
        scratch_shapes=[
            pltpu.VMEM((2, planes_here * ROWS + 8, COLS), F32),
            pltpu.VMEM((2, 32, COLS), F32),
            pltpu.VMEM((2 * share, COLS), jnp.int32),
            pltpu.VMEM((share, COLS), jnp.int32),
            pltpu.SMEM((2 * share, COLS), jnp.int32),
            pltpu.SMEM((share, COLS), jnp.int32),
            pltpu.SMEM((2 * share, COLS), F32),
            pltpu.SemaphoreType.DMA((6,)),
        ],
        compiler_params=pltpu.CompilerParams(vmem_limit_bytes=VMEM_LIMIT),
        cost_estimate=cost(11),
        name="extract",
    )(row_plane, row_line, row_weight, volume.reshape(2, planes_here * ROWS, COLS))


def combine_first_kernel(keep_a, got_a, keep_b, *rest):
    count_z = keep_a.shape[0]
    got_b = rest[: count_z - 1]
    out_a = rest[count_z : 2 * count_z]
    out_b = rest[2 * count_z :]
    for d in range(count_z):
        out_a[d][...] = keep_a[d] + got_a[d]
    for d in range(2):
        total = keep_b[d]
        for ref in got_b:
            total = total + ref[d]
        out_b[d][...] = total


def to_pixel_rows(messages, n_vol, first_with):
    keep_a, send_a, keep_b = messages[:3]
    count_z = n_vol // 2
    got_b = [lax.ppermute(m, "vol", along_z(n_vol, d + 1)) for d, m in enumerate(messages[3:])]
    got_a = lax.ppermute(send_a, "vol", flip(n_vol, 1))
    shape_a = jax.ShapeDtypeStruct(keep_a.shape[1:], BF16)
    shape_b = jax.ShapeDtypeStruct(keep_b.shape[1:], BF16)
    sums = pl.pallas_call(
        combine_first_kernel,
        out_shape=[shape_a] * count_z + [shape_b] * 2,
        in_specs=[vmem()] * (2 + count_z) + [hbm()],
        out_specs=[vmem()] * (count_z + 2),
        compiler_params=pltpu.CompilerParams(vmem_limit_bytes=VMEM_LIMIT),
        cost_estimate=cost(3),
        name="combine_first",
    )(keep_a, got_a, keep_b, *got_b, first_with)
    sums_a, sums_b = sums[:count_z], sums[count_z:]
    moved_b = lax.ppermute(sums_b[1], "vol", flip(n_vol, 1))
    moved = [lax.ppermute(sums_a[d], "vol", along_z(n_vol, d)) for d in range(1, count_z)]
    out_b = sums_b[0] + moved_b
    out_a = sum(moved, sums_a[0])
    return out_a, out_b


def from_partners(x, n_img):
    return [x] + [lax.ppermute(x, "img", flip(n_img, m)) for m in range(1, n_img)]


def ring_gather(x, n_vol):
    ring = ring_of(n_vol)
    ahead = [(ring[p], ring[(p + 1) % n_vol]) for p in range(n_vol)]
    back = [(b, a) for a, b in ahead]
    pieces = [x]
    one = two = x
    for _ in range(1, n_vol // 2):
        one = lax.ppermute(one, "vol", ahead)
        two = lax.ppermute(two, "vol", back)
        pieces += [one, two]

    def farthest(after):
        half = x.shape[1] // 2
        low, high = halves(one, two, after)
        return [lax.ppermute(low, "vol", ahead), lax.ppermute(high, "vol", back)]

    return pieces, farthest


def halves_kernel(one, two, after, low, high):
    half = low.shape[1]
    low[...] = one[:, :half]
    high[...] = two[:, half:]


def halves(one, two, after):
    shape = jax.ShapeDtypeStruct((one.shape[0], one.shape[1] // 2, COLS), BF16)
    return pl.pallas_call(
        halves_kernel,
        out_shape=[shape] * 2,
        in_specs=[vmem(), vmem(), hbm()],
        out_specs=[vmem()] * 2,
        compiler_params=pltpu.CompilerParams(vmem_limit_bytes=VMEM_LIMIT),
        cost_estimate=cost(1),
        name="halves",
    )(one, two, after)


def weigh_kernel(img_ref, sa_ref, ca_ref, sx_ref, cx_ref, nw_ref, wt_ref, sq_ref, buf):
    count = img_ref.shape[1]
    rows = img_ref.shape[2]
    pitch = rows + 1
    for j in range(2):
        for b in range(count):
            buf[j, b * pitch : b * pitch + rows, :] = img_ref[j, b].astype(F32)
    sx = sx_ref[...]
    cx = cx_ref[...]
    for r in range(rows):
        contrast = -(sa_ref[:, r : r + 1] * cx + ca_ref[:, r : r + 1] * sx)
        noise = nw_ref[r : r + 1, :]
        scale = contrast * noise
        for j in range(2):
            x = buf[j, pl.ds(r, count, stride=pitch), :]
            wt_ref[r, :, j * COLS : (j + 1) * COLS] = (scale * x).astype(BF16)
        sq_ref[r] = (contrast * contrast * noise).astype(BF16)


def weigh(images, defocus, noise_weight, row_freq, col_freq):
    count = images.shape[1]
    rows = images.shape[2]
    step = 64
    angle_r = defocus[:, None] * (row_freq * row_freq)[None, :] + math.asin(AMPLITUDE)
    angle_c = defocus[:, None] * (col_freq * col_freq)[None, :]
    return pl.pallas_call(
        weigh_kernel,
        grid=(count // step,),
        out_shape=[
            jax.ShapeDtypeStruct((rows, count, 2 * COLS), BF16),
            jax.ShapeDtypeStruct((rows, count, COLS), BF16),
        ],
        in_specs=[
            pl.BlockSpec((2, step, rows, COLS), lambda b: (0, b, 0, 0)),
            pl.BlockSpec((step, rows), lambda b: (b, 0)),
            pl.BlockSpec((step, rows), lambda b: (b, 0)),
            pl.BlockSpec((step, COLS), lambda b: (b, 0)),
            pl.BlockSpec((step, COLS), lambda b: (b, 0)),
            pl.BlockSpec((rows, COLS), lambda b: (0, 0)),
        ],
        out_specs=[
            pl.BlockSpec((rows, step, 2 * COLS), lambda b: (0, b, 0)),
            pl.BlockSpec((rows, step, COLS), lambda b: (0, b, 0)),
        ],
        scratch_shapes=[pltpu.VMEM((2, step * (rows + 1), COLS), F32)],
        compiler_params=params(1),
        cost_estimate=cost(12),
        name="weigh",
    )(
        images,
        jnp.sin(angle_r),
        jnp.cos(angle_r),
        jnp.sin(angle_c),
        jnp.cos(angle_c),
        noise_weight,
    )


def logits_kernel(wt_ref, sq_ref, cos_ref, sin_ref, cand_ref, *rest):
    sl_refs = rest[1:-4]
    out_ref, part, acc, quad = rest[-4:]
    step = pl.program_id(0)
    groups = len(sl_refs) // 2
    rows = part.shape[1] // K - 1
    share = K // groups
    pitch = rows + 1
    inner = wt_ref.shape[0]

    @pl.when(step == 0)
    def _():
        for m in range(groups):
            at = m * share
            for ref in sl_refs[2 * m : 2 * m + 2]:
                for j in range(2):
                    for k in range(ref.shape[1] // rows):
                        row = (at + k) * pitch
                        part[j, row : row + rows, :] = ref[j, k * rows : (k + 1) * rows].astype(F32)
                at += ref.shape[1] // rows
        acc[...] = jnp.zeros_like(acc)
        quad[...] = jnp.zeros_like(quad)

    dims = (((1,), (1,)), ((), ()))
    total = acc[...]
    total_q = quad[...]
    for u in range(inner):
        re = part[0, pl.ds(step * inner + u, K, stride=pitch), :]
        im = part[1, pl.ds(step * inner + u, K, stride=pitch), :]
        shifted = []
        for t in range(TRANS):
            c = cos_ref[t, u : u + 1, :]
            s = sin_ref[t, u : u + 1, :]
            shifted.append(
                jnp.concatenate(
                    [(c * re - s * im).astype(BF16), (s * re + c * im).astype(BF16)], axis=1
                )
            )
        left = jnp.concatenate(shifted, axis=0)
        power = (re * re + im * im).astype(BF16)
        total = total + lax.dot_general(left, wt_ref[u], dims, preferred_element_type=F32)
        total_q = total_q + lax.dot_general(power, sq_ref[u], dims, preferred_element_type=F32)
    acc[...] = total
    quad[...] = total_q

    @pl.when(step == pl.num_programs(0) - 1)
    def _():
        ids = lax.broadcasted_iota(jnp.int32, quad.shape, 0) ^ (lax.axis_index("img") * share)
        half = 0.5 * quad[...]
        for t in range(TRANS):
            value = acc[t * K : (t + 1) * K, :] - half
            for l in range(LMAX):
                pick = jnp.where(ids == cand_ref[l : l + 1, :], value, 0.0)
                out_ref[t * LMAX + l : t * LMAX + l + 1, :] = jnp.sum(pick, axis=0, keepdims=True)


def candidate_logits(after, slices, weighted, squared, cosine, sine, cand):
    rows, count = squared.shape[:2]
    inner = 8
    return pl.pallas_call(
        logits_kernel,
        grid=(rows // inner,),
        out_shape=jax.ShapeDtypeStruct((TRANS * LMAX, count), F32),
        in_specs=[
            pl.BlockSpec((inner, count, 2 * COLS), lambda s: (s, 0, 0)),
            pl.BlockSpec((inner, count, COLS), lambda s: (s, 0, 0)),
            pl.BlockSpec((TRANS, inner, COLS), lambda s: (0, s, 0)),
            pl.BlockSpec((TRANS, inner, COLS), lambda s: (0, s, 0)),
            pl.BlockSpec((LMAX, count), lambda s: (0, 0)),
        ]
        + [hbm()]
        + [pl.BlockSpec(x.shape, lambda s: (0, 0, 0)) for x in slices],
        out_specs=pl.BlockSpec((TRANS * LMAX, count), lambda s: (0, 0)),
        scratch_shapes=[
            pltpu.VMEM((2, K * (rows + 1), COLS), F32),
            pltpu.VMEM((TRANS * K, count), F32),
            pltpu.VMEM((K, count), F32),
        ],
        compiler_params=params(1),
        cost_estimate=cost(8),
        name="logits",
    )(weighted, squared, cosine, sine, cand, after, *slices)


def posterior_rows(logits, counts):
    place = lax.broadcasted_iota(jnp.int32, logits.shape, 0) % LMAX
    allowed = place < counts
    masked = jnp.where(allowed, logits, -1e30)
    highest = jnp.max(masked, axis=0, keepdims=True)
    exponent = jnp.where(allowed, jnp.exp(masked - highest), 0.0)
    return (exponent / jnp.sum(exponent, axis=0, keepdims=True)).astype(BF16).astype(F32)


def list_rows(num, src_s, len_s, outs, pick):
    parts = 2 * outs[0].shape[0]
    cap = outs[0].shape[2]
    comps = num.shape[0]
    lead = src_s.shape[0] // parts
    group = lax.axis_index("img")
    for m in range(parts):
        q = group ^ m

        def turn(g, carry, q=q, m=m):
            base = pl.multiple_of(g * 32, 32)
            at = q * lead + base
            for u in range(32):
                s = src_s[at + u]
                for c in range(comps):
                    pick[c, u : u + 1, :] = num[c, pl.ds(s, 1), :]
            for c in range(comps):
                outs[m % 2][m // 2, c, pl.ds(base, 32), :] = pick[c].astype(BF16)
            return carry

        lax.fori_loop(0, (jnp.minimum(len_s[q, 0], cap) + 31) // 32, turn, 0)


def project_kernel(src_s, len_s, cand_ref, cnt_ref, wt_ref, sq_ref, cos_ref, sin_ref, *rest):
    lg_refs = rest[:-6]
    keep_ref, send_ref, post, post_sum, num, pick = rest[-6:]
    step = pl.program_id(0)
    inner = wt_ref.shape[0]

    @pl.when(step == 0)
    def _():
        prob = posterior_rows(sum([ref[...] for ref in lg_refs[1:]], lg_refs[0][...]), cnt_ref[...])
        ids = lax.broadcasted_iota(jnp.int32, (K, prob.shape[1]), 0)
        total = jnp.zeros((K, prob.shape[1]), F32)
        for t in range(TRANS):
            dense = jnp.zeros((K, prob.shape[1]), F32)
            for l in range(LMAX):
                at = t * LMAX + l
                dense = jnp.where(ids == cand_ref[l : l + 1, :], dense + prob[at : at + 1, :], dense)
            post[t * K : (t + 1) * K, :] = dense.astype(BF16)
            total = total + dense
        high = total.astype(BF16)
        post_sum[:K, :] = high
        post_sum[K:, :] = (total - high.astype(F32)).astype(BF16)

    for u in range(inner):
        y = jnp.dot(post[...], wt_ref[u], preferred_element_type=F32)
        d = jnp.dot(post_sum[...], sq_ref[u], preferred_element_type=F32)
        re = jnp.zeros((K, COLS), F32)
        im = jnp.zeros((K, COLS), F32)
        for t in range(TRANS):
            c = cos_ref[t, u : u + 1, :]
            s = sin_ref[t, u : u + 1, :]
            y_re = y[t * K : (t + 1) * K, :COLS]
            y_im = y[t * K : (t + 1) * K, COLS:]
            re = re + (c * y_re + s * y_im)
            im = im + (c * y_im - s * y_re)
        base = pl.multiple_of((step * inner + u) * K, K)
        num[0, pl.ds(base, K), :] = re
        num[1, pl.ds(base, K), :] = im
        num[2, pl.ds(base, K), :] = d[:K] + d[K:]

    @pl.when(step == pl.num_programs(0) - 1)
    def _():
        list_rows(num, src_s, len_s, (keep_ref, send_ref), pick)


def project(src, lengths, n_img, logits, cand, counts, weighted, squared, cosine, sine, cap):
    rows, count = squared.shape[:2]
    inner = 8
    shape = (n_img // 2, 3, cap, COLS)
    return pl.pallas_call(
        project_kernel,
        grid=(rows // inner,),
        out_shape=[jax.ShapeDtypeStruct(shape, BF16)] * 2,
        in_specs=[
            smem(),
            smem(),
            pl.BlockSpec((LMAX, count), lambda s: (0, 0)),
            pl.BlockSpec((1, count), lambda s: (0, 0)),
            pl.BlockSpec((inner, count, 2 * COLS), lambda s: (s, 0, 0)),
            pl.BlockSpec((inner, count, COLS), lambda s: (s, 0, 0)),
            pl.BlockSpec((TRANS, inner, COLS), lambda s: (0, s, 0)),
            pl.BlockSpec((TRANS, inner, COLS), lambda s: (0, s, 0)),
        ]
        + [pl.BlockSpec((TRANS * LMAX, count), lambda s: (0, 0)) for _ in logits],
        out_specs=[pl.BlockSpec(shape, lambda s: (0, 0, 0, 0))] * 2,
        scratch_shapes=[
            pltpu.VMEM((TRANS * K, count), BF16),
            pltpu.VMEM((2 * K, count), BF16),
            pltpu.VMEM((3, rows * K, COLS), F32),
            pltpu.VMEM((3, 32, COLS), F32),
        ],
        compiler_params=params(1),
        cost_estimate=cost(12),
        name="project",
    )(src, lengths, cand, counts, weighted, squared, cosine, sine, *logits)


def to_member(keep, send, n_img):
    got = lax.ppermute(send, "img", flip(n_img, 1))
    summed = [keep[m] + got[m] for m in range(n_img // 2)]
    moved = [lax.ppermute(summed[m], "img", flip(n_img, 2 * m)) for m in range(1, n_img // 2)]
    return sum(moved, summed[0])


HEAD = 8


def line_stride(lines_here):
    return lines_here + 2 * HEAD


def insert_kernel(start, count, has_acc, mode, len_s, code_s, wgt_s, *rest):
    pieces = rest[:count]
    rest = rest[count:]
    out_ref, acc, acc_odd, buf = rest[-4:]
    extra = rest[:-4]
    both_acc = (acc, acc_odd)
    comps, cap = buf.shape[:2]
    blocks = len_s.shape[0]
    lead = code_s.shape[0] // blocks
    slab = lax.axis_index("vol")
    place = jnp.where(slab & 1, blocks - 1 - (slab >> 1), slab >> 1)
    if has_acc:
        pltpu.sync_copy(extra[-1], acc)
    else:
        acc[...] = jnp.zeros_like(acc)
    acc_odd[...] = jnp.zeros_like(acc_odd)
    first = lax.broadcasted_iota(jnp.int32, (2, COLS), 0) == 0
    index = 0
    while index < count:
        m = start + index
        whole = pieces[index].shape[1] == cap
        for c in range(comps):
            if whole:
                buf[c] = pieces[index][c].astype(F32)
            else:
                buf[c, : cap // 2, :] = pieces[index][c].astype(F32)
                buf[c, cap // 2 :, :] = pieces[index + 1][c].astype(F32)
        if whole:
            index += 1
        else:
            index += 2
        from_place = place + ((m + 1) // 2) * (-1 if m % 2 else 1)
        from_place = from_place & (blocks - 1)
        block = jnp.where(
            from_place >= blocks // 2, 2 * (blocks - 1 - from_place) + 1, 2 * from_place
        )

        def group_step(g, carry, block=block):
            at = block * lead + g * 4
            for u in range(4):
                code = code_s[at + u]
                s = code & 1023
                to = code >> 10
                w = wgt_s[at + u]
                both = jnp.where(first, w, 1.0 - w)
                into = both_acc[u % 2]
                for c in range(comps):
                    row = jnp.broadcast_to(buf[c, pl.ds(s, 1), :], (2, COLS))
                    into[c, pl.ds(to, 2), :] = into[c, pl.ds(to, 2), :] + both * row
            return carry

        lax.fori_loop(0, (jnp.minimum(len_s[block, 0], cap) + 3) // 4, group_step, 0)

    if mode == "sum":
        acc[...] = acc[...] + acc_odd[...]
        pltpu.sync_copy(acc, out_ref)
        return
    planes, lines_here = extra[0].shape[:2]
    stride = line_stride(lines_here)

    def plane_step(p, carry):
        base = pl.multiple_of(p * stride + HEAD, 8)
        total = [
            acc[c, pl.ds(base, lines_here), :] + acc_odd[c, pl.ds(base, lines_here), :]
            for c in range(3)
        ]
        inverse = 1.0 / (total[2] + extra[0][p])
        out_ref[0, p] = total[0] * inverse
        out_ref[1, p] = total[1] * inverse
        return carry

    lax.fori_loop(0, planes, plane_step, 0)


def insert(tables, start, pieces, cap, block, mode, extra=(), acc=None):
    comps = pieces[0].shape[0]
    planes, lines_here = block
    acc_shape = (comps, planes * line_stride(lines_here), COLS)
    out = {
        "sum": acc_shape,
        "result": (2, planes, lines_here, COLS),
    }[mode]
    more = list(extra) + ([] if acc is None else [acc])
    return pl.pallas_call(
        partial(insert_kernel, start, len(pieces), acc is not None, mode),
        out_shape=jax.ShapeDtypeStruct(out, F32),
        in_specs=[smem()] * 3
        + [vmem()] * (len(pieces) + len(extra))
        + [hbm()] * (acc is not None),
        out_specs=hbm() if mode == "sum" else vmem(),
        scratch_shapes=[pltpu.VMEM(acc_shape, F32)] * 2
        + [pltpu.VMEM((comps, cap, COLS), F32)],
        compiler_params=pltpu.CompilerParams(vmem_limit_bytes=VMEM_LIMIT),
        cost_estimate=cost(6),
        name="insert_" + mode,
    )(*tables, *pieces, *more)


def running(x):
    lanes = lax.broadcasted_iota(jnp.int32, x.shape, 1)
    step = 1
    while step < x.shape[1]:
        x = x + jnp.where(lanes >= step, pltpu.roll(x, step, 1), 0)
        step *= 2
    return x


def split_index(x):
    return [(x >> 5).astype(F32), (x & 31).astype(F32)]


def split_weight(w):
    a = w.astype(BF16).astype(F32)
    b = (w - a).astype(BF16).astype(F32)
    return [a, b, w - a - b]


def compacted(member, rank, values, lead):
    high = jnp.where(member, rank >> 5, -1)
    low = rank & 31
    spot = lax.broadcasted_iota(jnp.int32, (4 * lead, rank.shape[1]), 0)
    shift = lead.bit_length() - 1
    left = ((spot & (lead - 1)) * 4 + (spot >> shift)) == high
    hot = lax.broadcasted_iota(jnp.int32, (32, rank.shape[1]), 0) == low
    right = jnp.concatenate([jnp.where(hot, v, 0.0).astype(BF16) for v in values], axis=0)
    out = lax.dot_general(
        left.astype(F32).astype(BF16), right, (((1,), (1,)), ((), ())), preferred_element_type=F32
    )
    return [
        jnp.concatenate(
            [out[h * lead : (h + 1) * lead, 32 * i : 32 * (i + 1)] for h in range(4)], axis=1
        )
        for i in range(len(values))
    ]


def lists_kernel(
    n_img, planes_here, lines_here, cap,
    plane_ref, line_ref, wgt_ref,
    src_ref, code_ref, w_ref, send_len, recv_len, longest, own,
):
    slab = lax.axis_index("vol")
    group = lax.axis_index("img")
    blocks, number = line_ref.shape
    lead = src_ref.shape[0] // n_img
    lines = line_ref[...]

    def in_part(x, part):
        return (x >= part * lines_here - 1) & (x < (part + 1) * lines_here)

    top = jnp.zeros((blocks, COLS), jnp.int32)
    for q in range(n_img):
        size = jnp.sum(in_part(lines, q).astype(F32), axis=1, keepdims=True).astype(jnp.int32)
        top = jnp.maximum(top, jnp.broadcast_to(size, (blocks, COLS)))
    longest[...] = jnp.broadcast_to(jnp.max(top.astype(F32)), (8, COLS)).astype(jnp.int32)

    own[...] = jnp.broadcast_to(line_ref[pl.ds(slab, 1), :], own.shape)
    sent = in_part(own[...], lax.broadcasted_iota(jnp.int32, own.shape, 0))
    total = running(sent.astype(jnp.int32))
    send_len[...] = jnp.broadcast_to(total[:, number - 1 :], send_len.shape)
    rank = total - sent.astype(jnp.int32)
    row_ids = split_index(lax.broadcasted_iota(jnp.int32, (1, number), 1))
    for q in range(n_img):
        out = compacted(sent[q : q + 1], rank[q : q + 1], row_ids, lead)
        src_ref[q * lead : (q + 1) * lead, :] = (32.0 * out[0] + out[1]).astype(jnp.int32)

    member = in_part(lines, group)
    place = running(member.astype(jnp.int32)) - member.astype(jnp.int32)
    place = jnp.minimum(place, cap - 1)
    local = plane_ref[...] - slab * planes_here
    here = member & (local >= 0) & (local < planes_here)
    total = running(here.astype(jnp.int32))
    recv_len[...] = jnp.broadcast_to(total[:, number - 1 :], recv_len.shape)
    rank = total - here.astype(jnp.int32)
    target = local * line_stride(lines_here) + lines - group * lines_here + HEAD
    target = jnp.where(here, target, 0)
    for v in range(blocks):
        row = slice(v, v + 1)
        values = split_index(place[row]) + split_index(target[row]) + split_weight(wgt_ref[row, :])
        out = compacted(here[row], rank[row], values, lead)
        at = slice(v * lead, (v + 1) * lead)
        code_ref[at, :] = (
            32768.0 * out[2] + 1024.0 * out[3] + 32.0 * out[0] + out[1]
        ).astype(jnp.int32)
        w_ref[at, :] = out[4] + out[5] + out[6]


def lists(row_plane, row_line, row_weight, n_vol, n_img, planes_here, lines_here, cap):
    lead = 8
    assert cap <= lead * COLS
    number = ROWS // n_vol * K

    def order(x):
        return x.T.reshape(n_vol, number)

    def table(blocks, dtype=jnp.int32):
        return jax.ShapeDtypeStruct((blocks * lead, COLS), dtype)

    return pl.pallas_call(
        partial(lists_kernel, n_img, planes_here, lines_here, cap),
        out_shape=[
            table(n_img),
            table(n_vol),
            table(n_vol, F32),
            jax.ShapeDtypeStruct((8, COLS), jnp.int32),
            jax.ShapeDtypeStruct((n_vol, COLS), jnp.int32),
            jax.ShapeDtypeStruct((8, COLS), jnp.int32),
        ],
        in_specs=[vmem()] * 3,
        out_specs=[vmem()] * 6,
        scratch_shapes=[pltpu.VMEM((8, number), jnp.int32)],
        compiler_params=pltpu.CompilerParams(vmem_limit_bytes=VMEM_LIMIT),
        cost_estimate=cost(6),
        name="lists",
    )(order(row_plane), order(row_line), order(row_weight))


def insert_into(carry, piece, planes_all, lines_all, weights_all, slab_id, planes_here):
    local_plane = planes_all - slab_id * planes_here
    in_slab = (local_plane >= 0) & (local_plane < planes_here)
    dump_row = planes_here * ROWS
    lower_index = jnp.where(in_slab, local_plane * ROWS + lines_all, dump_row).reshape(-1)
    upper_index = jnp.where(in_slab, lower_index.reshape(in_slab.shape) + 1, dump_row).reshape(-1)
    values = piece.reshape(-1, 3 * COLS)
    weight = weights_all.reshape(-1, 1)
    carry = carry.at[lower_index].add(weight * values)
    return carry.at[upper_index].add((1.0 - weight) * values)


def dense_path(
    logits, cand, counts, weighted, squared, cosine, sine,
    plane_share, line_share, weight_share, regularizer, slab_id,
):
    prob = posterior_rows(logits, counts).reshape(TRANS, LMAX, -1)
    hot = (cand[:, None, :] == jnp.arange(K)[None, :, None]).astype(F32)
    post = jnp.einsum("tlb,lkb->tkb", prob, hot).astype(BF16)
    y = jnp.einsum("tkb,rbz->tkrz", post, weighted, preferred_element_type=F32)
    d = jnp.einsum("tkb,rbc->krc", post, squared, preferred_element_type=F32)
    y_re = y[..., :COLS]
    y_im = y[..., COLS:]
    num_re = jnp.sum(cosine[:, None] * y_re + sine[:, None] * y_im, axis=0)
    num_im = jnp.sum(cosine[:, None] * y_im - sine[:, None] * y_re, axis=0)
    partial_value = lax.psum_scatter(
        jnp.stack([num_re, num_im, d], axis=2), "img", scatter_dimension=0, tiled=True
    )
    planes_here = regularizer.shape[0]
    inserted = insert_into(
        jnp.zeros((planes_here * ROWS + 1, 3 * COLS), F32),
        lax.all_gather(partial_value, "vol", axis=1, tiled=True),
        plane_share,
        line_share,
        weight_share,
        slab_id,
        planes_here,
    )
    slab = inserted[: planes_here * ROWS].reshape(planes_here, ROWS, 3, COLS)
    summed = lax.psum_scatter(slab, "img", scatter_dimension=1, tiled=True)
    denom = summed[:, :, 2] + regularizer
    return jnp.stack([summed[:, :, 0] / denom, summed[:, :, 1] / denom], axis=0)


def body(
    images, defocus, candidates, counts, noise_weight, volume,
    row_plane, row_line, row_weight, regularizer,
):
    rows = noise_weight.shape[0]
    planes_here = volume.shape[1]
    lines_here = regularizer.shape[1]
    slab_id = lax.axis_index("vol")
    group_id = lax.axis_index("img")
    n_vol = lax.axis_size("vol")
    n_img = lax.axis_size("img")
    global_rows = slab_id * rows + jnp.arange(rows)
    row_freq = (global_rows.astype(F32) - ROWS // 2) / ROWS
    col_freq = jnp.arange(COLS).astype(F32) / (2 * COLS)
    share = K // n_img
    first = group_id * share
    plane_share = lax.dynamic_slice_in_dim(row_plane, first, share, 0)
    line_share = lax.dynamic_slice_in_dim(row_line, first, share, 0)
    weight_share = lax.dynamic_slice_in_dim(row_weight, first, share, 0)

    aligned = max(1, 16 // rows)
    share_a = share * 11 // 16 // aligned * aligned
    messages = extract(volume, row_plane, row_line, row_weight, n_vol, share, share_a)
    cosine, sine = shift_phases(row_freq, col_freq, TRANS)
    weighted, squared = weigh(images, defocus, noise_weight, row_freq, col_freq)
    mean = rows * K // n_img
    cap = -(-int(mean + 4.2 * math.sqrt(mean)) // 32) * 32
    src, code, wgt, send_len, recv_len, longest = lists(
        row_plane, row_line, row_weight, n_vol, n_img, planes_here, lines_here, cap
    )
    own_a, own_b = to_pixel_rows(messages, n_vol, weighted)
    slices_b = from_partners(own_b, n_img)
    slices_a = from_partners(own_a, n_img)
    slices = [x for both in zip(slices_a, slices_b) for x in both]
    cand = candidates.T
    count_row = counts[None, :]
    partial_logits = candidate_logits(code, slices, weighted, squared, cosine, sine, cand)
    pair_logits = partial_logits + lax.ppermute(partial_logits, "vol", flip(n_vol, 1))
    logits = [pair_logits] + [
        lax.ppermute(pair_logits, "vol", along_z(n_vol, d)) for d in range(1, n_vol // 2)
    ]

    keep, send = project(
        src.reshape(-1), send_len, n_img, logits, cand, count_row, weighted, squared, cosine, sine, cap
    )
    pieces, farthest = ring_gather(to_member(keep, send, n_img), n_vol)
    tables = (recv_len, code.reshape(-1), wgt.reshape(-1))
    block = (planes_here, lines_here)
    early = n_vol - 3
    late = n_vol - 1
    part_sum = insert(tables, 0, pieces[:early], cap, block, "sum")
    last = farthest(part_sum)
    most_sum = insert(tables, early, pieces[early:], cap, block, "sum", acc=part_sum)

    def listed():
        return insert(tables, late, last, cap, block, "result", [regularizer], most_sum)

    def dense():
        return dense_path(
            sum(logits[1:], logits[0]), cand, count_row, weighted, squared, cosine, sine,
            plane_share, line_share, weight_share, regularizer, slab_id,
        )

    return lax.cond(longest[0, 0] <= cap, listed, dense)


def solution(mesh):
    return jax.shard_map(
        body,
        mesh=mesh,
        in_specs=(
            P(None, "img", "vol", None),
            P("img"),
            P("img", None),
            P("img"),
            P("vol", None),
            P(None, "vol", None, None),
            P(),
            P(),
            P(),
            P("vol", "img", None),
        ),
        out_specs=P(None, "vol", "img", None),
        check_vma=False,
    )
```

```python
import math
from functools import partial

import jax
import jax.numpy as jnp
from jax import lax
from jax.experimental import pallas as pl
from jax.experimental.pallas import tpu as pltpu
from jax.sharding import PartitionSpec as P

ROWS = 256
COLS = 128
K = 64
TRANS = 4
LMAX = 8
AMPLITUDE = 0.1
VMEM_LIMIT = 56 * 1024 * 1024
BF16 = jnp.bfloat16
F32 = jnp.float32


def params(steps):
    return pltpu.CompilerParams(
        dimension_semantics=("arbitrary",) * steps, vmem_limit_bytes=VMEM_LIMIT
    )


def smem():
    return pl.BlockSpec(memory_space=pltpu.SMEM)


def vmem():
    return pl.BlockSpec(memory_space=pltpu.VMEM)


def cost(us):
    return pl.CostEstimate(flops=0, transcendentals=0, bytes_accessed=int(us * 3.69e6))


def hbm():
    return pl.BlockSpec(memory_space=pl.ANY)


def shift_phases(row_freq, col_freq, number):
    shift_ids = jnp.arange(number)
    shift_x = (shift_ids % 2).astype(F32) - 0.5
    shift_y = (shift_ids // 2).astype(F32) - 0.5
    angle = (
        -2.0
        * math.pi
        * (
            shift_x[:, None, None] * col_freq[None, None, :]
            + shift_y[:, None, None] * row_freq[None, :, None]
        )
    )
    return (jnp.cos(angle), jnp.sin(angle))


def along_z(n_vol, shift):
    count = n_vol // 2
    return [(v, (v // 2 + shift) % count * 2 + v % 2) for v in range(n_vol)]


def flip(number, mask):
    return [(v, v ^ mask) for v in range(number)]


def ring_of(n_vol):
    return list(range(0, n_vol, 2)) + list(range(n_vol - 1, 0, -2))


def extract_kernel(rows, planes_here, *refs):
    plane_ref, line_ref, weight_hbm, vol_hbm, keep_a, send_a = refs[:6]
    vol, pair, idx_v, flag_v, idx_s, flag_s, w_s, sem = refs[-8:]
    parts_b = refs[6:-8]
    slab = lax.axis_index("vol")
    share = idx_v.shape[0] // 2
    first = lax.axis_index("img") * share
    height = planes_here * ROWS
    count_z = keep_a.shape[0]
    groups_a = keep_a.shape[2] // 16
    groups_b = parts_b[0].shape[2] // 16
    load = pltpu.make_async_copy(vol_hbm, vol.at[:, :height, :], sem.at[0])
    load.start()
    loads_w = [
        pltpu.make_async_copy(
            weight_hbm.at[pl.ds(first, share), pl.ds(h * COLS, COLS)],
            w_s.at[pl.ds(h * share, share), :],
            sem.at[4 + h],
        )
        for h in range(2)
    ]
    for copy in loads_w:
        copy.start()
    local = plane_ref[pl.ds(first, share), :] - slab * planes_here
    owned = (local >= 0) & (local < planes_here)
    idx = jnp.where(owned, local * ROWS + line_ref[pl.ds(first, share), :], height)
    for h in range(2):
        idx_v[h * share : (h + 1) * share, :] = idx[:, h * COLS : (h + 1) * COLS]
    eights = (
        lax.broadcasted_iota(jnp.int32, (ROWS, COLS), 0) >> 3
        == lax.broadcasted_iota(jnp.int32, (ROWS, COLS), 1)
    )
    flag_v[...] = jnp.dot(
        owned.astype(F32).astype(BF16), eights.astype(F32).astype(BF16), preferred_element_type=F32
    ).astype(jnp.int32)
    to_idx = pltpu.make_async_copy(idx_v, idx_s, sem.at[2])
    to_flag = pltpu.make_async_copy(flag_v, flag_s, sem.at[3])
    to_idx.start()
    to_flag.start()
    vol[:, height : height + 8, :] = jnp.zeros((2, 8, COLS), F32)
    for ref in (keep_a, send_a) + parts_b:
        ref[...] = jnp.zeros_like(ref)
    to_idx.wait()
    to_flag.wait()
    for copy in loads_w:
        copy.wait()
    load.wait()
    lower_row = lax.broadcasted_iota(jnp.int32, (2, COLS), 0) == 0
    shift = rows.bit_length() - 1

    def fill(out, lead, block, skip, groups):
        def one_group(g):
            base = pl.multiple_of(g * 16, 16)
            at = []
            for h in range(2):
                n = (skip + g) * 16 + 8 * h
                at.append((n >> shift, block * rows + (n & (rows - 1))))
            hits = flag_s[at[0][0], at[0][1] >> 3] + flag_s[at[1][0], at[1][1] >> 3]

            @pl.when(hits > 0)
            def _():
                spot = [(k + share * (r >> 7), r & (COLS - 1)) for k, r in at]
                for u in range(16):
                    line, lane = spot[u // 8]
                    i = idx_s[line, lane + u % 8]
                    w = w_s[line, lane + u % 8]
                    both = jnp.where(lower_row, w, 1.0 - w)
                    for j in range(2):
                        pair[j, 2 * u : 2 * u + 2, :] = both * vol[j, pl.ds(i, 2), :]
                for j in range(2):
                    value = pair[j, pl.ds(0, 16, stride=2), :] + pair[j, pl.ds(1, 16, stride=2), :]
                    out[lead, j, pl.ds(base, 16), :] = value.astype(BF16)

        def turn(g, carry):
            for i in range(per_turn):
                one_group(g * per_turn + i)
            return carry

        per_turn = 2 if groups % 2 == 0 else 1
        lax.fori_loop(0, groups // per_turn, turn, 0)

    for dz in range(count_z):
        for dy in range(2):
            z = (slab >> 1) + dz
            block = jnp.where(z >= count_z, z - count_z, z) * 2 + ((slab + dy) & 1)
            fill((keep_a, send_a)[dy], dz, block, 0, groups_a)
            fill(parts_b[dz], dy, block, groups_a, groups_b)


def extract(volume, row_plane, row_line, row_weight, n_vol, share, share_a):
    planes_here = volume.shape[1]
    rows = ROWS // n_vol
    count_z = n_vol // 2
    shape_a = jax.ShapeDtypeStruct((count_z, 2, share_a * rows, COLS), BF16)
    shape_b = jax.ShapeDtypeStruct((2, 2, (share - share_a) * rows, COLS), BF16)
    return pl.pallas_call(
        partial(extract_kernel, rows, planes_here),
        out_shape=[shape_a, shape_a] + [shape_b] * count_z,
        in_specs=[vmem(), vmem(), hbm(), hbm()],
        out_specs=[vmem()] * (2 + count_z),
        scratch_shapes=[
            pltpu.VMEM((2, planes_here * ROWS + 8, COLS), F32),
            pltpu.VMEM((2, 32, COLS), F32),
            pltpu.VMEM((2 * share, COLS), jnp.int32),
            pltpu.VMEM((share, COLS), jnp.int32),
            pltpu.SMEM((2 * share, COLS), jnp.int32),
            pltpu.SMEM((share, COLS), jnp.int32),
            pltpu.SMEM((2 * share, COLS), F32),
            pltpu.SemaphoreType.DMA((6,)),
        ],
        compiler_params=pltpu.CompilerParams(vmem_limit_bytes=VMEM_LIMIT),
        cost_estimate=cost(11),
        name="extract",
    )(row_plane, row_line, row_weight, volume.reshape(2, planes_here * ROWS, COLS))


def combine_first_kernel(keep_a, got_a, keep_b, *rest):
    count_z = keep_a.shape[0]
    got_b = rest[: count_z - 1]
    out_a = rest[count_z : 2 * count_z]
    out_b = rest[2 * count_z :]
    for d in range(count_z):
        out_a[d][...] = keep_a[d] + got_a[d]
    for d in range(2):
        total = keep_b[d]
        for ref in got_b:
            total = total + ref[d]
        out_b[d][...] = total


def to_pixel_rows(messages, n_vol, first_with):
    keep_a, send_a, keep_b = messages[:3]
    count_z = n_vol // 2
    got_b = [lax.ppermute(m, "vol", along_z(n_vol, d + 1)) for d, m in enumerate(messages[3:])]
    got_a = lax.ppermute(send_a, "vol", flip(n_vol, 1))
    shape_a = jax.ShapeDtypeStruct(keep_a.shape[1:], BF16)
    shape_b = jax.ShapeDtypeStruct(keep_b.shape[1:], BF16)
    sums = pl.pallas_call(
        combine_first_kernel,
        out_shape=[shape_a] * count_z + [shape_b] * 2,
        in_specs=[vmem()] * (2 + count_z) + [hbm()],
        out_specs=[vmem()] * (count_z + 2),
        compiler_params=pltpu.CompilerParams(vmem_limit_bytes=VMEM_LIMIT),
        cost_estimate=cost(3),
        name="combine_first",
    )(keep_a, got_a, keep_b, *got_b, first_with)
    sums_a, sums_b = sums[:count_z], sums[count_z:]
    moved_b = lax.ppermute(sums_b[1], "vol", flip(n_vol, 1))
    moved = [lax.ppermute(sums_a[d], "vol", along_z(n_vol, d)) for d in range(1, count_z)]
    out_b = sums_b[0] + moved_b
    out_a = sum(moved, sums_a[0])
    return out_a, out_b


def from_partners(x, n_img):
    return [x] + [lax.ppermute(x, "img", flip(n_img, m)) for m in range(1, n_img)]


def ring_gather(low, high, n_vol):
    ring = ring_of(n_vol)
    ahead = [(ring[p], ring[(p + 1) % n_vol]) for p in range(n_vol)]
    back = [(b, a) for a, b in ahead]
    pieces = [low, high]
    one = two = (low, high)
    for _ in range(1, n_vol // 2):
        one_low, two_low = lax.ppermute(one[0], "vol", ahead), lax.ppermute(two[0], "vol", back)
        one_high, two_high = lax.ppermute(one[1], "vol", ahead), lax.ppermute(two[1], "vol", back)
        one, two = (one_low, one_high), (two_low, two_high)
        pieces += [*one, *two]
    return pieces + [lax.ppermute(one[0], "vol", ahead), lax.ppermute(two[1], "vol", back)]


def weigh_kernel(img_ref, sa_ref, ca_ref, sx_ref, cx_ref, nw_ref, wt_ref, sq_ref, buf):
    count = img_ref.shape[1]
    rows = img_ref.shape[2]
    pitch = rows + 1
    for j in range(2):
        for b in range(count):
            buf[j, b * pitch : b * pitch + rows, :] = img_ref[j, b].astype(F32)
    sx = sx_ref[...]
    cx = cx_ref[...]
    for r in range(rows):
        contrast = -(sa_ref[:, r : r + 1] * cx + ca_ref[:, r : r + 1] * sx)
        noise = nw_ref[r : r + 1, :]
        scale = contrast * noise
        for j in range(2):
            x = buf[j, pl.ds(r, count, stride=pitch), :]
            wt_ref[r, :, j * COLS : (j + 1) * COLS] = (scale * x).astype(BF16)
        sq_ref[r] = (contrast * contrast * noise).astype(BF16)


def weigh(images, defocus, noise_weight, row_freq, col_freq):
    count = images.shape[1]
    rows = images.shape[2]
    step = 64
    angle_r = defocus[:, None] * (row_freq * row_freq)[None, :] + math.asin(AMPLITUDE)
    angle_c = defocus[:, None] * (col_freq * col_freq)[None, :]
    return pl.pallas_call(
        weigh_kernel,
        grid=(count // step,),
        out_shape=[
            jax.ShapeDtypeStruct((rows, count, 2 * COLS), BF16),
            jax.ShapeDtypeStruct((rows, count, COLS), BF16),
        ],
        in_specs=[
            pl.BlockSpec((2, step, rows, COLS), lambda b: (0, b, 0, 0)),
            pl.BlockSpec((step, rows), lambda b: (b, 0)),
            pl.BlockSpec((step, rows), lambda b: (b, 0)),
            pl.BlockSpec((step, COLS), lambda b: (b, 0)),
            pl.BlockSpec((step, COLS), lambda b: (b, 0)),
            pl.BlockSpec((rows, COLS), lambda b: (0, 0)),
        ],
        out_specs=[
            pl.BlockSpec((rows, step, 2 * COLS), lambda b: (0, b, 0)),
            pl.BlockSpec((rows, step, COLS), lambda b: (0, b, 0)),
        ],
        scratch_shapes=[pltpu.VMEM((2, step * (rows + 1), COLS), F32)],
        compiler_params=params(1),
        cost_estimate=cost(12),
        name="weigh",
    )(
        images,
        jnp.sin(angle_r),
        jnp.cos(angle_r),
        jnp.sin(angle_c),
        jnp.cos(angle_c),
        noise_weight,
    )


def logits_kernel(wt_ref, sq_ref, cos_ref, sin_ref, cand_ref, *rest):
    sl_refs = rest[1:-4]
    out_ref, part, acc, quad = rest[-4:]
    step = pl.program_id(0)
    groups = len(sl_refs) // 2
    rows = part.shape[1] // K - 1
    share = K // groups
    pitch = rows + 1
    inner = wt_ref.shape[0]

    @pl.when(step == 0)
    def _():
        for m in range(groups):
            at = m * share
            for ref in sl_refs[2 * m : 2 * m + 2]:
                for j in range(2):
                    for k in range(ref.shape[1] // rows):
                        row = (at + k) * pitch
                        part[j, row : row + rows, :] = ref[j, k * rows : (k + 1) * rows].astype(F32)
                at += ref.shape[1] // rows
        acc[...] = jnp.zeros_like(acc)
        quad[...] = jnp.zeros_like(quad)

    dims = (((1,), (1,)), ((), ()))
    total = acc[...]
    total_q = quad[...]
    for u in range(inner):
        re = part[0, pl.ds(step * inner + u, K, stride=pitch), :]
        im = part[1, pl.ds(step * inner + u, K, stride=pitch), :]
        shifted = []
        for t in range(TRANS):
            c = cos_ref[t, u : u + 1, :]
            s = sin_ref[t, u : u + 1, :]
            shifted.append(
                jnp.concatenate(
                    [(c * re - s * im).astype(BF16), (s * re + c * im).astype(BF16)], axis=1
                )
            )
        left = jnp.concatenate(shifted, axis=0)
        power = (re * re + im * im).astype(BF16)
        total = total + lax.dot_general(left, wt_ref[u], dims, preferred_element_type=F32)
        total_q = total_q + lax.dot_general(power, sq_ref[u], dims, preferred_element_type=F32)
    acc[...] = total
    quad[...] = total_q

    @pl.when(step == pl.num_programs(0) - 1)
    def _():
        ids = lax.broadcasted_iota(jnp.int32, quad.shape, 0) ^ (lax.axis_index("img") * share)
        half = 0.5 * quad[...]
        for t in range(TRANS):
            value = acc[t * K : (t + 1) * K, :] - half
            for l in range(LMAX):
                pick = jnp.where(ids == cand_ref[l : l + 1, :], value, 0.0)
                out_ref[t * LMAX + l : t * LMAX + l + 1, :] = jnp.sum(pick, axis=0, keepdims=True)


def candidate_logits(after, slices, weighted, squared, cosine, sine, cand):
    rows, count = squared.shape[:2]
    inner = 8
    return pl.pallas_call(
        logits_kernel,
        grid=(rows // inner,),
        out_shape=jax.ShapeDtypeStruct((TRANS * LMAX, count), F32),
        in_specs=[
            pl.BlockSpec((inner, count, 2 * COLS), lambda s: (s, 0, 0)),
            pl.BlockSpec((inner, count, COLS), lambda s: (s, 0, 0)),
            pl.BlockSpec((TRANS, inner, COLS), lambda s: (0, s, 0)),
            pl.BlockSpec((TRANS, inner, COLS), lambda s: (0, s, 0)),
            pl.BlockSpec((LMAX, count), lambda s: (0, 0)),
        ]
        + [hbm()]
        + [pl.BlockSpec(x.shape, lambda s: (0, 0, 0)) for x in slices],
        out_specs=pl.BlockSpec((TRANS * LMAX, count), lambda s: (0, 0)),
        scratch_shapes=[
            pltpu.VMEM((2, K * (rows + 1), COLS), F32),
            pltpu.VMEM((TRANS * K, count), F32),
            pltpu.VMEM((K, count), F32),
        ],
        compiler_params=params(1),
        cost_estimate=cost(8),
        name="logits",
    )(weighted, squared, cosine, sine, cand, after, *slices)


def posterior_rows(logits, counts):
    place = lax.broadcasted_iota(jnp.int32, logits.shape, 0) % LMAX
    allowed = place < counts
    masked = jnp.where(allowed, logits, -1e30)
    highest = jnp.max(masked, axis=0, keepdims=True)
    exponent = jnp.where(allowed, jnp.exp(masked - highest), 0.0)
    return (exponent / jnp.sum(exponent, axis=0, keepdims=True)).astype(BF16).astype(F32)


def list_rows(num, src_s, len_s, outs, pick):
    parts = 2 * outs[0].shape[0]
    cap = outs[0].shape[2]
    comps = num.shape[0]
    lead = src_s.shape[0] // parts
    group = lax.axis_index("img")
    for m in range(parts):
        q = group ^ m

        def turn(g, carry, q=q, m=m):
            base = pl.multiple_of(g * 32, 32)
            at = q * lead + base
            for u in range(32):
                s = src_s[at + u]
                for c in range(comps):
                    pick[c, u : u + 1, :] = num[c, pl.ds(s, 1), :]
            for c in range(comps):
                outs[m % 2][m // 2, c, pl.ds(base, 32), :] = pick[c].astype(BF16)
            return carry

        lax.fori_loop(0, (jnp.minimum(len_s[q, 0], cap) + 31) // 32, turn, 0)


def project_kernel(src_s, len_s, cand_ref, cnt_ref, wt_ref, sq_ref, cos_ref, sin_ref, *rest):
    lg_refs = rest[:-6]
    keep_ref, send_ref, post, post_sum, num, pick = rest[-6:]
    step = pl.program_id(0)
    inner = wt_ref.shape[0]

    @pl.when(step == 0)
    def _():
        prob = posterior_rows(sum([ref[...] for ref in lg_refs[1:]], lg_refs[0][...]), cnt_ref[...])
        ids = lax.broadcasted_iota(jnp.int32, (K, prob.shape[1]), 0)
        total = jnp.zeros((K, prob.shape[1]), F32)
        for t in range(TRANS):
            dense = jnp.zeros((K, prob.shape[1]), F32)
            for l in range(LMAX):
                at = t * LMAX + l
                dense = jnp.where(ids == cand_ref[l : l + 1, :], dense + prob[at : at + 1, :], dense)
            post[t * K : (t + 1) * K, :] = dense.astype(BF16)
            total = total + dense
        high = total.astype(BF16)
        post_sum[:K, :] = high
        post_sum[K:, :] = (total - high.astype(F32)).astype(BF16)

    for u in range(inner):
        y = jnp.dot(post[...], wt_ref[u], preferred_element_type=F32)
        d = jnp.dot(post_sum[...], sq_ref[u], preferred_element_type=F32)
        re = jnp.zeros((K, COLS), F32)
        im = jnp.zeros((K, COLS), F32)
        for t in range(TRANS):
            c = cos_ref[t, u : u + 1, :]
            s = sin_ref[t, u : u + 1, :]
            y_re = y[t * K : (t + 1) * K, :COLS]
            y_im = y[t * K : (t + 1) * K, COLS:]
            re = re + (c * y_re + s * y_im)
            im = im + (c * y_im - s * y_re)
        base = pl.multiple_of((step * inner + u) * K, K)
        num[0, pl.ds(base, K), :] = re
        num[1, pl.ds(base, K), :] = im
        num[2, pl.ds(base, K), :] = d[:K] + d[K:]

    @pl.when(step == pl.num_programs(0) - 1)
    def _():
        list_rows(num, src_s, len_s, (keep_ref, send_ref), pick)


def project(src, lengths, n_img, logits, cand, counts, weighted, squared, cosine, sine, cap):
    rows, count = squared.shape[:2]
    inner = 8
    shape = (n_img // 2, 3, cap, COLS)
    return pl.pallas_call(
        project_kernel,
        grid=(rows // inner,),
        out_shape=[jax.ShapeDtypeStruct(shape, BF16)] * 2,
        in_specs=[
            smem(),
            smem(),
            pl.BlockSpec((LMAX, count), lambda s: (0, 0)),
            pl.BlockSpec((1, count), lambda s: (0, 0)),
            pl.BlockSpec((inner, count, 2 * COLS), lambda s: (s, 0, 0)),
            pl.BlockSpec((inner, count, COLS), lambda s: (s, 0, 0)),
            pl.BlockSpec((TRANS, inner, COLS), lambda s: (0, s, 0)),
            pl.BlockSpec((TRANS, inner, COLS), lambda s: (0, s, 0)),
        ]
        + [pl.BlockSpec((TRANS * LMAX, count), lambda s: (0, 0)) for _ in logits],
        out_specs=[pl.BlockSpec(shape, lambda s: (0, 0, 0, 0))] * 2,
        scratch_shapes=[
            pltpu.VMEM((TRANS * K, count), BF16),
            pltpu.VMEM((2 * K, count), BF16),
            pltpu.VMEM((3, rows * K, COLS), F32),
            pltpu.VMEM((3, 32, COLS), F32),
        ],
        compiler_params=params(1),
        cost_estimate=cost(12),
        name="project",
    )(src, lengths, cand, counts, weighted, squared, cosine, sine, *logits)


def to_member(keep, send, n_img):
    got = lax.ppermute(send, "img", flip(n_img, 1))
    half = keep.shape[2] // 2
    owns = []
    for h in range(2):
        cut = slice(h * half, (h + 1) * half)
        summed = [keep[m, :, cut] + got[m, :, cut] for m in range(n_img // 2)]
        moved = [lax.ppermute(summed[m], "img", flip(n_img, 2 * m)) for m in range(1, n_img // 2)]
        owns.append(sum(moved, summed[0]))
    return owns


HEAD = 8


def line_stride(lines_here):
    return lines_here + 2 * HEAD


def insert_kernel(count, len_s, code_hbm, wgt_hbm, reg_hbm, *rest):
    pieces = rest[:count]
    out_hbm = rest[count]
    code_s, wgt_s, held, reg, out, acc, acc_odd, buf, sem_in, sem_piece, sem_out = rest[count + 1 :]
    both_acc = (acc, acc_odd)
    cap = buf.shape[1]
    half = cap // 2
    blocks = len_s.shape[0]
    lead = code_s.shape[0] // blocks
    planes, lines_here = reg.shape[:2]
    stride = line_stride(lines_here)
    slab = lax.axis_index("vol")
    place = jnp.where(slab & 1, blocks - 1 - (slab >> 1), slab >> 1)
    tables = [
        pltpu.make_async_copy(code_hbm, code_s, sem_in.at[0]),
        pltpu.make_async_copy(wgt_hbm, wgt_s, sem_in.at[1]),
    ]
    prior = pltpu.make_async_copy(reg_hbm, reg, sem_in.at[2])
    loads = [
        pltpu.make_async_copy(pieces[i], held.at[i], sem_piece.at[i]) for i in range(count)
    ]
    for copy in tables + loads + [prior]:
        copy.start()
    acc[...] = jnp.zeros_like(acc)
    acc_odd[...] = jnp.zeros_like(acc_odd)
    first = lax.broadcasted_iota(jnp.int32, (2, COLS), 0) == 0
    for copy in tables:
        copy.wait()
    for m in range(count // 2):
        for h in range(2):
            loads[2 * m + h].wait()
            for c in range(3):
                buf[c, h * half : (h + 1) * half, :] = held[2 * m + h, c].astype(F32)
        from_place = place + ((m + 1) // 2) * (-1 if m % 2 else 1)
        from_place = from_place & (blocks - 1)
        block = jnp.where(
            from_place >= blocks // 2, 2 * (blocks - 1 - from_place) + 1, 2 * from_place
        )

        def group_step(g, carry, block=block):
            at = block * lead + g * 4
            for u in range(4):
                code = code_s[at + u]
                s = code & 1023
                to = code >> 10
                w = wgt_s[at + u]
                both = jnp.where(first, w, 1.0 - w)
                into = both_acc[u % 2]
                for c in range(3):
                    row = jnp.broadcast_to(buf[c, pl.ds(s, 1), :], (2, COLS))
                    into[c, pl.ds(to, 2), :] = into[c, pl.ds(to, 2), :] + both * row
            return carry

        lax.fori_loop(0, (jnp.minimum(len_s[block, 0], cap) + 3) // 4, group_step, 0)

    prior.wait()
    chunks = sem_out.shape[0]
    span = planes // chunks
    stores = []
    for i in range(chunks):

        def plane_step(p, carry):
            base = pl.multiple_of(p * stride + HEAD, 8)
            total = [
                acc[c, pl.ds(base, lines_here), :] + acc_odd[c, pl.ds(base, lines_here), :]
                for c in range(3)
            ]
            inverse = 1.0 / (total[2] + reg[p])
            out[0, p] = total[0] * inverse
            out[1, p] = total[1] * inverse
            return carry

        lax.fori_loop(i * span, (i + 1) * span, plane_step, 0)
        part = pl.ds(i * span, span)
        stores.append(pltpu.make_async_copy(out.at[:, part], out_hbm.at[:, part], sem_out.at[i]))
        stores[-1].start()
    for copy in stores:
        copy.wait()


def insert(lengths, code, weights, pieces, regularizer):
    half = pieces[0].shape[1]
    planes, lines_here = regularizer.shape[:2]
    count = len(pieces)
    chunks = 4
    acc = pltpu.VMEM((3, planes * line_stride(lines_here), COLS), F32)
    result = (2, planes, lines_here, COLS)
    return pl.pallas_call(
        partial(insert_kernel, count),
        out_shape=jax.ShapeDtypeStruct(result, F32),
        in_specs=[smem()] + [hbm()] * (3 + count),
        out_specs=hbm(),
        scratch_shapes=[
            pltpu.SMEM(code.shape, jnp.int32),
            pltpu.SMEM(weights.shape, F32),
            pltpu.VMEM((count, 3, half, COLS), BF16),
            pltpu.VMEM(regularizer.shape, F32),
            pltpu.VMEM(result, F32),
            acc,
            acc,
            pltpu.VMEM((3, 2 * half, COLS), F32),
            pltpu.SemaphoreType.DMA((3,)),
            pltpu.SemaphoreType.DMA((count,)),
            pltpu.SemaphoreType.DMA((chunks,)),
        ],
        compiler_params=pltpu.CompilerParams(vmem_limit_bytes=VMEM_LIMIT),
        cost_estimate=cost(9),
        name="insert",
    )(lengths, code, weights, regularizer, *pieces)


def running(x):
    lanes = lax.broadcasted_iota(jnp.int32, x.shape, 1)
    step = 1
    while step < x.shape[1]:
        x = x + jnp.where(lanes >= step, pltpu.roll(x, step, 1), 0)
        step *= 2
    return x


def split_index(x):
    return [(x >> 5).astype(F32), (x & 31).astype(F32)]


def split_weight(w):
    a = w.astype(BF16).astype(F32)
    b = (w - a).astype(BF16).astype(F32)
    return [a, b, w - a - b]


def compacted(member, rank, values, lead):
    high = jnp.where(member, rank >> 5, -1)
    low = rank & 31
    spot = lax.broadcasted_iota(jnp.int32, (4 * lead, rank.shape[1]), 0)
    shift = lead.bit_length() - 1
    left = ((spot & (lead - 1)) * 4 + (spot >> shift)) == high
    hot = lax.broadcasted_iota(jnp.int32, (32, rank.shape[1]), 0) == low
    right = jnp.concatenate([jnp.where(hot, v, 0.0).astype(BF16) for v in values], axis=0)
    out = lax.dot_general(
        left.astype(F32).astype(BF16), right, (((1,), (1,)), ((), ())), preferred_element_type=F32
    )
    return [
        jnp.concatenate(
            [out[h * lead : (h + 1) * lead, 32 * i : 32 * (i + 1)] for h in range(4)], axis=1
        )
        for i in range(len(values))
    ]


def lists_kernel(
    n_img, planes_here, lines_here, cap,
    plane_ref, line_ref, wgt_ref,
    src_ref, code_ref, w_ref, send_len, recv_len, longest, own,
):
    slab = lax.axis_index("vol")
    group = lax.axis_index("img")
    blocks, number = line_ref.shape
    lead = src_ref.shape[0] // n_img
    lines = line_ref[...]

    def in_part(x, part):
        return (x >= part * lines_here - 1) & (x < (part + 1) * lines_here)

    top = jnp.zeros((blocks, COLS), jnp.int32)
    for q in range(n_img):
        size = jnp.sum(in_part(lines, q).astype(F32), axis=1, keepdims=True).astype(jnp.int32)
        top = jnp.maximum(top, jnp.broadcast_to(size, (blocks, COLS)))
    longest[...] = jnp.broadcast_to(jnp.max(top.astype(F32)), (8, COLS)).astype(jnp.int32)

    own[...] = jnp.broadcast_to(line_ref[pl.ds(slab, 1), :], own.shape)
    sent = in_part(own[...], lax.broadcasted_iota(jnp.int32, own.shape, 0))
    total = running(sent.astype(jnp.int32))
    send_len[...] = jnp.broadcast_to(total[:, number - 1 :], send_len.shape)
    rank = total - sent.astype(jnp.int32)
    row_ids = split_index(lax.broadcasted_iota(jnp.int32, (1, number), 1))
    for q in range(n_img):
        out = compacted(sent[q : q + 1], rank[q : q + 1], row_ids, lead)
        src_ref[q * lead : (q + 1) * lead, :] = (32.0 * out[0] + out[1]).astype(jnp.int32)

    member = in_part(lines, group)
    place = running(member.astype(jnp.int32)) - member.astype(jnp.int32)
    place = jnp.minimum(place, cap - 1)
    local = plane_ref[...] - slab * planes_here
    here = member & (local >= 0) & (local < planes_here)
    total = running(here.astype(jnp.int32))
    recv_len[...] = jnp.broadcast_to(total[:, number - 1 :], recv_len.shape)
    rank = total - here.astype(jnp.int32)
    target = local * line_stride(lines_here) + lines - group * lines_here + HEAD
    target = jnp.where(here, target, 0)
    for v in range(blocks):
        row = slice(v, v + 1)
        values = split_index(place[row]) + split_index(target[row]) + split_weight(wgt_ref[row, :])
        out = compacted(here[row], rank[row], values, lead)
        at = slice(v * lead, (v + 1) * lead)
        code_ref[at, :] = (
            32768.0 * out[2] + 1024.0 * out[3] + 32.0 * out[0] + out[1]
        ).astype(jnp.int32)
        w_ref[at, :] = out[4] + out[5] + out[6]


def lists(row_plane, row_line, row_weight, n_vol, n_img, planes_here, lines_here, cap):
    lead = 8
    assert cap <= lead * COLS
    number = ROWS // n_vol * K

    def order(x):
        return x.T.reshape(n_vol, number)

    def table(blocks, dtype=jnp.int32):
        return jax.ShapeDtypeStruct((blocks * lead, COLS), dtype)

    return pl.pallas_call(
        partial(lists_kernel, n_img, planes_here, lines_here, cap),
        out_shape=[
            table(n_img),
            table(n_vol),
            table(n_vol, F32),
            jax.ShapeDtypeStruct((8, COLS), jnp.int32),
            jax.ShapeDtypeStruct((n_vol, COLS), jnp.int32),
            jax.ShapeDtypeStruct((8, COLS), jnp.int32),
        ],
        in_specs=[vmem()] * 3,
        out_specs=[vmem()] * 6,
        scratch_shapes=[pltpu.VMEM((8, number), jnp.int32)],
        compiler_params=pltpu.CompilerParams(vmem_limit_bytes=VMEM_LIMIT),
        cost_estimate=cost(6),
        name="lists",
    )(order(row_plane), order(row_line), order(row_weight))


def insert_into(carry, piece, planes_all, lines_all, weights_all, slab_id, planes_here):
    local_plane = planes_all - slab_id * planes_here
    in_slab = (local_plane >= 0) & (local_plane < planes_here)
    dump_row = planes_here * ROWS
    lower_index = jnp.where(in_slab, local_plane * ROWS + lines_all, dump_row).reshape(-1)
    upper_index = jnp.where(in_slab, lower_index.reshape(in_slab.shape) + 1, dump_row).reshape(-1)
    values = piece.reshape(-1, 3 * COLS)
    weight = weights_all.reshape(-1, 1)
    carry = carry.at[lower_index].add(weight * values)
    return carry.at[upper_index].add((1.0 - weight) * values)


def dense_path(
    logits, cand, counts, weighted, squared, cosine, sine,
    plane_share, line_share, weight_share, regularizer, slab_id,
):
    prob = posterior_rows(logits, counts).reshape(TRANS, LMAX, -1)
    hot = (cand[:, None, :] == jnp.arange(K)[None, :, None]).astype(F32)
    post = jnp.einsum("tlb,lkb->tkb", prob, hot).astype(BF16)
    y = jnp.einsum("tkb,rbz->tkrz", post, weighted, preferred_element_type=F32)
    d = jnp.einsum("tkb,rbc->krc", post, squared, preferred_element_type=F32)
    y_re = y[..., :COLS]
    y_im = y[..., COLS:]
    num_re = jnp.sum(cosine[:, None] * y_re + sine[:, None] * y_im, axis=0)
    num_im = jnp.sum(cosine[:, None] * y_im - sine[:, None] * y_re, axis=0)
    partial_value = lax.psum_scatter(
        jnp.stack([num_re, num_im, d], axis=2), "img", scatter_dimension=0, tiled=True
    )
    planes_here = regularizer.shape[0]
    inserted = insert_into(
        jnp.zeros((planes_here * ROWS + 1, 3 * COLS), F32),
        lax.all_gather(partial_value, "vol", axis=1, tiled=True),
        plane_share,
        line_share,
        weight_share,
        slab_id,
        planes_here,
    )
    slab = inserted[: planes_here * ROWS].reshape(planes_here, ROWS, 3, COLS)
    summed = lax.psum_scatter(slab, "img", scatter_dimension=1, tiled=True)
    denom = summed[:, :, 2] + regularizer
    return jnp.stack([summed[:, :, 0] / denom, summed[:, :, 1] / denom], axis=0)


def body(
    images, defocus, candidates, counts, noise_weight, volume,
    row_plane, row_line, row_weight, regularizer,
):
    rows = noise_weight.shape[0]
    planes_here = volume.shape[1]
    lines_here = regularizer.shape[1]
    slab_id = lax.axis_index("vol")
    group_id = lax.axis_index("img")
    n_vol = lax.axis_size("vol")
    n_img = lax.axis_size("img")
    global_rows = slab_id * rows + jnp.arange(rows)
    row_freq = (global_rows.astype(F32) - ROWS // 2) / ROWS
    col_freq = jnp.arange(COLS).astype(F32) / (2 * COLS)
    share = K // n_img
    first = group_id * share
    plane_share = lax.dynamic_slice_in_dim(row_plane, first, share, 0)
    line_share = lax.dynamic_slice_in_dim(row_line, first, share, 0)
    weight_share = lax.dynamic_slice_in_dim(row_weight, first, share, 0)

    aligned = max(1, 16 // rows)
    share_a = share * 11 // 16 // aligned * aligned
    messages = extract(volume, row_plane, row_line, row_weight, n_vol, share, share_a)
    cosine, sine = shift_phases(row_freq, col_freq, TRANS)
    weighted, squared = weigh(images, defocus, noise_weight, row_freq, col_freq)
    mean = rows * K // n_img
    cap = -(-int(mean + 4.2 * math.sqrt(mean)) // 32) * 32
    src, code, wgt, send_len, recv_len, longest = lists(
        row_plane, row_line, row_weight, n_vol, n_img, planes_here, lines_here, cap
    )
    own_a, own_b = to_pixel_rows(messages, n_vol, weighted)
    slices_b = from_partners(own_b, n_img)
    slices_a = from_partners(own_a, n_img)
    slices = [x for both in zip(slices_a, slices_b) for x in both]
    cand = candidates.T
    count_row = counts[None, :]
    partial_logits = candidate_logits(code, slices, weighted, squared, cosine, sine, cand)
    pair_logits = partial_logits + lax.ppermute(partial_logits, "vol", flip(n_vol, 1))
    logits = [pair_logits] + [
        lax.ppermute(pair_logits, "vol", along_z(n_vol, d)) for d in range(1, n_vol // 2)
    ]

    keep, send = project(
        src.reshape(-1), send_len, n_img, logits, cand, count_row, weighted, squared, cosine, sine, cap
    )
    low, high = to_member(keep, send, n_img)
    pieces = ring_gather(low, high, n_vol)

    def listed():
        return insert(recv_len, code.reshape(-1), wgt.reshape(-1), pieces, regularizer)

    def dense():
        return dense_path(
            sum(logits[1:], logits[0]), cand, count_row, weighted, squared, cosine, sine,
            plane_share, line_share, weight_share, regularizer, slab_id,
        )

    return lax.cond(longest[0, 0] <= cap, listed, dense)


def solution(mesh):
    return jax.shard_map(
        body,
        mesh=mesh,
        in_specs=(
            P(None, "img", "vol", None),
            P("img"),
            P("img", None),
            P("img"),
            P("vol", None),
            P(None, "vol", None, None),
            P(),
            P(),
            P(),
            P("vol", "img", None),
        ),
        out_specs=P(None, "vol", "img", None),
        check_vma=False,
    )
```

```python
import math
from functools import partial

import jax
import jax.numpy as jnp
from jax import lax
from jax.experimental import pallas as pl
from jax.experimental.pallas import tpu as pltpu
from jax.sharding import PartitionSpec as P

ROWS = 256
COLS = 128
K = 64
TRANS = 4
LMAX = 8
AMPLITUDE = 0.1
VMEM_LIMIT = 56 * 1024 * 1024
BF16 = jnp.bfloat16
F32 = jnp.float32


def params(steps):
    return pltpu.CompilerParams(
        dimension_semantics=("arbitrary",) * steps, vmem_limit_bytes=VMEM_LIMIT
    )


def smem():
    return pl.BlockSpec(memory_space=pltpu.SMEM)


def vmem():
    return pl.BlockSpec(memory_space=pltpu.VMEM)


def cost(us):
    return pl.CostEstimate(flops=0, transcendentals=0, bytes_accessed=int(us * 3.69e6))


def hbm():
    return pl.BlockSpec(memory_space=pl.ANY)


def shift_phases(row_freq, col_freq, number):
    shift_ids = jnp.arange(number)
    shift_x = (shift_ids % 2).astype(F32) - 0.5
    shift_y = (shift_ids // 2).astype(F32) - 0.5
    angle = (
        -2.0
        * math.pi
        * (
            shift_x[:, None, None] * col_freq[None, None, :]
            + shift_y[:, None, None] * row_freq[None, :, None]
        )
    )
    return (jnp.cos(angle), jnp.sin(angle))


def along_z(n_vol, shift):
    count = n_vol // 2
    return [(v, (v // 2 + shift) % count * 2 + v % 2) for v in range(n_vol)]


def flip(number, mask):
    return [(v, v ^ mask) for v in range(number)]


def ring_of(n_vol):
    return list(range(0, n_vol, 2)) + list(range(n_vol - 1, 0, -2))


def extract_kernel(rows, planes_here, *refs):
    plane_ref, line_ref, weight_hbm, vol_hbm, keep_a, send_a = refs[:6]
    vol, pair, idx_v, flag_v, idx_s, flag_s, w_s, sem = refs[-8:]
    parts_b = refs[6:-8]
    slab = lax.axis_index("vol")
    share = idx_v.shape[0] // 2
    first = lax.axis_index("img") * share
    height = planes_here * ROWS
    count_z = keep_a.shape[0]
    groups_a = keep_a.shape[2] // 16
    groups_b = parts_b[0].shape[2] // 16
    load = pltpu.make_async_copy(vol_hbm, vol.at[:, :height, :], sem.at[0])
    load.start()
    loads_w = [
        pltpu.make_async_copy(
            weight_hbm.at[pl.ds(first, share), pl.ds(h * COLS, COLS)],
            w_s.at[pl.ds(h * share, share), :],
            sem.at[4 + h],
        )
        for h in range(2)
    ]
    for copy in loads_w:
        copy.start()
    local = plane_ref[pl.ds(first, share), :] - slab * planes_here
    owned = (local >= 0) & (local < planes_here)
    idx = jnp.where(owned, local * ROWS + line_ref[pl.ds(first, share), :], height)
    for h in range(2):
        idx_v[h * share : (h + 1) * share, :] = idx[:, h * COLS : (h + 1) * COLS]
    eights = (
        lax.broadcasted_iota(jnp.int32, (ROWS, COLS), 0) >> 3
        == lax.broadcasted_iota(jnp.int32, (ROWS, COLS), 1)
    )
    held = jnp.dot(
        owned.astype(F32).astype(BF16), eights.astype(F32).astype(BF16), preferred_element_type=F32
    )
    eight = lax.broadcasted_iota(jnp.int32, (COLS, COLS), 0)
    bits = jnp.where(
        eight >> 4 == lax.broadcasted_iota(jnp.int32, (COLS, COLS), 1), 1 << (eight & 15), 0
    )
    flag_v[...] = jnp.dot(
        (held > 0.0).astype(F32).astype(BF16),
        bits.astype(F32).astype(BF16),
        preferred_element_type=F32,
    ).astype(jnp.int32)
    to_idx = pltpu.make_async_copy(idx_v, idx_s, sem.at[2])
    to_flag = pltpu.make_async_copy(flag_v, flag_s, sem.at[3])
    to_idx.start()
    to_flag.start()
    vol[:, height : height + 8, :] = jnp.zeros((2, 8, COLS), F32)
    for ref in (keep_a, send_a) + parts_b:
        ref[...] = jnp.zeros_like(ref)
    to_idx.wait()
    to_flag.wait()
    for copy in loads_w:
        copy.wait()
    load.wait()
    lower_row = lax.broadcasted_iota(jnp.int32, (2, COLS), 0) == 0
    per_k = max(1, 16 // rows)
    per_block = max(1, rows // 16)
    run = min(rows, 16)

    def message(out, lead, k, words, r0, base):
        word = jnp.where(r0 >= COLS, words[1], words[0])
        lane = r0 & (COLS - 1)
        hits = (word >> (lane >> 3)) & ((1 << (run // 8)) - 1)

        @pl.when(hits > 0)
        def _():
            line = k + share * (r0 >> 7)
            for u in range(16):
                i = idx_s[line + u // run, lane + u % run]
                w = w_s[line + u // run, lane + u % run]
                both = jnp.where(lower_row, w, 1.0 - w)
                for j in range(2):
                    pair[j, 2 * u : 2 * u + 2, :] = both * vol[j, pl.ds(i, 2), :]
            for j in range(2):
                value = pair[j, pl.ds(0, 16, stride=2), :] + pair[j, pl.ds(1, 16, stride=2), :]
                out[lead, j, pl.ds(base, 16), :] = value.astype(BF16)

    places = []
    for dz in range(count_z):
        for dy in range(2):
            z = (slab >> 1) + dz
            block = jnp.where(z >= count_z, z - count_z, z) * 2 + ((slab + dy) & 1)
            places.append((dz, dy, block))
    share_a = keep_a.shape[2] // rows
    for k0, count in ((0, share_a), (share_a, share - share_a)):

        def turn(t, carry, k0=k0):
            k = k0 + t * per_k
            words = [flag_s[k, 0], flag_s[k, 1]]
            for i in range(1, per_k):
                words = [words[0] | flag_s[k + i, 0], words[1] | flag_s[k + i, 1]]
            for dz, dy, block in places:
                out, lead = ((keep_a, send_a)[dy], dz) if k0 == 0 else (parts_b[dz], dy)
                for g in range(per_block):
                    base = pl.multiple_of((t * per_block + g) * 16, 16)
                    message(out, lead, k, words, block * rows + 16 * g, base)
            return carry

        lax.fori_loop(0, count // per_k, turn, 0)


def extract(volume, row_plane, row_line, row_weight, n_vol, share, share_a):
    planes_here = volume.shape[1]
    rows = ROWS // n_vol
    count_z = n_vol // 2
    shape_a = jax.ShapeDtypeStruct((count_z, 2, share_a * rows, COLS), BF16)
    shape_b = jax.ShapeDtypeStruct((2, 2, (share - share_a) * rows, COLS), BF16)
    return pl.pallas_call(
        partial(extract_kernel, rows, planes_here),
        out_shape=[shape_a, shape_a] + [shape_b] * count_z,
        in_specs=[vmem(), vmem(), hbm(), hbm()],
        out_specs=[vmem()] * (2 + count_z),
        scratch_shapes=[
            pltpu.VMEM((2, planes_here * ROWS + 8, COLS), F32),
            pltpu.VMEM((2, 32, COLS), F32),
            pltpu.VMEM((2 * share, COLS), jnp.int32),
            pltpu.VMEM((share, COLS), jnp.int32),
            pltpu.SMEM((2 * share, COLS), jnp.int32),
            pltpu.SMEM((share, COLS), jnp.int32),
            pltpu.SMEM((2 * share, COLS), F32),
            pltpu.SemaphoreType.DMA((6,)),
        ],
        compiler_params=pltpu.CompilerParams(vmem_limit_bytes=VMEM_LIMIT),
        cost_estimate=cost(11),
        name="extract",
    )(row_plane, row_line, row_weight, volume.reshape(2, planes_here * ROWS, COLS))


def combine_first_kernel(keep_a, got_a, keep_b, *rest):
    count_z = keep_a.shape[0]
    got_b = rest[: count_z - 1]
    out_a = rest[count_z : 2 * count_z]
    out_b = rest[2 * count_z :]
    for d in range(count_z):
        out_a[d][...] = keep_a[d] + got_a[d]
    for d in range(2):
        total = keep_b[d]
        for ref in got_b:
            total = total + ref[d]
        out_b[d][...] = total


def to_pixel_rows(messages, n_vol, first_with):
    keep_a, send_a, keep_b = messages[:3]
    count_z = n_vol // 2
    got_b = [lax.ppermute(m, "vol", along_z(n_vol, d + 1)) for d, m in enumerate(messages[3:])]
    got_a = lax.ppermute(send_a, "vol", flip(n_vol, 1))
    shape_a = jax.ShapeDtypeStruct(keep_a.shape[1:], BF16)
    shape_b = jax.ShapeDtypeStruct(keep_b.shape[1:], BF16)
    sums = pl.pallas_call(
        combine_first_kernel,
        out_shape=[shape_a] * count_z + [shape_b] * 2,
        in_specs=[vmem()] * (2 + count_z) + [hbm()],
        out_specs=[vmem()] * (count_z + 2),
        compiler_params=pltpu.CompilerParams(vmem_limit_bytes=VMEM_LIMIT),
        cost_estimate=cost(3),
        name="combine_first",
    )(keep_a, got_a, keep_b, *got_b, first_with)
    sums_a, sums_b = sums[:count_z], sums[count_z:]
    moved_b = lax.ppermute(sums_b[1], "vol", flip(n_vol, 1))
    moved = [lax.ppermute(sums_a[d], "vol", along_z(n_vol, d)) for d in range(1, count_z)]
    out_b = sums_b[0] + moved_b
    out_a = sum(moved, sums_a[0])
    return out_a, out_b


def from_partners(x, n_img):
    return [x] + [lax.ppermute(x, "img", flip(n_img, m)) for m in range(1, n_img)]


def ring_gather(low, high, n_vol):
    ring = ring_of(n_vol)
    ahead = [(ring[p], ring[(p + 1) % n_vol]) for p in range(n_vol)]
    back = [(b, a) for a, b in ahead]
    pieces = [low, high]
    one = two = (low, high)
    for _ in range(1, n_vol // 2):
        one_low, two_low = lax.ppermute(one[0], "vol", ahead), lax.ppermute(two[0], "vol", back)
        one_high, two_high = lax.ppermute(one[1], "vol", ahead), lax.ppermute(two[1], "vol", back)
        one, two = (one_low, one_high), (two_low, two_high)
        pieces += [*one, *two]
    return pieces + [lax.ppermute(one[0], "vol", ahead), lax.ppermute(two[1], "vol", back)]


def weigh_kernel(img_ref, sa_ref, ca_ref, sx_ref, cx_ref, nw_ref, wt_ref, sq_ref, buf):
    count = img_ref.shape[1]
    rows = img_ref.shape[2]
    pitch = rows + 1
    for j in range(2):
        for b in range(count):
            buf[j, b * pitch : b * pitch + rows, :] = img_ref[j, b].astype(F32)
    sx = sx_ref[...]
    cx = cx_ref[...]
    for r in range(rows):
        contrast = -(sa_ref[:, r : r + 1] * cx + ca_ref[:, r : r + 1] * sx)
        noise = nw_ref[r : r + 1, :]
        scale = contrast * noise
        for j in range(2):
            x = buf[j, pl.ds(r, count, stride=pitch), :]
            wt_ref[r, :, j * COLS : (j + 1) * COLS] = (scale * x).astype(BF16)
        sq_ref[r] = (contrast * contrast * noise).astype(BF16)


def weigh(images, defocus, noise_weight, row_freq, col_freq):
    count = images.shape[1]
    rows = images.shape[2]
    step = 64
    angle_r = defocus[:, None] * (row_freq * row_freq)[None, :] + math.asin(AMPLITUDE)
    angle_c = defocus[:, None] * (col_freq * col_freq)[None, :]
    return pl.pallas_call(
        weigh_kernel,
        grid=(count // step,),
        out_shape=[
            jax.ShapeDtypeStruct((rows, count, 2 * COLS), BF16),
            jax.ShapeDtypeStruct((rows, count, COLS), BF16),
        ],
        in_specs=[
            pl.BlockSpec((2, step, rows, COLS), lambda b: (0, b, 0, 0)),
            pl.BlockSpec((step, rows), lambda b: (b, 0)),
            pl.BlockSpec((step, rows), lambda b: (b, 0)),
            pl.BlockSpec((step, COLS), lambda b: (b, 0)),
            pl.BlockSpec((step, COLS), lambda b: (b, 0)),
            pl.BlockSpec((rows, COLS), lambda b: (0, 0)),
        ],
        out_specs=[
            pl.BlockSpec((rows, step, 2 * COLS), lambda b: (0, b, 0)),
            pl.BlockSpec((rows, step, COLS), lambda b: (0, b, 0)),
        ],
        scratch_shapes=[pltpu.VMEM((2, step * (rows + 1), COLS), F32)],
        compiler_params=params(1),
        cost_estimate=cost(12),
        name="weigh",
    )(
        images,
        jnp.sin(angle_r),
        jnp.cos(angle_r),
        jnp.sin(angle_c),
        jnp.cos(angle_c),
        noise_weight,
    )


def logits_kernel(wt_ref, sq_ref, cos_ref, sin_ref, cand_ref, *rest):
    sl_refs = rest[1:-4]
    out_ref, part, acc, quad = rest[-4:]
    step = pl.program_id(0)
    groups = len(sl_refs) // 2
    rows = part.shape[1] // K - 1
    share = K // groups
    pitch = rows + 1
    inner = wt_ref.shape[0]

    @pl.when(step == 0)
    def _():
        for m in range(groups):
            at = m * share
            for ref in sl_refs[2 * m : 2 * m + 2]:
                for j in range(2):
                    for k in range(ref.shape[1] // rows):
                        row = (at + k) * pitch
                        part[j, row : row + rows, :] = ref[j, k * rows : (k + 1) * rows].astype(F32)
                at += ref.shape[1] // rows
        acc[...] = jnp.zeros_like(acc)
        quad[...] = jnp.zeros_like(quad)

    dims = (((1,), (1,)), ((), ()))
    total = acc[...]
    total_q = quad[...]
    for u in range(inner):
        re = part[0, pl.ds(step * inner + u, K, stride=pitch), :]
        im = part[1, pl.ds(step * inner + u, K, stride=pitch), :]
        shifted = []
        for t in range(TRANS):
            c = cos_ref[t, u : u + 1, :]
            s = sin_ref[t, u : u + 1, :]
            shifted.append(
                jnp.concatenate(
                    [(c * re - s * im).astype(BF16), (s * re + c * im).astype(BF16)], axis=1
                )
            )
        left = jnp.concatenate(shifted, axis=0)
        power = (re * re + im * im).astype(BF16)
        total = total + lax.dot_general(left, wt_ref[u], dims, preferred_element_type=F32)
        total_q = total_q + lax.dot_general(power, sq_ref[u], dims, preferred_element_type=F32)
    acc[...] = total
    quad[...] = total_q

    @pl.when(step == pl.num_programs(0) - 1)
    def _():
        ids = lax.broadcasted_iota(jnp.int32, quad.shape, 0) ^ (lax.axis_index("img") * share)
        half = 0.5 * quad[...]
        for t in range(TRANS):
            value = acc[t * K : (t + 1) * K, :] - half
            for l in range(LMAX):
                pick = jnp.where(ids == cand_ref[l : l + 1, :], value, 0.0)
                out_ref[t * LMAX + l : t * LMAX + l + 1, :] = jnp.sum(pick, axis=0, keepdims=True)


def candidate_logits(after, slices, weighted, squared, cosine, sine, cand):
    rows, count = squared.shape[:2]
    inner = 8
    return pl.pallas_call(
        logits_kernel,
        grid=(rows // inner,),
        out_shape=jax.ShapeDtypeStruct((TRANS * LMAX, count), F32),
        in_specs=[
            pl.BlockSpec((inner, count, 2 * COLS), lambda s: (s, 0, 0)),
            pl.BlockSpec((inner, count, COLS), lambda s: (s, 0, 0)),
            pl.BlockSpec((TRANS, inner, COLS), lambda s: (0, s, 0)),
            pl.BlockSpec((TRANS, inner, COLS), lambda s: (0, s, 0)),
            pl.BlockSpec((LMAX, count), lambda s: (0, 0)),
        ]
        + [hbm()]
        + [pl.BlockSpec(x.shape, lambda s: (0, 0, 0)) for x in slices],
        out_specs=pl.BlockSpec((TRANS * LMAX, count), lambda s: (0, 0)),
        scratch_shapes=[
            pltpu.VMEM((2, K * (rows + 1), COLS), F32),
            pltpu.VMEM((TRANS * K, count), F32),
            pltpu.VMEM((K, count), F32),
        ],
        compiler_params=params(1),
        cost_estimate=cost(8),
        name="logits",
    )(weighted, squared, cosine, sine, cand, after, *slices)


def posterior_rows(logits, counts):
    place = lax.broadcasted_iota(jnp.int32, logits.shape, 0) % LMAX
    allowed = place < counts
    masked = jnp.where(allowed, logits, -1e30)
    highest = jnp.max(masked, axis=0, keepdims=True)
    exponent = jnp.where(allowed, jnp.exp(masked - highest), 0.0)
    return (exponent / jnp.sum(exponent, axis=0, keepdims=True)).astype(BF16).astype(F32)


def list_rows(num, src_s, len_s, outs, pick):
    parts = 2 * outs[0].shape[0]
    cap = outs[0].shape[2]
    comps = num.shape[0]
    lead = src_s.shape[0] // parts
    group = lax.axis_index("img")
    for m in range(parts):
        q = group ^ m

        def turn(g, carry, q=q, m=m):
            base = pl.multiple_of(g * 32, 32)
            at = q * lead + base
            for u in range(32):
                s = src_s[at + u]
                for c in range(comps):
                    pick[c, u : u + 1, :] = num[c, pl.ds(s, 1), :]
            for c in range(comps):
                outs[m % 2][m // 2, c, pl.ds(base, 32), :] = pick[c].astype(BF16)
            return carry

        lax.fori_loop(0, (jnp.minimum(len_s[q, 0], cap) + 31) // 32, turn, 0)


def project_kernel(src_s, len_s, cand_ref, cnt_ref, wt_ref, sq_ref, cos_ref, sin_ref, *rest):
    lg_refs = rest[:-6]
    keep_ref, send_ref, post, post_sum, num, pick = rest[-6:]
    step = pl.program_id(0)
    inner = wt_ref.shape[0]

    @pl.when(step == 0)
    def _():
        prob = posterior_rows(sum([ref[...] for ref in lg_refs[1:]], lg_refs[0][...]), cnt_ref[...])
        ids = lax.broadcasted_iota(jnp.int32, (K, prob.shape[1]), 0)
        total = jnp.zeros((K, prob.shape[1]), F32)
        for t in range(TRANS):
            dense = jnp.zeros((K, prob.shape[1]), F32)
            for l in range(LMAX):
                at = t * LMAX + l
                dense = jnp.where(ids == cand_ref[l : l + 1, :], dense + prob[at : at + 1, :], dense)
            post[t * K : (t + 1) * K, :] = dense.astype(BF16)
            total = total + dense
        high = total.astype(BF16)
        post_sum[:K, :] = high
        post_sum[K:, :] = (total - high.astype(F32)).astype(BF16)

    for u in range(inner):
        y = jnp.dot(post[...], wt_ref[u], preferred_element_type=F32)
        d = jnp.dot(post_sum[...], sq_ref[u], preferred_element_type=F32)
        re = jnp.zeros((K, COLS), F32)
        im = jnp.zeros((K, COLS), F32)
        for t in range(TRANS):
            c = cos_ref[t, u : u + 1, :]
            s = sin_ref[t, u : u + 1, :]
            y_re = y[t * K : (t + 1) * K, :COLS]
            y_im = y[t * K : (t + 1) * K, COLS:]
            re = re + (c * y_re + s * y_im)
            im = im + (c * y_im - s * y_re)
        base = pl.multiple_of((step * inner + u) * K, K)
        num[0, pl.ds(base, K), :] = re
        num[1, pl.ds(base, K), :] = im
        num[2, pl.ds(base, K), :] = d[:K] + d[K:]

    @pl.when(step == pl.num_programs(0) - 1)
    def _():
        list_rows(num, src_s, len_s, (keep_ref, send_ref), pick)


def project(src, lengths, n_img, logits, cand, counts, weighted, squared, cosine, sine, cap):
    rows, count = squared.shape[:2]
    inner = 8
    shape = (n_img // 2, 3, cap, COLS)
    return pl.pallas_call(
        project_kernel,
        grid=(rows // inner,),
        out_shape=[jax.ShapeDtypeStruct(shape, BF16)] * 2,
        in_specs=[
            smem(),
            smem(),
            pl.BlockSpec((LMAX, count), lambda s: (0, 0)),
            pl.BlockSpec((1, count), lambda s: (0, 0)),
            pl.BlockSpec((inner, count, 2 * COLS), lambda s: (s, 0, 0)),
            pl.BlockSpec((inner, count, COLS), lambda s: (s, 0, 0)),
            pl.BlockSpec((TRANS, inner, COLS), lambda s: (0, s, 0)),
            pl.BlockSpec((TRANS, inner, COLS), lambda s: (0, s, 0)),
        ]
        + [pl.BlockSpec((TRANS * LMAX, count), lambda s: (0, 0)) for _ in logits],
        out_specs=[pl.BlockSpec(shape, lambda s: (0, 0, 0, 0))] * 2,
        scratch_shapes=[
            pltpu.VMEM((TRANS * K, count), BF16),
            pltpu.VMEM((2 * K, count), BF16),
            pltpu.VMEM((3, rows * K, COLS), F32),
            pltpu.VMEM((3, 32, COLS), F32),
        ],
        compiler_params=params(1),
        cost_estimate=cost(12),
        name="project",
    )(src, lengths, cand, counts, weighted, squared, cosine, sine, *logits)


def to_member(keep, send, n_img):
    got = lax.ppermute(send, "img", flip(n_img, 1))
    half = keep.shape[2] // 2
    owns = []
    for h in range(2):
        cut = slice(h * half, (h + 1) * half)
        summed = [keep[m, :, cut] + got[m, :, cut] for m in range(n_img // 2)]
        moved = [lax.ppermute(summed[m], "img", flip(n_img, 2 * m)) for m in range(1, n_img // 2)]
        owns.append(added(summed[0], *moved))
    return owns


def added_kernel(*refs):
    total = refs[0][...]
    for ref in refs[1:-1]:
        total = total + ref[...]
    refs[-1][...] = total


def added(*terms):
    return pl.pallas_call(
        added_kernel,
        out_shape=jax.ShapeDtypeStruct(terms[0].shape, terms[0].dtype),
        in_specs=[vmem()] * len(terms),
        out_specs=vmem(),
        compiler_params=pltpu.CompilerParams(vmem_limit_bytes=VMEM_LIMIT),
        cost_estimate=cost(1),
        name="added",
    )(*terms)


HEAD = 8


def line_stride(lines_here):
    return lines_here + 2 * HEAD


def insert_kernel(count, len_s, code_hbm, wgt_hbm, reg_hbm, *rest):
    pieces = rest[:count]
    out_hbm = rest[count]
    code_s, wgt_s, held, reg, out, acc, acc_odd, buf, sem_in, sem_piece, sem_out = rest[count + 1 :]
    both_acc = (acc, acc_odd)
    cap = buf.shape[1]
    half = cap // 2
    blocks = len_s.shape[0]
    lead = code_s.shape[0] // blocks
    planes, lines_here = reg.shape[:2]
    stride = line_stride(lines_here)
    slab = lax.axis_index("vol")
    place = jnp.where(slab & 1, blocks - 1 - (slab >> 1), slab >> 1)
    tables = [
        pltpu.make_async_copy(code_hbm, code_s, sem_in.at[0]),
        pltpu.make_async_copy(wgt_hbm, wgt_s, sem_in.at[1]),
    ]
    prior = pltpu.make_async_copy(reg_hbm, reg, sem_in.at[2])
    loads = [
        pltpu.make_async_copy(pieces[i], held.at[i], sem_piece.at[i]) for i in range(count)
    ]
    for copy in tables + loads + [prior]:
        copy.start()
    acc[...] = jnp.zeros_like(acc)
    acc_odd[...] = jnp.zeros_like(acc_odd)
    first = lax.broadcasted_iota(jnp.int32, (2, COLS), 0) == 0
    for copy in tables:
        copy.wait()
    for m in range(count // 2):
        for h in range(2):
            loads[2 * m + h].wait()
            for c in range(3):
                buf[c, h * half : (h + 1) * half, :] = held[2 * m + h, c].astype(F32)
        from_place = place + ((m + 1) // 2) * (-1 if m % 2 else 1)
        from_place = from_place & (blocks - 1)
        block = jnp.where(
            from_place >= blocks // 2, 2 * (blocks - 1 - from_place) + 1, 2 * from_place
        )

        def group_step(g, carry, block=block):
            at = block * lead + g * 4
            for u in range(4):
                code = code_s[at + u]
                s = code & 1023
                to = code >> 10
                w = wgt_s[at + u]
                both = jnp.where(first, w, 1.0 - w)
                into = both_acc[u % 2]
                for c in range(3):
                    row = jnp.broadcast_to(buf[c, pl.ds(s, 1), :], (2, COLS))
                    into[c, pl.ds(to, 2), :] = into[c, pl.ds(to, 2), :] + both * row
            return carry

        lax.fori_loop(0, (jnp.minimum(len_s[block, 0], cap) + 3) // 4, group_step, 0)

    prior.wait()
    chunks = sem_out.shape[0]
    span = planes // chunks
    stores = []
    for i in range(chunks):

        def plane_step(p, carry):
            base = pl.multiple_of(p * stride + HEAD, 8)
            total = [
                acc[c, pl.ds(base, lines_here), :] + acc_odd[c, pl.ds(base, lines_here), :]
                for c in range(3)
            ]
            inverse = 1.0 / (total[2] + reg[p])
            out[0, p] = total[0] * inverse
            out[1, p] = total[1] * inverse
            return carry

        lax.fori_loop(i * span, (i + 1) * span, plane_step, 0)
        part = pl.ds(i * span, span)
        stores.append(pltpu.make_async_copy(out.at[:, part], out_hbm.at[:, part], sem_out.at[i]))
        stores[-1].start()
    for copy in stores:
        copy.wait()


def insert(lengths, code, weights, pieces, regularizer):
    half = pieces[0].shape[1]
    planes, lines_here = regularizer.shape[:2]
    count = len(pieces)
    chunks = 4
    acc = pltpu.VMEM((3, planes * line_stride(lines_here), COLS), F32)
    result = (2, planes, lines_here, COLS)
    return pl.pallas_call(
        partial(insert_kernel, count),
        out_shape=jax.ShapeDtypeStruct(result, F32),
        in_specs=[smem()] + [hbm()] * (3 + count),
        out_specs=hbm(),
        scratch_shapes=[
            pltpu.SMEM(code.shape, jnp.int32),
            pltpu.SMEM(weights.shape, F32),
            pltpu.VMEM((count, 3, half, COLS), BF16),
            pltpu.VMEM(regularizer.shape, F32),
            pltpu.VMEM(result, F32),
            acc,
            acc,
            pltpu.VMEM((3, 2 * half, COLS), F32),
            pltpu.SemaphoreType.DMA((3,)),
            pltpu.SemaphoreType.DMA((count,)),
            pltpu.SemaphoreType.DMA((chunks,)),
        ],
        compiler_params=pltpu.CompilerParams(vmem_limit_bytes=VMEM_LIMIT),
        cost_estimate=cost(9),
        name="insert",
    )(lengths, code, weights, regularizer, *pieces)


def running(x):
    lanes = lax.broadcasted_iota(jnp.int32, x.shape, 1)
    step = 1
    while step < x.shape[1]:
        x = x + jnp.where(lanes >= step, pltpu.roll(x, step, 1), 0)
        step *= 2
    return x


def split_index(x):
    return [(x >> 5).astype(F32), (x & 31).astype(F32)]


def split_weight(w):
    a = w.astype(BF16).astype(F32)
    b = (w - a).astype(BF16).astype(F32)
    return [a, b, w - a - b]


def compacted(member, rank, values, lead):
    high = jnp.where(member, rank >> 5, -1)
    low = rank & 31
    spot = lax.broadcasted_iota(jnp.int32, (4 * lead, rank.shape[1]), 0)
    shift = lead.bit_length() - 1
    left = ((spot & (lead - 1)) * 4 + (spot >> shift)) == high
    hot = lax.broadcasted_iota(jnp.int32, (32, rank.shape[1]), 0) == low
    right = jnp.concatenate([jnp.where(hot, v, 0.0).astype(BF16) for v in values], axis=0)
    out = lax.dot_general(
        left.astype(F32).astype(BF16), right, (((1,), (1,)), ((), ())), preferred_element_type=F32
    )
    return [
        jnp.concatenate(
            [out[h * lead : (h + 1) * lead, 32 * i : 32 * (i + 1)] for h in range(4)], axis=1
        )
        for i in range(len(values))
    ]


def lists_kernel(
    n_img, planes_here, lines_here, cap,
    plane_ref, line_ref, wgt_ref,
    src_ref, code_ref, w_ref, send_len, recv_len, longest, own,
):
    slab = lax.axis_index("vol")
    group = lax.axis_index("img")
    blocks, number = line_ref.shape
    lead = src_ref.shape[0] // n_img
    lines = line_ref[...]

    def in_part(x, part):
        return (x >= part * lines_here - 1) & (x < (part + 1) * lines_here)

    top = jnp.zeros((blocks, COLS), jnp.int32)
    for q in range(n_img):
        size = jnp.sum(in_part(lines, q).astype(F32), axis=1, keepdims=True).astype(jnp.int32)
        top = jnp.maximum(top, jnp.broadcast_to(size, (blocks, COLS)))
    longest[...] = jnp.broadcast_to(jnp.max(top.astype(F32)), (8, COLS)).astype(jnp.int32)

    own[...] = jnp.broadcast_to(line_ref[pl.ds(slab, 1), :], own.shape)
    sent = in_part(own[...], lax.broadcasted_iota(jnp.int32, own.shape, 0))
    total = running(sent.astype(jnp.int32))
    send_len[...] = jnp.broadcast_to(total[:, number - 1 :], send_len.shape)
    rank = total - sent.astype(jnp.int32)
    row_ids = split_index(lax.broadcasted_iota(jnp.int32, (1, number), 1))
    for q in range(n_img):
        out = compacted(sent[q : q + 1], rank[q : q + 1], row_ids, lead)
        src_ref[q * lead : (q + 1) * lead, :] = (32.0 * out[0] + out[1]).astype(jnp.int32)

    member = in_part(lines, group)
    place = running(member.astype(jnp.int32)) - member.astype(jnp.int32)
    place = jnp.minimum(place, cap - 1)
    local = plane_ref[...] - slab * planes_here
    here = member & (local >= 0) & (local < planes_here)
    total = running(here.astype(jnp.int32))
    recv_len[...] = jnp.broadcast_to(total[:, number - 1 :], recv_len.shape)
    rank = total - here.astype(jnp.int32)
    target = local * line_stride(lines_here) + lines - group * lines_here + HEAD
    target = jnp.where(here, target, 0)
    for v in range(blocks):
        row = slice(v, v + 1)
        values = split_index(place[row]) + split_index(target[row]) + split_weight(wgt_ref[row, :])
        out = compacted(here[row], rank[row], values, lead)
        at = slice(v * lead, (v + 1) * lead)
        code_ref[at, :] = (
            32768.0 * out[2] + 1024.0 * out[3] + 32.0 * out[0] + out[1]
        ).astype(jnp.int32)
        w_ref[at, :] = out[4] + out[5] + out[6]


def lists(row_plane, row_line, row_weight, n_vol, n_img, planes_here, lines_here, cap):
    lead = 8
    assert cap <= lead * COLS
    number = ROWS // n_vol * K

    def order(x):
        return x.T.reshape(n_vol, number)

    def table(blocks, dtype=jnp.int32):
        return jax.ShapeDtypeStruct((blocks * lead, COLS), dtype)

    return pl.pallas_call(
        partial(lists_kernel, n_img, planes_here, lines_here, cap),
        out_shape=[
            table(n_img),
            table(n_vol),
            table(n_vol, F32),
            jax.ShapeDtypeStruct((8, COLS), jnp.int32),
            jax.ShapeDtypeStruct((n_vol, COLS), jnp.int32),
            jax.ShapeDtypeStruct((8, COLS), jnp.int32),
        ],
        in_specs=[vmem()] * 3,
        out_specs=[vmem()] * 6,
        scratch_shapes=[pltpu.VMEM((8, number), jnp.int32)],
        compiler_params=pltpu.CompilerParams(vmem_limit_bytes=VMEM_LIMIT),
        cost_estimate=cost(6),
        name="lists",
    )(order(row_plane), order(row_line), order(row_weight))


def insert_into(carry, piece, planes_all, lines_all, weights_all, slab_id, planes_here):
    local_plane = planes_all - slab_id * planes_here
    in_slab = (local_plane >= 0) & (local_plane < planes_here)
    dump_row = planes_here * ROWS
    lower_index = jnp.where(in_slab, local_plane * ROWS + lines_all, dump_row).reshape(-1)
    upper_index = jnp.where(in_slab, lower_index.reshape(in_slab.shape) + 1, dump_row).reshape(-1)
    values = piece.reshape(-1, 3 * COLS)
    weight = weights_all.reshape(-1, 1)
    carry = carry.at[lower_index].add(weight * values)
    return carry.at[upper_index].add((1.0 - weight) * values)


def dense_path(
    logits, cand, counts, weighted, squared, cosine, sine,
    plane_share, line_share, weight_share, regularizer, slab_id,
):
    prob = posterior_rows(logits, counts).reshape(TRANS, LMAX, -1)
    hot = (cand[:, None, :] == jnp.arange(K)[None, :, None]).astype(F32)
    post = jnp.einsum("tlb,lkb->tkb", prob, hot).astype(BF16)
    y = jnp.einsum("tkb,rbz->tkrz", post, weighted, preferred_element_type=F32)
    d = jnp.einsum("tkb,rbc->krc", post, squared, preferred_element_type=F32)
    y_re = y[..., :COLS]
    y_im = y[..., COLS:]
    num_re = jnp.sum(cosine[:, None] * y_re + sine[:, None] * y_im, axis=0)
    num_im = jnp.sum(cosine[:, None] * y_im - sine[:, None] * y_re, axis=0)
    partial_value = lax.psum_scatter(
        jnp.stack([num_re, num_im, d], axis=2), "img", scatter_dimension=0, tiled=True
    )
    planes_here = regularizer.shape[0]
    inserted = insert_into(
        jnp.zeros((planes_here * ROWS + 1, 3 * COLS), F32),
        lax.all_gather(partial_value, "vol", axis=1, tiled=True),
        plane_share,
        line_share,
        weight_share,
        slab_id,
        planes_here,
    )
    slab = inserted[: planes_here * ROWS].reshape(planes_here, ROWS, 3, COLS)
    summed = lax.psum_scatter(slab, "img", scatter_dimension=1, tiled=True)
    denom = summed[:, :, 2] + regularizer
    return jnp.stack([summed[:, :, 0] / denom, summed[:, :, 1] / denom], axis=0)


def body(
    images, defocus, candidates, counts, noise_weight, volume,
    row_plane, row_line, row_weight, regularizer,
):
    rows = noise_weight.shape[0]
    planes_here = volume.shape[1]
    lines_here = regularizer.shape[1]
    slab_id = lax.axis_index("vol")
    group_id = lax.axis_index("img")
    n_vol = lax.axis_size("vol")
    n_img = lax.axis_size("img")
    global_rows = slab_id * rows + jnp.arange(rows)
    row_freq = (global_rows.astype(F32) - ROWS // 2) / ROWS
    col_freq = jnp.arange(COLS).astype(F32) / (2 * COLS)
    share = K // n_img
    first = group_id * share
    plane_share = lax.dynamic_slice_in_dim(row_plane, first, share, 0)
    line_share = lax.dynamic_slice_in_dim(row_line, first, share, 0)
    weight_share = lax.dynamic_slice_in_dim(row_weight, first, share, 0)

    aligned = max(1, 16 // rows)
    share_a = share * 11 // 16 // aligned * aligned
    messages = extract(volume, row_plane, row_line, row_weight, n_vol, share, share_a)
    cosine, sine = shift_phases(row_freq, col_freq, TRANS)
    weighted, squared = weigh(images, defocus, noise_weight, row_freq, col_freq)
    mean = rows * K // n_img
    cap = -(-int(mean + 4.2 * math.sqrt(mean)) // 32) * 32
    src, code, wgt, send_len, recv_len, longest = lists(
        row_plane, row_line, row_weight, n_vol, n_img, planes_here, lines_here, cap
    )
    own_a, own_b = to_pixel_rows(messages, n_vol, weighted)
    slices_b = from_partners(own_b, n_img)
    slices_a = from_partners(own_a, n_img)
    slices = [x for both in zip(slices_a, slices_b) for x in both]
    cand = candidates.T
    count_row = counts[None, :]
    partial_logits = candidate_logits(code, slices, weighted, squared, cosine, sine, cand)
    pair_logits = partial_logits + lax.ppermute(partial_logits, "vol", flip(n_vol, 1))
    logits = [pair_logits] + [
        lax.ppermute(pair_logits, "vol", along_z(n_vol, d)) for d in range(1, n_vol // 2)
    ]

    keep, send = project(
        src.reshape(-1), send_len, n_img, logits, cand, count_row, weighted, squared, cosine, sine, cap
    )
    low, high = to_member(keep, send, n_img)
    pieces = ring_gather(low, high, n_vol)

    def listed():
        return insert(recv_len, code.reshape(-1), wgt.reshape(-1), pieces, regularizer)

    def dense():
        return dense_path(
            sum(logits[1:], logits[0]), cand, count_row, weighted, squared, cosine, sine,
            plane_share, line_share, weight_share, regularizer, slab_id,
        )

    return lax.cond(longest[0, 0] <= cap, listed, dense)


def solution(mesh):
    return jax.shard_map(
        body,
        mesh=mesh,
        in_specs=(
            P(None, "img", "vol", None),
            P("img"),
            P("img", None),
            P("img"),
            P("vol", None),
            P(None, "vol", None, None),
            P(),
            P(),
            P(),
            P("vol", "img", None),
        ),
        out_specs=P(None, "vol", "img", None),
        check_vma=False,
    )
```

```python
import math
from functools import partial

import jax
import jax.numpy as jnp
from jax import lax
from jax.experimental import pallas as pl
from jax.experimental.pallas import tpu as pltpu
from jax.sharding import PartitionSpec as P

ROWS = 256
COLS = 128
K = 64
TRANS = 4
LMAX = 8
AMPLITUDE = 0.1
VMEM_LIMIT = 56 * 1024 * 1024
BF16 = jnp.bfloat16
F32 = jnp.float32


def params(steps):
    return pltpu.CompilerParams(
        dimension_semantics=("arbitrary",) * steps, vmem_limit_bytes=VMEM_LIMIT
    )


def smem():
    return pl.BlockSpec(memory_space=pltpu.SMEM)


def vmem():
    return pl.BlockSpec(memory_space=pltpu.VMEM)


def cost(us):
    return pl.CostEstimate(flops=0, transcendentals=0, bytes_accessed=int(us * 3.69e6))


def hbm():
    return pl.BlockSpec(memory_space=pl.ANY)


def shift_phases(row_freq, col_freq, number):
    shift_ids = jnp.arange(number)
    shift_x = (shift_ids % 2).astype(F32) - 0.5
    shift_y = (shift_ids // 2).astype(F32) - 0.5
    angle = (
        -2.0
        * math.pi
        * (
            shift_x[:, None, None] * col_freq[None, None, :]
            + shift_y[:, None, None] * row_freq[None, :, None]
        )
    )
    return (jnp.cos(angle), jnp.sin(angle))


def along_z(n_vol, shift):
    count = n_vol // 2
    return [(v, (v // 2 + shift) % count * 2 + v % 2) for v in range(n_vol)]


def flip(number, mask):
    return [(v, v ^ mask) for v in range(number)]


def ring_of(n_vol):
    return list(range(0, n_vol, 2)) + list(range(n_vol - 1, 0, -2))


def extract_kernel(rows, planes_here, *refs):
    plane_ref, line_ref, weight_hbm, vol_hbm = refs[:4]
    parts_a = (refs[4:6], refs[6:8])
    vol, pair, idx_v, flag_v, idx_s, flag_s, w_s, sem = refs[-8:]
    parts_b = refs[8:-8]
    slab = lax.axis_index("vol")
    share = idx_v.shape[0] // 2
    first = lax.axis_index("img") * share
    height = planes_here * ROWS
    count_z = len(parts_b)
    load = pltpu.make_async_copy(vol_hbm, vol.at[:, :height, :], sem.at[0])
    load.start()
    loads_w = [
        pltpu.make_async_copy(
            weight_hbm.at[pl.ds(first, share), pl.ds(h * COLS, COLS)],
            w_s.at[pl.ds(h * share, share), :],
            sem.at[4 + h],
        )
        for h in range(2)
    ]
    for copy in loads_w:
        copy.start()
    local = plane_ref[pl.ds(first, share), :] - slab * planes_here
    owned = (local >= 0) & (local < planes_here)
    idx = jnp.where(owned, local * ROWS + line_ref[pl.ds(first, share), :], height)
    for h in range(2):
        idx_v[h * share : (h + 1) * share, :] = idx[:, h * COLS : (h + 1) * COLS]
    eights = (
        lax.broadcasted_iota(jnp.int32, (ROWS, COLS), 0) >> 3
        == lax.broadcasted_iota(jnp.int32, (ROWS, COLS), 1)
    )
    held = jnp.dot(
        owned.astype(F32).astype(BF16), eights.astype(F32).astype(BF16), preferred_element_type=F32
    )
    eight = lax.broadcasted_iota(jnp.int32, (COLS, COLS), 0)
    bits = jnp.where(
        eight >> 4 == lax.broadcasted_iota(jnp.int32, (COLS, COLS), 1), 1 << (eight & 15), 0
    )
    flag_v[...] = jnp.dot(
        (held > 0.0).astype(F32).astype(BF16),
        bits.astype(F32).astype(BF16),
        preferred_element_type=F32,
    ).astype(jnp.int32)
    to_idx = pltpu.make_async_copy(idx_v, idx_s, sem.at[2])
    to_flag = pltpu.make_async_copy(flag_v, flag_s, sem.at[3])
    to_idx.start()
    to_flag.start()
    vol[:, height : height + 8, :] = jnp.zeros((2, 8, COLS), F32)
    for ref in refs[4:-8]:
        ref[...] = jnp.zeros_like(ref)
    to_idx.wait()
    to_flag.wait()
    for copy in loads_w:
        copy.wait()
    load.wait()
    lower_row = lax.broadcasted_iota(jnp.int32, (2, COLS), 0) == 0
    per_k = max(1, 16 // rows)
    per_block = max(1, rows // 16)
    run = min(rows, 16)

    def message(out, lead, k, words, r0, base):
        word = jnp.where(r0 >= COLS, words[1], words[0])
        lane = r0 & (COLS - 1)
        hits = (word >> (lane >> 3)) & ((1 << (run // 8)) - 1)

        @pl.when(hits > 0)
        def _():
            line = k + share * (r0 >> 7)
            for u in range(16):
                i = idx_s[line + u // run, lane + u % run]
                w = w_s[line + u // run, lane + u % run]
                both = jnp.where(lower_row, w, 1.0 - w)
                for j in range(2):
                    pair[j, 2 * u : 2 * u + 2, :] = both * vol[j, pl.ds(i, 2), :]
            for j in range(2):
                value = pair[j, pl.ds(0, 16, stride=2), :] + pair[j, pl.ds(1, 16, stride=2), :]
                out[lead, j, pl.ds(base, 16), :] = value.astype(BF16)

    places = []
    for dz in range(count_z):
        for dy in range(2):
            z = (slab >> 1) + dz
            block = jnp.where(z >= count_z, z - count_z, z) * 2 + ((slab + dy) & 1)
            places.append((dz, dy, block))
    k0 = 0
    for part in range(3):
        count = (parts_a + (parts_b,))[part][0].shape[2] // rows

        def turn(t, carry, k0=k0, part=part):
            k = k0 + t * per_k
            words = [flag_s[k, 0], flag_s[k, 1]]
            for i in range(1, per_k):
                words = [words[0] | flag_s[k + i, 0], words[1] | flag_s[k + i, 1]]
            for dz, dy, block in places:
                out, lead = (parts_a[part][dy], dz) if part < 2 else (parts_b[dz], dy)
                for g in range(per_block):
                    base = pl.multiple_of((t * per_block + g) * 16, 16)
                    message(out, lead, k, words, block * rows + 16 * g, base)
            return carry

        lax.fori_loop(0, count // per_k, turn, 0)
        k0 += count


def extract(volume, row_plane, row_line, row_weight, n_vol, shares):
    planes_here = volume.shape[1]
    rows = ROWS // n_vol
    count_z = n_vol // 2
    share = sum(shares)
    shape_a, shape_c = [
        jax.ShapeDtypeStruct((count_z, 2, n * rows, COLS), BF16) for n in shares[:2]
    ]
    shape_b = jax.ShapeDtypeStruct((2, 2, shares[2] * rows, COLS), BF16)
    return pl.pallas_call(
        partial(extract_kernel, rows, planes_here),
        out_shape=[shape_a, shape_a, shape_c, shape_c] + [shape_b] * count_z,
        in_specs=[vmem(), vmem(), hbm(), hbm()],
        out_specs=[vmem()] * (4 + count_z),
        scratch_shapes=[
            pltpu.VMEM((2, planes_here * ROWS + 8, COLS), F32),
            pltpu.VMEM((2, 32, COLS), F32),
            pltpu.VMEM((2 * share, COLS), jnp.int32),
            pltpu.VMEM((share, COLS), jnp.int32),
            pltpu.SMEM((2 * share, COLS), jnp.int32),
            pltpu.SMEM((share, COLS), jnp.int32),
            pltpu.SMEM((2 * share, COLS), F32),
            pltpu.SemaphoreType.DMA((6,)),
        ],
        compiler_params=pltpu.CompilerParams(vmem_limit_bytes=VMEM_LIMIT),
        cost_estimate=cost(11),
        name="extract",
    )(row_plane, row_line, row_weight, volume.reshape(2, planes_here * ROWS, COLS))


def combine_kernel(count, *refs):
    outs = refs[count + 1 :]
    for d, out in enumerate(outs):
        total = refs[0][d]
        for ref in refs[1:count]:
            total = total + ref[d]
        out[...] = total


def combine(terms, after):
    shape = terms[0].shape
    return pl.pallas_call(
        partial(combine_kernel, len(terms)),
        out_shape=[jax.ShapeDtypeStruct(shape[1:], BF16)] * shape[0],
        in_specs=[vmem()] * len(terms) + [hbm()],
        out_specs=[vmem()] * shape[0],
        compiler_params=pltpu.CompilerParams(vmem_limit_bytes=VMEM_LIMIT),
        cost_estimate=cost(2),
        name="combine",
    )(*terms, after)


def to_pixel_rows(messages, n_vol, first_with):
    keep_1, send_1, keep_2, send_2, keep_b = messages[:5]
    count_z = n_vol // 2
    got_1 = lax.ppermute(send_1, "vol", flip(n_vol, 1))
    got_b = [lax.ppermute(m, "vol", along_z(n_vol, d + 1)) for d, m in enumerate(messages[5:])]
    got_2 = lax.ppermute(send_2, "vol", flip(n_vol, 1))
    sums_1 = combine([keep_1, got_1], first_with)
    moved_1 = [lax.ppermute(sums_1[d], "vol", along_z(n_vol, d)) for d in range(1, count_z)]
    sums_b = combine([keep_b, *got_b], sums_1[0])
    moved_b = lax.ppermute(sums_b[1], "vol", flip(n_vol, 1))
    sums_2 = combine([keep_2, got_2], sums_b[0])
    moved_2 = [lax.ppermute(sums_2[d], "vol", along_z(n_vol, d)) for d in range(1, count_z)]
    return [added(sums_1[0], *moved_1), added(sums_2[0], *moved_2), added(sums_b[0], moved_b)]


def from_partners(x, n_img):
    return [x] + [lax.ppermute(x, "img", flip(n_img, m)) for m in range(1, n_img)]


def ring_gather(low, high_terms, n_vol):
    ring = ring_of(n_vol)
    ahead = [(ring[p], ring[(p + 1) % n_vol]) for p in range(n_vol)]
    back = [(b, a) for a, b in ahead]
    one_low, two_low = lax.ppermute(low, "vol", ahead), lax.ppermute(low, "vol", back)
    high = added(*high_terms, after=[one_low, two_low])
    pieces = [low, high]
    one_high, two_high = high, high
    for d in range(1, n_vol // 2):
        if d > 1:
            one_low, two_low = lax.ppermute(one_low, "vol", ahead), lax.ppermute(two_low, "vol", back)
        one_high, two_high = lax.ppermute(one_high, "vol", ahead), lax.ppermute(two_high, "vol", back)
        pieces += [one_low, one_high, two_low, two_high]
    return pieces + [lax.ppermute(one_low, "vol", ahead), lax.ppermute(two_high, "vol", back)]


def weigh_kernel(img_ref, sa_ref, ca_ref, sx_ref, cx_ref, nw_ref, wt_ref, sq_ref, buf):
    count = img_ref.shape[1]
    rows = img_ref.shape[2]
    pitch = rows + 1
    for j in range(2):
        for b in range(count):
            buf[j, b * pitch : b * pitch + rows, :] = img_ref[j, b].astype(F32)
    sx = sx_ref[...]
    cx = cx_ref[...]
    for r in range(rows):
        contrast = -(sa_ref[:, r : r + 1] * cx + ca_ref[:, r : r + 1] * sx)
        noise = nw_ref[r : r + 1, :]
        scale = contrast * noise
        for j in range(2):
            x = buf[j, pl.ds(r, count, stride=pitch), :]
            wt_ref[r, :, j * COLS : (j + 1) * COLS] = (scale * x).astype(BF16)
        sq_ref[r] = (contrast * contrast * noise).astype(BF16)


def weigh(images, defocus, noise_weight, row_freq, col_freq):
    count = images.shape[1]
    rows = images.shape[2]
    step = 64
    angle_r = defocus[:, None] * (row_freq * row_freq)[None, :] + math.asin(AMPLITUDE)
    angle_c = defocus[:, None] * (col_freq * col_freq)[None, :]
    return pl.pallas_call(
        weigh_kernel,
        grid=(count // step,),
        out_shape=[
            jax.ShapeDtypeStruct((rows, count, 2 * COLS), BF16),
            jax.ShapeDtypeStruct((rows, count, COLS), BF16),
        ],
        in_specs=[
            pl.BlockSpec((2, step, rows, COLS), lambda b: (0, b, 0, 0)),
            pl.BlockSpec((step, rows), lambda b: (b, 0)),
            pl.BlockSpec((step, rows), lambda b: (b, 0)),
            pl.BlockSpec((step, COLS), lambda b: (b, 0)),
            pl.BlockSpec((step, COLS), lambda b: (b, 0)),
            pl.BlockSpec((rows, COLS), lambda b: (0, 0)),
        ],
        out_specs=[
            pl.BlockSpec((rows, step, 2 * COLS), lambda b: (0, b, 0)),
            pl.BlockSpec((rows, step, COLS), lambda b: (0, b, 0)),
        ],
        scratch_shapes=[pltpu.VMEM((2, step * (rows + 1), COLS), F32)],
        compiler_params=params(1),
        cost_estimate=cost(12),
        name="weigh",
    )(
        images,
        jnp.sin(angle_r),
        jnp.cos(angle_r),
        jnp.sin(angle_c),
        jnp.cos(angle_c),
        noise_weight,
    )


def logits_kernel(wt_ref, sq_ref, cos_ref, sin_ref, cand_ref, *rest):
    sl_refs = rest[1:-4]
    out_ref, part, acc, quad = rest[-4:]
    step = pl.program_id(0)
    groups = len(sl_refs) // 3
    rows = part.shape[1] // K - 1
    share = K // groups
    pitch = rows + 1
    inner = wt_ref.shape[0]

    @pl.when(step == 0)
    def _():
        for m in range(groups):
            at = m * share
            for ref in sl_refs[3 * m : 3 * m + 3]:
                for j in range(2):
                    for k in range(ref.shape[1] // rows):
                        row = (at + k) * pitch
                        part[j, row : row + rows, :] = ref[j, k * rows : (k + 1) * rows].astype(F32)
                at += ref.shape[1] // rows
        acc[...] = jnp.zeros_like(acc)
        quad[...] = jnp.zeros_like(quad)

    dims = (((1,), (1,)), ((), ()))
    total = acc[...]
    total_q = quad[...]
    for u in range(inner):
        re = part[0, pl.ds(step * inner + u, K, stride=pitch), :]
        im = part[1, pl.ds(step * inner + u, K, stride=pitch), :]
        shifted = []
        for t in range(TRANS):
            c = cos_ref[t, u : u + 1, :]
            s = sin_ref[t, u : u + 1, :]
            shifted.append(
                jnp.concatenate(
                    [(c * re - s * im).astype(BF16), (s * re + c * im).astype(BF16)], axis=1
                )
            )
        left = jnp.concatenate(shifted, axis=0)
        power = (re * re + im * im).astype(BF16)
        total = total + lax.dot_general(left, wt_ref[u], dims, preferred_element_type=F32)
        total_q = total_q + lax.dot_general(power, sq_ref[u], dims, preferred_element_type=F32)
    acc[...] = total
    quad[...] = total_q

    @pl.when(step == pl.num_programs(0) - 1)
    def _():
        ids = lax.broadcasted_iota(jnp.int32, quad.shape, 0) ^ (lax.axis_index("img") * share)
        half = 0.5 * quad[...]
        for t in range(TRANS):
            value = acc[t * K : (t + 1) * K, :] - half
            for l in range(LMAX):
                pick = jnp.where(ids == cand_ref[l : l + 1, :], value, 0.0)
                out_ref[t * LMAX + l : t * LMAX + l + 1, :] = jnp.sum(pick, axis=0, keepdims=True)


def candidate_logits(after, slices, weighted, squared, cosine, sine, cand):
    rows, count = squared.shape[:2]
    inner = 8
    return pl.pallas_call(
        logits_kernel,
        grid=(rows // inner,),
        out_shape=jax.ShapeDtypeStruct((TRANS * LMAX, count), F32),
        in_specs=[
            pl.BlockSpec((inner, count, 2 * COLS), lambda s: (s, 0, 0)),
            pl.BlockSpec((inner, count, COLS), lambda s: (s, 0, 0)),
            pl.BlockSpec((TRANS, inner, COLS), lambda s: (0, s, 0)),
            pl.BlockSpec((TRANS, inner, COLS), lambda s: (0, s, 0)),
            pl.BlockSpec((LMAX, count), lambda s: (0, 0)),
        ]
        + [hbm()]
        + [pl.BlockSpec(x.shape, lambda s: (0, 0, 0)) for x in slices],
        out_specs=pl.BlockSpec((TRANS * LMAX, count), lambda s: (0, 0)),
        scratch_shapes=[
            pltpu.VMEM((2, K * (rows + 1), COLS), F32),
            pltpu.VMEM((TRANS * K, count), F32),
            pltpu.VMEM((K, count), F32),
        ],
        compiler_params=params(1),
        cost_estimate=cost(8),
        name="logits",
    )(weighted, squared, cosine, sine, cand, after, *slices)


def posterior_rows(logits, counts):
    place = lax.broadcasted_iota(jnp.int32, logits.shape, 0) % LMAX
    allowed = place < counts
    masked = jnp.where(allowed, logits, -1e30)
    highest = jnp.max(masked, axis=0, keepdims=True)
    exponent = jnp.where(allowed, jnp.exp(masked - highest), 0.0)
    return (exponent / jnp.sum(exponent, axis=0, keepdims=True)).astype(BF16).astype(F32)


def list_rows(num, src_s, len_s, outs, pick):
    parts = 2 * outs[0].shape[0]
    cap = outs[0].shape[2]
    comps = num.shape[0]
    lead = src_s.shape[0] // parts
    group = lax.axis_index("img")
    for m in range(parts):
        q = group ^ m

        def turn(g, carry, q=q, m=m):
            base = pl.multiple_of(g * 32, 32)
            at = q * lead + base
            for u in range(32):
                s = src_s[at + u]
                for c in range(comps):
                    pick[c, u : u + 1, :] = num[c, pl.ds(s, 1), :]
            for c in range(comps):
                outs[m % 2][m // 2, c, pl.ds(base, 32), :] = pick[c].astype(BF16)
            return carry

        lax.fori_loop(0, (jnp.minimum(len_s[q, 0], cap) + 31) // 32, turn, 0)


def project_kernel(src_s, len_s, cand_ref, cnt_ref, wt_ref, sq_ref, cos_ref, sin_ref, *rest):
    lg_refs = rest[:-6]
    keep_ref, send_ref, post, post_sum, num, pick = rest[-6:]
    step = pl.program_id(0)
    inner = wt_ref.shape[0]

    @pl.when(step == 0)
    def _():
        prob = posterior_rows(sum([ref[...] for ref in lg_refs[1:]], lg_refs[0][...]), cnt_ref[...])
        ids = lax.broadcasted_iota(jnp.int32, (K, prob.shape[1]), 0)
        total = jnp.zeros((K, prob.shape[1]), F32)
        for t in range(TRANS):
            dense = jnp.zeros((K, prob.shape[1]), F32)
            for l in range(LMAX):
                at = t * LMAX + l
                dense = jnp.where(ids == cand_ref[l : l + 1, :], dense + prob[at : at + 1, :], dense)
            post[t * K : (t + 1) * K, :] = dense.astype(BF16)
            total = total + dense
        high = total.astype(BF16)
        post_sum[:K, :] = high
        post_sum[K:, :] = (total - high.astype(F32)).astype(BF16)

    for u in range(inner):
        y = jnp.dot(post[...], wt_ref[u], preferred_element_type=F32)
        d = jnp.dot(post_sum[...], sq_ref[u], preferred_element_type=F32)
        re = jnp.zeros((K, COLS), F32)
        im = jnp.zeros((K, COLS), F32)
        for t in range(TRANS):
            c = cos_ref[t, u : u + 1, :]
            s = sin_ref[t, u : u + 1, :]
            y_re = y[t * K : (t + 1) * K, :COLS]
            y_im = y[t * K : (t + 1) * K, COLS:]
            re = re + (c * y_re + s * y_im)
            im = im + (c * y_im - s * y_re)
        base = pl.multiple_of((step * inner + u) * K, K)
        num[0, pl.ds(base, K), :] = re
        num[1, pl.ds(base, K), :] = im
        num[2, pl.ds(base, K), :] = d[:K] + d[K:]

    @pl.when(step == pl.num_programs(0) - 1)
    def _():
        list_rows(num, src_s, len_s, (keep_ref, send_ref), pick)


def project(src, lengths, n_img, logits, cand, counts, weighted, squared, cosine, sine, cap):
    rows, count = squared.shape[:2]
    inner = 8
    shape = (n_img // 2, 3, cap, COLS)
    return pl.pallas_call(
        project_kernel,
        grid=(rows // inner,),
        out_shape=[jax.ShapeDtypeStruct(shape, BF16)] * 2,
        in_specs=[
            smem(),
            smem(),
            pl.BlockSpec((LMAX, count), lambda s: (0, 0)),
            pl.BlockSpec((1, count), lambda s: (0, 0)),
            pl.BlockSpec((inner, count, 2 * COLS), lambda s: (s, 0, 0)),
            pl.BlockSpec((inner, count, COLS), lambda s: (s, 0, 0)),
            pl.BlockSpec((TRANS, inner, COLS), lambda s: (0, s, 0)),
            pl.BlockSpec((TRANS, inner, COLS), lambda s: (0, s, 0)),
        ]
        + [pl.BlockSpec((TRANS * LMAX, count), lambda s: (0, 0)) for _ in logits],
        out_specs=[pl.BlockSpec(shape, lambda s: (0, 0, 0, 0))] * 2,
        scratch_shapes=[
            pltpu.VMEM((TRANS * K, count), BF16),
            pltpu.VMEM((2 * K, count), BF16),
            pltpu.VMEM((3, rows * K, COLS), F32),
            pltpu.VMEM((3, 32, COLS), F32),
        ],
        compiler_params=params(1),
        cost_estimate=cost(12),
        name="project",
    )(src, lengths, cand, counts, weighted, squared, cosine, sine, *logits)


def to_member(keep, send, n_img):
    got = lax.ppermute(send, "img", flip(n_img, 1))
    half = keep.shape[2] // 2
    terms = []
    for h in range(2):
        cut = slice(h * half, (h + 1) * half)
        summed = [keep[m, :, cut] + got[m, :, cut] for m in range(n_img // 2)]
        moved = [lax.ppermute(summed[m], "img", flip(n_img, 2 * m)) for m in range(1, n_img // 2)]
        terms.append([summed[0], *moved])
    return terms


def added_kernel(count, *refs):
    total = refs[0][...]
    for ref in refs[1:count]:
        total = total + ref[...]
    refs[-1][...] = total


def added(*terms, after=()):
    return pl.pallas_call(
        partial(added_kernel, len(terms)),
        out_shape=jax.ShapeDtypeStruct(terms[0].shape, terms[0].dtype),
        in_specs=[vmem()] * len(terms) + [hbm()] * len(after),
        out_specs=vmem(),
        compiler_params=pltpu.CompilerParams(vmem_limit_bytes=VMEM_LIMIT),
        cost_estimate=cost(1),
        name="added",
    )(*terms, *after)


HEAD = 8


def line_stride(lines_here):
    return lines_here + 2 * HEAD


def insert_kernel(count, len_s, code_hbm, wgt_hbm, reg_hbm, *rest):
    pieces = rest[:count]
    out_hbm = rest[count]
    code_s, wgt_s, held, reg, out, acc, acc_odd, buf, sem_in, sem_piece, sem_out = rest[count + 1 :]
    both_acc = (acc, acc_odd)
    cap = buf.shape[1]
    half = cap // 2
    blocks = len_s.shape[0]
    lead = code_s.shape[0] // blocks
    planes, lines_here = reg.shape[:2]
    stride = line_stride(lines_here)
    slab = lax.axis_index("vol")
    place = jnp.where(slab & 1, blocks - 1 - (slab >> 1), slab >> 1)
    tables = [
        pltpu.make_async_copy(code_hbm, code_s, sem_in.at[0]),
        pltpu.make_async_copy(wgt_hbm, wgt_s, sem_in.at[1]),
    ]
    prior = pltpu.make_async_copy(reg_hbm, reg, sem_in.at[2])
    loads = [
        pltpu.make_async_copy(pieces[i], held.at[i], sem_piece.at[i]) for i in range(count)
    ]
    for copy in tables + loads + [prior]:
        copy.start()
    acc[...] = jnp.zeros_like(acc)
    acc_odd[...] = jnp.zeros_like(acc_odd)
    first = lax.broadcasted_iota(jnp.int32, (2, COLS), 0) == 0
    for copy in tables:
        copy.wait()
    for m in range(count // 2):
        for h in range(2):
            loads[2 * m + h].wait()
            for c in range(3):
                buf[c, h * half : (h + 1) * half, :] = held[2 * m + h, c].astype(F32)
        from_place = place + ((m + 1) // 2) * (-1 if m % 2 else 1)
        from_place = from_place & (blocks - 1)
        block = jnp.where(
            from_place >= blocks // 2, 2 * (blocks - 1 - from_place) + 1, 2 * from_place
        )

        def group_step(g, carry, block=block):
            at = block * lead + g * 8
            for u in range(8):
                code = code_s[at + u]
                s = code & 1023
                to = code >> 10
                w = wgt_s[at + u]
                both = jnp.where(first, w, 1.0 - w)
                into = both_acc[u % 2]
                for c in range(3):
                    row = jnp.broadcast_to(buf[c, pl.ds(s, 1), :], (2, COLS))
                    into[c, pl.ds(to, 2), :] = into[c, pl.ds(to, 2), :] + both * row
            return carry

        lax.fori_loop(0, (jnp.minimum(len_s[block, 0], cap) + 7) // 8, group_step, 0)

    prior.wait()
    chunks = sem_out.shape[0]
    span = planes // chunks
    stores = []
    for i in range(chunks):

        def plane_step(p, carry):
            base = pl.multiple_of(p * stride + HEAD, 8)
            total = [
                acc[c, pl.ds(base, lines_here), :] + acc_odd[c, pl.ds(base, lines_here), :]
                for c in range(3)
            ]
            inverse = 1.0 / (total[2] + reg[p])
            out[0, p] = total[0] * inverse
            out[1, p] = total[1] * inverse
            return carry

        lax.fori_loop(i * span, (i + 1) * span, plane_step, 0)
        part = pl.ds(i * span, span)
        stores.append(pltpu.make_async_copy(out.at[:, part], out_hbm.at[:, part], sem_out.at[i]))
        stores[-1].start()
    for copy in stores:
        copy.wait()


def insert(lengths, code, weights, pieces, regularizer):
    half = pieces[0].shape[1]
    planes, lines_here = regularizer.shape[:2]
    count = len(pieces)
    chunks = 4
    acc = pltpu.VMEM((3, planes * line_stride(lines_here), COLS), F32)
    result = (2, planes, lines_here, COLS)
    return pl.pallas_call(
        partial(insert_kernel, count),
        out_shape=jax.ShapeDtypeStruct(result, F32),
        in_specs=[smem()] + [hbm()] * (3 + count),
        out_specs=hbm(),
        scratch_shapes=[
            pltpu.SMEM(code.shape, jnp.int32),
            pltpu.SMEM(weights.shape, F32),
            pltpu.VMEM((count, 3, half, COLS), BF16),
            pltpu.VMEM(regularizer.shape, F32),
            pltpu.VMEM(result, F32),
            acc,
            acc,
            pltpu.VMEM((3, 2 * half, COLS), F32),
            pltpu.SemaphoreType.DMA((3,)),
            pltpu.SemaphoreType.DMA((count,)),
            pltpu.SemaphoreType.DMA((chunks,)),
        ],
        compiler_params=pltpu.CompilerParams(vmem_limit_bytes=VMEM_LIMIT),
        cost_estimate=cost(9),
        name="insert",
    )(lengths, code, weights, regularizer, *pieces)


def running(x):
    lanes = lax.broadcasted_iota(jnp.int32, x.shape, 1)
    step = 1
    while step < x.shape[1]:
        x = x + jnp.where(lanes >= step, pltpu.roll(x, step, 1), 0)
        step *= 2
    return x


def split_index(x):
    return [(x >> 5).astype(F32), (x & 31).astype(F32)]


def split_weight(w):
    a = w.astype(BF16).astype(F32)
    b = (w - a).astype(BF16).astype(F32)
    return [a, b, w - a - b]


def compacted(member, rank, values, lead):
    high = jnp.where(member, rank >> 5, -1)
    low = rank & 31
    spot = lax.broadcasted_iota(jnp.int32, (4 * lead, rank.shape[1]), 0)
    shift = lead.bit_length() - 1
    left = ((spot & (lead - 1)) * 4 + (spot >> shift)) == high
    hot = lax.broadcasted_iota(jnp.int32, (32, rank.shape[1]), 0) == low
    right = jnp.concatenate([jnp.where(hot, v, 0.0).astype(BF16) for v in values], axis=0)
    out = lax.dot_general(
        left.astype(F32).astype(BF16), right, (((1,), (1,)), ((), ())), preferred_element_type=F32
    )
    return [
        jnp.concatenate(
            [out[h * lead : (h + 1) * lead, 32 * i : 32 * (i + 1)] for h in range(4)], axis=1
        )
        for i in range(len(values))
    ]


def lists_kernel(
    n_img, planes_here, lines_here, cap,
    plane_ref, line_ref, wgt_ref,
    src_ref, code_ref, w_ref, send_len, recv_len, longest, own,
):
    slab = lax.axis_index("vol")
    group = lax.axis_index("img")
    blocks, number = line_ref.shape
    lead = src_ref.shape[0] // n_img
    lines = line_ref[...]

    def in_part(x, part):
        return (x >= part * lines_here - 1) & (x < (part + 1) * lines_here)

    top = jnp.zeros((blocks, COLS), jnp.int32)
    for q in range(n_img):
        size = jnp.sum(in_part(lines, q).astype(F32), axis=1, keepdims=True).astype(jnp.int32)
        top = jnp.maximum(top, jnp.broadcast_to(size, (blocks, COLS)))
    longest[...] = jnp.broadcast_to(jnp.max(top.astype(F32)), (8, COLS)).astype(jnp.int32)

    own[...] = jnp.broadcast_to(line_ref[pl.ds(slab, 1), :], own.shape)
    sent = in_part(own[...], lax.broadcasted_iota(jnp.int32, own.shape, 0))
    total = running(sent.astype(jnp.int32))
    send_len[...] = jnp.broadcast_to(total[:, number - 1 :], send_len.shape)
    rank = total - sent.astype(jnp.int32)
    row_ids = split_index(lax.broadcasted_iota(jnp.int32, (1, number), 1))
    for q in range(n_img):
        out = compacted(sent[q : q + 1], rank[q : q + 1], row_ids, lead)
        src_ref[q * lead : (q + 1) * lead, :] = (32.0 * out[0] + out[1]).astype(jnp.int32)

    member = in_part(lines, group)
    place = running(member.astype(jnp.int32)) - member.astype(jnp.int32)
    place = jnp.minimum(place, cap - 1)
    local = plane_ref[...] - slab * planes_here
    here = member & (local >= 0) & (local < planes_here)
    total = running(here.astype(jnp.int32))
    recv_len[...] = jnp.broadcast_to(total[:, number - 1 :], recv_len.shape)
    rank = total - here.astype(jnp.int32)
    target = local * line_stride(lines_here) + lines - group * lines_here + HEAD
    target = jnp.where(here, target, 0)
    for v in range(blocks):
        row = slice(v, v + 1)
        values = split_index(place[row]) + split_index(target[row]) + split_weight(wgt_ref[row, :])
        out = compacted(here[row], rank[row], values, lead)
        at = slice(v * lead, (v + 1) * lead)
        code_ref[at, :] = (
            32768.0 * out[2] + 1024.0 * out[3] + 32.0 * out[0] + out[1]
        ).astype(jnp.int32)
        w_ref[at, :] = out[4] + out[5] + out[6]


def lists(row_plane, row_line, row_weight, n_vol, n_img, planes_here, lines_here, cap):
    lead = 8
    assert cap <= lead * COLS
    number = ROWS // n_vol * K

    def order(x):
        return x.T.reshape(n_vol, number)

    def table(blocks, dtype=jnp.int32):
        return jax.ShapeDtypeStruct((blocks * lead, COLS), dtype)

    return pl.pallas_call(
        partial(lists_kernel, n_img, planes_here, lines_here, cap),
        out_shape=[
            table(n_img),
            table(n_vol),
            table(n_vol, F32),
            jax.ShapeDtypeStruct((8, COLS), jnp.int32),
            jax.ShapeDtypeStruct((n_vol, COLS), jnp.int32),
            jax.ShapeDtypeStruct((8, COLS), jnp.int32),
        ],
        in_specs=[vmem()] * 3,
        out_specs=[vmem()] * 6,
        scratch_shapes=[pltpu.VMEM((8, number), jnp.int32)],
        compiler_params=pltpu.CompilerParams(vmem_limit_bytes=VMEM_LIMIT),
        cost_estimate=cost(6),
        name="lists",
    )(order(row_plane), order(row_line), order(row_weight))


def insert_into(carry, piece, planes_all, lines_all, weights_all, slab_id, planes_here):
    local_plane = planes_all - slab_id * planes_here
    in_slab = (local_plane >= 0) & (local_plane < planes_here)
    dump_row = planes_here * ROWS
    lower_index = jnp.where(in_slab, local_plane * ROWS + lines_all, dump_row).reshape(-1)
    upper_index = jnp.where(in_slab, lower_index.reshape(in_slab.shape) + 1, dump_row).reshape(-1)
    values = piece.reshape(-1, 3 * COLS)
    weight = weights_all.reshape(-1, 1)
    carry = carry.at[lower_index].add(weight * values)
    return carry.at[upper_index].add((1.0 - weight) * values)


def dense_path(
    logits, cand, counts, weighted, squared, cosine, sine,
    plane_share, line_share, weight_share, regularizer, slab_id,
):
    prob = posterior_rows(logits, counts).reshape(TRANS, LMAX, -1)
    hot = (cand[:, None, :] == jnp.arange(K)[None, :, None]).astype(F32)
    post = jnp.einsum("tlb,lkb->tkb", prob, hot).astype(BF16)
    y = jnp.einsum("tkb,rbz->tkrz", post, weighted, preferred_element_type=F32)
    d = jnp.einsum("tkb,rbc->krc", post, squared, preferred_element_type=F32)
    y_re = y[..., :COLS]
    y_im = y[..., COLS:]
    num_re = jnp.sum(cosine[:, None] * y_re + sine[:, None] * y_im, axis=0)
    num_im = jnp.sum(cosine[:, None] * y_im - sine[:, None] * y_re, axis=0)
    partial_value = lax.psum_scatter(
        jnp.stack([num_re, num_im, d], axis=2), "img", scatter_dimension=0, tiled=True
    )
    planes_here = regularizer.shape[0]
    inserted = insert_into(
        jnp.zeros((planes_here * ROWS + 1, 3 * COLS), F32),
        lax.all_gather(partial_value, "vol", axis=1, tiled=True),
        plane_share,
        line_share,
        weight_share,
        slab_id,
        planes_here,
    )
    slab = inserted[: planes_here * ROWS].reshape(planes_here, ROWS, 3, COLS)
    summed = lax.psum_scatter(slab, "img", scatter_dimension=1, tiled=True)
    denom = summed[:, :, 2] + regularizer
    return jnp.stack([summed[:, :, 0] / denom, summed[:, :, 1] / denom], axis=0)


def body(
    images, defocus, candidates, counts, noise_weight, volume,
    row_plane, row_line, row_weight, regularizer,
):
    rows = noise_weight.shape[0]
    planes_here = volume.shape[1]
    lines_here = regularizer.shape[1]
    slab_id = lax.axis_index("vol")
    group_id = lax.axis_index("img")
    n_vol = lax.axis_size("vol")
    n_img = lax.axis_size("img")
    global_rows = slab_id * rows + jnp.arange(rows)
    row_freq = (global_rows.astype(F32) - ROWS // 2) / ROWS
    col_freq = jnp.arange(COLS).astype(F32) / (2 * COLS)
    share = K // n_img
    first = group_id * share
    plane_share = lax.dynamic_slice_in_dim(row_plane, first, share, 0)
    line_share = lax.dynamic_slice_in_dim(row_line, first, share, 0)
    weight_share = lax.dynamic_slice_in_dim(row_weight, first, share, 0)

    aligned = max(1, 16 // rows)
    share_b = max(1, share * 5 // 16 // aligned) * aligned
    share_2 = max(1, (share - share_b) // 2 // aligned) * aligned
    shares = (share - share_b - share_2, share_2, share_b)
    messages = extract(volume, row_plane, row_line, row_weight, n_vol, shares)
    cosine, sine = shift_phases(row_freq, col_freq, TRANS)
    weighted, squared = weigh(images, defocus, noise_weight, row_freq, col_freq)
    mean = rows * K // n_img
    cap = -(-int(mean + 4.2 * math.sqrt(mean)) // 32) * 32
    src, code, wgt, send_len, recv_len, longest = lists(
        row_plane, row_line, row_weight, n_vol, n_img, planes_here, lines_here, cap
    )
    owns = to_pixel_rows(messages, n_vol, weighted)
    parts = [from_partners(own, n_img) for own in (owns[2], owns[0], owns[1])]
    slices = [x for three in zip(parts[1], parts[2], parts[0]) for x in three]

    cand = candidates.T
    count_row = counts[None, :]
    partial_logits = candidate_logits(code, slices, weighted, squared, cosine, sine, cand)
    pair_logits = partial_logits + lax.ppermute(partial_logits, "vol", flip(n_vol, 1))
    logits = [pair_logits] + [
        lax.ppermute(pair_logits, "vol", along_z(n_vol, d)) for d in range(1, n_vol // 2)
    ]

    keep, send = project(
        src.reshape(-1), send_len, n_img, logits, cand, count_row, weighted, squared, cosine, sine, cap
    )
    low_terms, high_terms = to_member(keep, send, n_img)
    pieces = ring_gather(added(*low_terms), high_terms, n_vol)

    def listed():
        return insert(recv_len, code.reshape(-1), wgt.reshape(-1), pieces, regularizer)

    def dense():
        return dense_path(
            sum(logits[1:], logits[0]), cand, count_row, weighted, squared, cosine, sine,
            plane_share, line_share, weight_share, regularizer, slab_id,
        )

    return lax.cond(longest[0, 0] <= cap, listed, dense)


def solution(mesh):
    return jax.shard_map(
        body,
        mesh=mesh,
        in_specs=(
            P(None, "img", "vol", None),
            P("img"),
            P("img", None),
            P("img"),
            P("vol", None),
            P(None, "vol", None, None),
            P(),
            P(),
            P(),
            P("vol", "img", None),
        ),
        out_specs=P(None, "vol", "img", None),
        check_vma=False,
    )
```

```python
import math
from functools import partial

import jax
import jax.numpy as jnp
from jax import lax
from jax.experimental import pallas as pl
from jax.experimental.pallas import tpu as pltpu
from jax.sharding import PartitionSpec as P

ROWS = 256
COLS = 128
K = 64
TRANS = 4
LMAX = 8
AMPLITUDE = 0.1
VMEM_LIMIT = 56 * 1024 * 1024
BF16 = jnp.bfloat16
F32 = jnp.float32


def params(steps):
    return pltpu.CompilerParams(
        dimension_semantics=("arbitrary",) * steps, vmem_limit_bytes=VMEM_LIMIT
    )


def smem():
    return pl.BlockSpec(memory_space=pltpu.SMEM)


def vmem():
    return pl.BlockSpec(memory_space=pltpu.VMEM)


def cost(us):
    return pl.CostEstimate(flops=0, transcendentals=0, bytes_accessed=int(us * 3.69e6))


def hbm():
    return pl.BlockSpec(memory_space=pl.ANY)


def shift_phases(row_freq, col_freq, number):
    shift_ids = jnp.arange(number)
    shift_x = (shift_ids % 2).astype(F32) - 0.5
    shift_y = (shift_ids // 2).astype(F32) - 0.5
    angle = (
        -2.0
        * math.pi
        * (
            shift_x[:, None, None] * col_freq[None, None, :]
            + shift_y[:, None, None] * row_freq[None, :, None]
        )
    )
    return (jnp.cos(angle), jnp.sin(angle))


def along_z(n_vol, shift):
    count = n_vol // 2
    return [(v, (v // 2 + shift) % count * 2 + v % 2) for v in range(n_vol)]


def flip(number, mask):
    return [(v, v ^ mask) for v in range(number)]


def ring_of(n_vol):
    return list(range(0, n_vol, 2)) + list(range(n_vol - 1, 0, -2))


def extract_kernel(rows, planes_here, *refs):
    plane_ref, line_ref, weight_hbm, vol_hbm, keep_a, send_a = refs[:6]
    vol, pair, idx_v, flag_v, idx_s, flag_s, w_s, sem = refs[-8:]
    parts_b = refs[6:-8]
    slab = lax.axis_index("vol")
    share = idx_v.shape[0] // 2
    first = lax.axis_index("img") * share
    height = planes_here * ROWS
    count_z = keep_a.shape[0]
    groups_a = keep_a.shape[2] // 16
    groups_b = parts_b[0].shape[2] // 16
    load = pltpu.make_async_copy(vol_hbm, vol.at[:, :height, :], sem.at[0])
    load.start()
    loads_w = [
        pltpu.make_async_copy(
            weight_hbm.at[pl.ds(first, share), pl.ds(h * COLS, COLS)],
            w_s.at[pl.ds(h * share, share), :],
            sem.at[4 + h],
        )
        for h in range(2)
    ]
    for copy in loads_w:
        copy.start()
    local = plane_ref[pl.ds(first, share), :] - slab * planes_here
    owned = (local >= 0) & (local < planes_here)
    idx = jnp.where(owned, local * ROWS + line_ref[pl.ds(first, share), :], height)
    for h in range(2):
        idx_v[h * share : (h + 1) * share, :] = idx[:, h * COLS : (h + 1) * COLS]
    eights = (
        lax.broadcasted_iota(jnp.int32, (ROWS, COLS), 0) >> 3
        == lax.broadcasted_iota(jnp.int32, (ROWS, COLS), 1)
    )
    held = jnp.dot(
        owned.astype(F32).astype(BF16), eights.astype(F32).astype(BF16), preferred_element_type=F32
    )
    eight = lax.broadcasted_iota(jnp.int32, (COLS, COLS), 0)
    bits = jnp.where(
        eight >> 4 == lax.broadcasted_iota(jnp.int32, (COLS, COLS), 1), 1 << (eight & 15), 0
    )
    flag_v[...] = jnp.dot(
        (held > 0.0).astype(F32).astype(BF16),
        bits.astype(F32).astype(BF16),
        preferred_element_type=F32,
    ).astype(jnp.int32)
    to_idx = pltpu.make_async_copy(idx_v, idx_s, sem.at[2])
    to_flag = pltpu.make_async_copy(flag_v, flag_s, sem.at[3])
    to_idx.start()
    to_flag.start()
    vol[:, height : height + 8, :] = jnp.zeros((2, 8, COLS), F32)
    for ref in (keep_a, send_a) + parts_b:
        ref[...] = jnp.zeros_like(ref)
    to_idx.wait()
    to_flag.wait()
    for copy in loads_w:
        copy.wait()
    load.wait()
    lower_row = lax.broadcasted_iota(jnp.int32, (2, COLS), 0) == 0
    per_k = max(1, 16 // rows)
    per_block = max(1, rows // 16)
    run = min(rows, 16)

    def message(out, lead, k, words, r0, base):
        word = jnp.where(r0 >= COLS, words[1], words[0])
        lane = r0 & (COLS - 1)
        hits = (word >> (lane >> 3)) & ((1 << (run // 8)) - 1)

        @pl.when(hits > 0)
        def _():
            line = k + share * (r0 >> 7)
            for u in range(16):
                i = idx_s[line + u // run, lane + u % run]
                w = w_s[line + u // run, lane + u % run]
                both = jnp.where(lower_row, w, 1.0 - w)
                for j in range(2):
                    pair[j, 2 * u : 2 * u + 2, :] = both * vol[j, pl.ds(i, 2), :]
            for j in range(2):
                value = pair[j, pl.ds(0, 16, stride=2), :] + pair[j, pl.ds(1, 16, stride=2), :]
                out[lead, j, pl.ds(base, 16), :] = value.astype(BF16)

    places = []
    for dz in range(count_z):
        for dy in range(2):
            z = (slab >> 1) + dz
            block = jnp.where(z >= count_z, z - count_z, z) * 2 + ((slab + dy) & 1)
            places.append((dz, dy, block))
    share_a = keep_a.shape[2] // rows
    for k0, count in ((0, share_a), (share_a, share - share_a)):

        def turn(t, carry, k0=k0):
            k = k0 + t * per_k
            words = [flag_s[k, 0], flag_s[k, 1]]
            for i in range(1, per_k):
                words = [words[0] | flag_s[k + i, 0], words[1] | flag_s[k + i, 1]]
            for dz, dy, block in places:
                out, lead = ((keep_a, send_a)[dy], dz) if k0 == 0 else (parts_b[dz], dy)
                for g in range(per_block):
                    base = pl.multiple_of((t * per_block + g) * 16, 16)
                    message(out, lead, k, words, block * rows + 16 * g, base)
            return carry

        lax.fori_loop(0, count // per_k, turn, 0)


def extract(volume, row_plane, row_line, row_weight, n_vol, share, share_a):
    planes_here = volume.shape[1]
    rows = ROWS // n_vol
    count_z = n_vol // 2
    shape_a = jax.ShapeDtypeStruct((count_z, 2, share_a * rows, COLS), BF16)
    shape_b = jax.ShapeDtypeStruct((2, 2, (share - share_a) * rows, COLS), BF16)
    return pl.pallas_call(
        partial(extract_kernel, rows, planes_here),
        out_shape=[shape_a, shape_a] + [shape_b] * count_z,
        in_specs=[vmem(), vmem(), hbm(), hbm()],
        out_specs=[vmem()] * (2 + count_z),
        scratch_shapes=[
            pltpu.VMEM((2, planes_here * ROWS + 8, COLS), F32),
            pltpu.VMEM((2, 32, COLS), F32),
            pltpu.VMEM((2 * share, COLS), jnp.int32),
            pltpu.VMEM((share, COLS), jnp.int32),
            pltpu.SMEM((2 * share, COLS), jnp.int32),
            pltpu.SMEM((share, COLS), jnp.int32),
            pltpu.SMEM((2 * share, COLS), F32),
            pltpu.SemaphoreType.DMA((6,)),
        ],
        compiler_params=pltpu.CompilerParams(vmem_limit_bytes=VMEM_LIMIT),
        cost_estimate=cost(11),
        name="extract",
    )(row_plane, row_line, row_weight, volume.reshape(2, planes_here * ROWS, COLS))


def combine_first_kernel(keep_a, got_a, keep_b, *rest):
    count_z = keep_a.shape[0]
    got_b = rest[: count_z - 1]
    out_a = rest[count_z : 2 * count_z]
    out_b = rest[2 * count_z :]
    for d in range(count_z):
        out_a[d][...] = keep_a[d] + got_a[d]
    for d in range(2):
        total = keep_b[d]
        for ref in got_b:
            total = total + ref[d]
        out_b[d][...] = total


def to_pixel_rows(messages, n_vol, first_with):
    keep_a, send_a, keep_b = messages[:3]
    count_z = n_vol // 2
    got_b = [lax.ppermute(m, "vol", along_z(n_vol, d + 1)) for d, m in enumerate(messages[3:])]
    got_a = lax.ppermute(send_a, "vol", flip(n_vol, 1))
    shape_a = jax.ShapeDtypeStruct(keep_a.shape[1:], BF16)
    shape_b = jax.ShapeDtypeStruct(keep_b.shape[1:], BF16)
    sums = pl.pallas_call(
        combine_first_kernel,
        out_shape=[shape_a] * count_z + [shape_b] * 2,
        in_specs=[vmem()] * (2 + count_z) + [hbm()],
        out_specs=[vmem()] * (count_z + 2),
        compiler_params=pltpu.CompilerParams(vmem_limit_bytes=VMEM_LIMIT),
        cost_estimate=cost(3),
        name="combine_first",
    )(keep_a, got_a, keep_b, *got_b, first_with)
    sums_a, sums_b = sums[:count_z], sums[count_z:]
    moved_b = lax.ppermute(sums_b[1], "vol", flip(n_vol, 1))
    moved = [lax.ppermute(sums_a[d], "vol", along_z(n_vol, d)) for d in range(1, count_z)]
    out_b = sums_b[0] + moved_b
    out_a = sum(moved, sums_a[0])
    return out_a, out_b


def from_partners(x, n_img):
    return [x] + [lax.ppermute(x, "img", flip(n_img, m)) for m in range(1, n_img)]


def ring_gather(low, high, n_vol):
    ring = ring_of(n_vol)
    ahead = [(ring[p], ring[(p + 1) % n_vol]) for p in range(n_vol)]
    back = [(b, a) for a, b in ahead]
    pieces = [low, high]
    one = two = (low, high)
    for _ in range(1, n_vol // 2):
        one_low, two_low = lax.ppermute(one[0], "vol", ahead), lax.ppermute(two[0], "vol", back)
        one_high, two_high = lax.ppermute(one[1], "vol", ahead), lax.ppermute(two[1], "vol", back)
        one, two = (one_low, one_high), (two_low, two_high)
        pieces += [*one, *two]
    return pieces + [lax.ppermute(one[0], "vol", ahead), lax.ppermute(two[1], "vol", back)]


def weigh_kernel(img_ref, sa_ref, ca_ref, sx_ref, cx_ref, nw_ref, wt_ref, sq_ref, buf):
    count = img_ref.shape[1]
    rows = img_ref.shape[2]
    pitch = rows + 1
    for j in range(2):
        for b in range(count):
            buf[j, b * pitch : b * pitch + rows, :] = img_ref[j, b].astype(F32)
    sx = sx_ref[...]
    cx = cx_ref[...]
    for r in range(rows):
        contrast = -(sa_ref[:, r : r + 1] * cx + ca_ref[:, r : r + 1] * sx)
        noise = nw_ref[r : r + 1, :]
        scale = contrast * noise
        for j in range(2):
            x = buf[j, pl.ds(r, count, stride=pitch), :]
            wt_ref[r, :, j * COLS : (j + 1) * COLS] = (scale * x).astype(BF16)
        sq_ref[r] = (contrast * contrast * noise).astype(BF16)


def weigh(images, defocus, noise_weight, row_freq, col_freq):
    count = images.shape[1]
    rows = images.shape[2]
    step = 64
    angle_r = defocus[:, None] * (row_freq * row_freq)[None, :] + math.asin(AMPLITUDE)
    angle_c = defocus[:, None] * (col_freq * col_freq)[None, :]
    return pl.pallas_call(
        weigh_kernel,
        grid=(count // step,),
        out_shape=[
            jax.ShapeDtypeStruct((rows, count, 2 * COLS), BF16),
            jax.ShapeDtypeStruct((rows, count, COLS), BF16),
        ],
        in_specs=[
            pl.BlockSpec((2, step, rows, COLS), lambda b: (0, b, 0, 0)),
            pl.BlockSpec((step, rows), lambda b: (b, 0)),
            pl.BlockSpec((step, rows), lambda b: (b, 0)),
            pl.BlockSpec((step, COLS), lambda b: (b, 0)),
            pl.BlockSpec((step, COLS), lambda b: (b, 0)),
            pl.BlockSpec((rows, COLS), lambda b: (0, 0)),
        ],
        out_specs=[
            pl.BlockSpec((rows, step, 2 * COLS), lambda b: (0, b, 0)),
            pl.BlockSpec((rows, step, COLS), lambda b: (0, b, 0)),
        ],
        scratch_shapes=[pltpu.VMEM((2, step * (rows + 1), COLS), F32)],
        compiler_params=params(1),
        cost_estimate=cost(12),
        name="weigh",
    )(
        images,
        jnp.sin(angle_r),
        jnp.cos(angle_r),
        jnp.sin(angle_c),
        jnp.cos(angle_c),
        noise_weight,
    )


def logits_kernel(wt_ref, sq_ref, cos_ref, sin_ref, cand_ref, *rest):
    sl_refs = rest[1:-4]
    out_ref, part, acc, quad = rest[-4:]
    step = pl.program_id(0)
    groups = len(sl_refs) // 2
    rows = part.shape[1] // K - 1
    share = K // groups
    pitch = rows + 1
    inner = wt_ref.shape[0]

    @pl.when(step == 0)
    def _():
        for m in range(groups):
            at = m * share
            for ref in sl_refs[2 * m : 2 * m + 2]:
                for j in range(2):
                    for k in range(ref.shape[1] // rows):
                        row = (at + k) * pitch
                        part[j, row : row + rows, :] = ref[j, k * rows : (k + 1) * rows].astype(F32)
                at += ref.shape[1] // rows
        acc[...] = jnp.zeros_like(acc)
        quad[...] = jnp.zeros_like(quad)

    dims = (((1,), (1,)), ((), ()))
    total = acc[...]
    total_q = quad[...]
    left, power = [], []
    for u in range(inner):
        re = part[0, pl.ds(step * inner + u, K, stride=pitch), :]
        im = part[1, pl.ds(step * inner + u, K, stride=pitch), :]
        shifted = []
        for t in range(TRANS):
            c = cos_ref[t, u : u + 1, :]
            s = sin_ref[t, u : u + 1, :]
            shifted.append(
                jnp.concatenate(
                    [(c * re - s * im).astype(BF16), (s * re + c * im).astype(BF16)], axis=1
                )
            )
        left.append(jnp.concatenate(shifted, axis=0))
        power.append((re * re + im * im).astype(BF16))
        if u % 4 == 3:
            right = jnp.concatenate([wt_ref[i] for i in range(u - 3, u + 1)], axis=1)
            right_q = jnp.concatenate([sq_ref[i] for i in range(u - 3, u + 1)], axis=1)
            total = total + lax.dot_general(
                jnp.concatenate(left, axis=1), right, dims, preferred_element_type=F32
            )
            total_q = total_q + lax.dot_general(
                jnp.concatenate(power, axis=1), right_q, dims, preferred_element_type=F32
            )
            left, power = [], []
    acc[...] = total
    quad[...] = total_q

    @pl.when(step == pl.num_programs(0) - 1)
    def _():
        ids = lax.broadcasted_iota(jnp.int32, quad.shape, 0) ^ (lax.axis_index("img") * share)
        half = 0.5 * quad[...]
        for t in range(TRANS):
            value = acc[t * K : (t + 1) * K, :] - half
            for l in range(LMAX):
                pick = jnp.where(ids == cand_ref[l : l + 1, :], value, 0.0)
                out_ref[t * LMAX + l : t * LMAX + l + 1, :] = jnp.sum(pick, axis=0, keepdims=True)


def candidate_logits(after, slices, weighted, squared, cosine, sine, cand):
    rows, count = squared.shape[:2]
    inner = 8
    return pl.pallas_call(
        logits_kernel,
        grid=(rows // inner,),
        out_shape=jax.ShapeDtypeStruct((TRANS * LMAX, count), F32),
        in_specs=[
            pl.BlockSpec((inner, count, 2 * COLS), lambda s: (s, 0, 0)),
            pl.BlockSpec((inner, count, COLS), lambda s: (s, 0, 0)),
            pl.BlockSpec((TRANS, inner, COLS), lambda s: (0, s, 0)),
            pl.BlockSpec((TRANS, inner, COLS), lambda s: (0, s, 0)),
            pl.BlockSpec((LMAX, count), lambda s: (0, 0)),
        ]
        + [hbm()]
        + [pl.BlockSpec(x.shape, lambda s: (0, 0, 0)) for x in slices],
        out_specs=pl.BlockSpec((TRANS * LMAX, count), lambda s: (0, 0)),
        scratch_shapes=[
            pltpu.VMEM((2, K * (rows + 1), COLS), F32),
            pltpu.VMEM((TRANS * K, count), F32),
            pltpu.VMEM((K, count), F32),
        ],
        compiler_params=params(1),
        cost_estimate=cost(8),
        name="logits",
    )(weighted, squared, cosine, sine, cand, after, *slices)


def posterior_rows(logits, counts):
    place = lax.broadcasted_iota(jnp.int32, logits.shape, 0) % LMAX
    allowed = place < counts
    masked = jnp.where(allowed, logits, -1e30)
    highest = jnp.max(masked, axis=0, keepdims=True)
    exponent = jnp.where(allowed, jnp.exp(masked - highest), 0.0)
    return (exponent / jnp.sum(exponent, axis=0, keepdims=True)).astype(BF16).astype(F32)


def list_rows(num, src_s, len_s, outs, pick):
    parts = 2 * outs[0].shape[0]
    cap = outs[0].shape[2]
    comps = num.shape[0]
    lead = src_s.shape[0] // parts
    group = lax.axis_index("img")
    for m in range(parts):
        q = group ^ m

        def turn(g, carry, q=q, m=m):
            base = pl.multiple_of(g * 32, 32)
            at = q * lead + base
            for u in range(32):
                s = src_s[at + u]
                for c in range(comps):
                    pick[c, u : u + 1, :] = num[c, pl.ds(s, 1), :]
            for c in range(comps):
                outs[m % 2][m // 2, c, pl.ds(base, 32), :] = pick[c].astype(BF16)
            return carry

        lax.fori_loop(0, (jnp.minimum(len_s[q, 0], cap) + 31) // 32, turn, 0)


def project_kernel(src_s, len_s, cand_ref, cnt_ref, wt_ref, sq_ref, cos_ref, sin_ref, *rest):
    lg_refs = rest[:-6]
    keep_ref, send_ref, post, post_sum, num, pick = rest[-6:]
    step = pl.program_id(0)
    inner = wt_ref.shape[0]

    @pl.when(step == 0)
    def _():
        prob = posterior_rows(sum([ref[...] for ref in lg_refs[1:]], lg_refs[0][...]), cnt_ref[...])
        ids = lax.broadcasted_iota(jnp.int32, (K, prob.shape[1]), 0)
        total = jnp.zeros((K, prob.shape[1]), F32)
        for t in range(TRANS):
            dense = jnp.zeros((K, prob.shape[1]), F32)
            for l in range(LMAX):
                at = t * LMAX + l
                dense = jnp.where(ids == cand_ref[l : l + 1, :], dense + prob[at : at + 1, :], dense)
            post[t * K : (t + 1) * K, :] = dense.astype(BF16)
            total = total + dense
        high = total.astype(BF16)
        post_sum[:K, :] = high
        post_sum[K:, :] = (total - high.astype(F32)).astype(BF16)

    for u in range(inner):
        y = jnp.dot(post[...], wt_ref[u], preferred_element_type=F32)
        d = jnp.dot(post_sum[...], sq_ref[u], preferred_element_type=F32)
        re = jnp.zeros((K, COLS), F32)
        im = jnp.zeros((K, COLS), F32)
        for t in range(TRANS):
            c = cos_ref[t, u : u + 1, :]
            s = sin_ref[t, u : u + 1, :]
            y_re = y[t * K : (t + 1) * K, :COLS]
            y_im = y[t * K : (t + 1) * K, COLS:]
            re = re + (c * y_re + s * y_im)
            im = im + (c * y_im - s * y_re)
        base = pl.multiple_of((step * inner + u) * K, K)
        num[0, pl.ds(base, K), :] = re
        num[1, pl.ds(base, K), :] = im
        num[2, pl.ds(base, K), :] = d[:K] + d[K:]

    @pl.when(step == pl.num_programs(0) - 1)
    def _():
        list_rows(num, src_s, len_s, (keep_ref, send_ref), pick)


def project(src, lengths, n_img, logits, cand, counts, weighted, squared, cosine, sine, cap):
    rows, count = squared.shape[:2]
    inner = 8
    shape = (n_img // 2, 3, cap, COLS)
    return pl.pallas_call(
        project_kernel,
        grid=(rows // inner,),
        out_shape=[jax.ShapeDtypeStruct(shape, BF16)] * 2,
        in_specs=[
            smem(),
            smem(),
            pl.BlockSpec((LMAX, count), lambda s: (0, 0)),
            pl.BlockSpec((1, count), lambda s: (0, 0)),
            pl.BlockSpec((inner, count, 2 * COLS), lambda s: (s, 0, 0)),
            pl.BlockSpec((inner, count, COLS), lambda s: (s, 0, 0)),
            pl.BlockSpec((TRANS, inner, COLS), lambda s: (0, s, 0)),
            pl.BlockSpec((TRANS, inner, COLS), lambda s: (0, s, 0)),
        ]
        + [pl.BlockSpec((TRANS * LMAX, count), lambda s: (0, 0)) for _ in logits],
        out_specs=[pl.BlockSpec(shape, lambda s: (0, 0, 0, 0))] * 2,
        scratch_shapes=[
            pltpu.VMEM((TRANS * K, count), BF16),
            pltpu.VMEM((2 * K, count), BF16),
            pltpu.VMEM((3, rows * K, COLS), F32),
            pltpu.VMEM((3, 32, COLS), F32),
        ],
        compiler_params=params(1),
        cost_estimate=cost(12),
        name="project",
    )(src, lengths, cand, counts, weighted, squared, cosine, sine, *logits)


def to_member(keep, send, n_img):
    got = lax.ppermute(send, "img", flip(n_img, 1))
    half = keep.shape[2] // 2
    owns = []
    for h in range(2):
        cut = slice(h * half, (h + 1) * half)
        summed = [keep[m, :, cut] + got[m, :, cut] for m in range(n_img // 2)]
        moved = [lax.ppermute(summed[m], "img", flip(n_img, 2 * m)) for m in range(1, n_img // 2)]
        owns.append(added(summed[0], *moved))
    return owns


def added_kernel(*refs):
    total = refs[0][...]
    for ref in refs[1:-1]:
        total = total + ref[...]
    refs[-1][...] = total


def added(*terms):
    return pl.pallas_call(
        added_kernel,
        out_shape=jax.ShapeDtypeStruct(terms[0].shape, terms[0].dtype),
        in_specs=[vmem()] * len(terms),
        out_specs=vmem(),
        compiler_params=pltpu.CompilerParams(vmem_limit_bytes=VMEM_LIMIT),
        cost_estimate=cost(1),
        name="added",
    )(*terms)


HEAD = 8


def line_stride(lines_here):
    return lines_here + 2 * HEAD


def insert_kernel(count, len_s, code_hbm, wgt_hbm, reg_hbm, *rest):
    pieces = rest[:count]
    out_hbm = rest[count]
    code_s, wgt_s, held, reg, out, acc, acc_odd, buf, sem_in, sem_piece, sem_out = rest[count + 1 :]
    both_acc = (acc, acc_odd)
    cap = buf.shape[1]
    half = cap // 2
    blocks = len_s.shape[0]
    lead = code_s.shape[0] // blocks
    planes, lines_here = reg.shape[:2]
    stride = line_stride(lines_here)
    slab = lax.axis_index("vol")
    place = jnp.where(slab & 1, blocks - 1 - (slab >> 1), slab >> 1)
    tables = [
        pltpu.make_async_copy(code_hbm, code_s, sem_in.at[0]),
        pltpu.make_async_copy(wgt_hbm, wgt_s, sem_in.at[1]),
    ]
    prior = pltpu.make_async_copy(reg_hbm, reg, sem_in.at[2])
    loads = [
        pltpu.make_async_copy(pieces[i], held.at[i], sem_piece.at[i]) for i in range(count)
    ]
    for copy in tables + loads + [prior]:
        copy.start()
    acc[...] = jnp.zeros_like(acc)
    acc_odd[...] = jnp.zeros_like(acc_odd)
    first = lax.broadcasted_iota(jnp.int32, (2, COLS), 0) == 0
    for copy in tables:
        copy.wait()
    for m in range(count // 2):
        for h in range(2):
            loads[2 * m + h].wait()
            for c in range(3):
                buf[c, h * half : (h + 1) * half, :] = held[2 * m + h, c].astype(F32)
        from_place = place + ((m + 1) // 2) * (-1 if m % 2 else 1)
        from_place = from_place & (blocks - 1)
        block = jnp.where(
            from_place >= blocks // 2, 2 * (blocks - 1 - from_place) + 1, 2 * from_place
        )

        def group_step(g, carry, block=block):
            at = block * lead + g * 8
            for u in range(8):
                code = code_s[at + u]
                s = code & 1023
                to = code >> 10
                w = wgt_s[at + u]
                both = jnp.where(first, w, 1.0 - w)
                into = both_acc[u % 2]
                for c in range(3):
                    row = jnp.broadcast_to(buf[c, pl.ds(s, 1), :], (2, COLS))
                    into[c, pl.ds(to, 2), :] = into[c, pl.ds(to, 2), :] + both * row
            return carry

        lax.fori_loop(0, (jnp.minimum(len_s[block, 0], cap) + 7) // 8, group_step, 0)

    prior.wait()
    chunks = sem_out.shape[0]
    span = planes // chunks
    stores = []
    for i in range(chunks):

        def plane_step(p, carry):
            base = pl.multiple_of(p * stride + HEAD, 8)
            total = [
                acc[c, pl.ds(base, lines_here), :] + acc_odd[c, pl.ds(base, lines_here), :]
                for c in range(3)
            ]
            inverse = 1.0 / (total[2] + reg[p])
            out[0, p] = total[0] * inverse
            out[1, p] = total[1] * inverse
            return carry

        lax.fori_loop(i * span, (i + 1) * span, plane_step, 0)
        part = pl.ds(i * span, span)
        stores.append(pltpu.make_async_copy(out.at[:, part], out_hbm.at[:, part], sem_out.at[i]))
        stores[-1].start()
    for copy in stores:
        copy.wait()


def insert(lengths, code, weights, pieces, regularizer):
    half = pieces[0].shape[1]
    planes, lines_here = regularizer.shape[:2]
    count = len(pieces)
    chunks = 4
    acc = pltpu.VMEM((3, planes * line_stride(lines_here), COLS), F32)
    result = (2, planes, lines_here, COLS)
    return pl.pallas_call(
        partial(insert_kernel, count),
        out_shape=jax.ShapeDtypeStruct(result, F32),
        in_specs=[smem()] + [hbm()] * (3 + count),
        out_specs=hbm(),
        scratch_shapes=[
            pltpu.SMEM(code.shape, jnp.int32),
            pltpu.SMEM(weights.shape, F32),
            pltpu.VMEM((count, 3, half, COLS), BF16),
            pltpu.VMEM(regularizer.shape, F32),
            pltpu.VMEM(result, F32),
            acc,
            acc,
            pltpu.VMEM((3, 2 * half, COLS), F32),
            pltpu.SemaphoreType.DMA((3,)),
            pltpu.SemaphoreType.DMA((count,)),
            pltpu.SemaphoreType.DMA((chunks,)),
        ],
        compiler_params=pltpu.CompilerParams(vmem_limit_bytes=VMEM_LIMIT),
        cost_estimate=cost(9),
        name="insert",
    )(lengths, code, weights, regularizer, *pieces)


def running(x):
    lanes = lax.broadcasted_iota(jnp.int32, x.shape, 1)
    step = 1
    while step < x.shape[1]:
        x = x + jnp.where(lanes >= step, pltpu.roll(x, step, 1), 0)
        step *= 2
    return x


def split_index(x):
    return [(x >> 5).astype(F32), (x & 31).astype(F32)]


def split_weight(w):
    a = w.astype(BF16).astype(F32)
    b = (w - a).astype(BF16).astype(F32)
    return [a, b, w - a - b]


def compacted(member, rank, values, lead):
    high = jnp.where(member, rank >> 5, -1)
    low = rank & 31
    spot = lax.broadcasted_iota(jnp.int32, (4 * lead, rank.shape[1]), 0)
    shift = lead.bit_length() - 1
    left = ((spot & (lead - 1)) * 4 + (spot >> shift)) == high
    hot = lax.broadcasted_iota(jnp.int32, (32, rank.shape[1]), 0) == low
    right = jnp.concatenate([jnp.where(hot, v, 0.0).astype(BF16) for v in values], axis=0)
    out = lax.dot_general(
        left.astype(F32).astype(BF16), right, (((1,), (1,)), ((), ())), preferred_element_type=F32
    )
    return [
        jnp.concatenate(
            [out[h * lead : (h + 1) * lead, 32 * i : 32 * (i + 1)] for h in range(4)], axis=1
        )
        for i in range(len(values))
    ]


def lists_kernel(
    n_img, planes_here, lines_here, cap,
    plane_ref, line_ref, wgt_ref,
    src_ref, code_ref, w_ref, send_len, recv_len, longest, own,
):
    slab = lax.axis_index("vol")
    group = lax.axis_index("img")
    blocks, number = line_ref.shape
    lead = src_ref.shape[0] // n_img
    lines = line_ref[...]

    def in_part(x, part):
        return (x >= part * lines_here - 1) & (x < (part + 1) * lines_here)

    top = jnp.zeros((blocks, COLS), jnp.int32)
    for q in range(n_img):
        size = jnp.sum(in_part(lines, q).astype(F32), axis=1, keepdims=True).astype(jnp.int32)
        top = jnp.maximum(top, jnp.broadcast_to(size, (blocks, COLS)))
    longest[...] = jnp.broadcast_to(jnp.max(top.astype(F32)), (8, COLS)).astype(jnp.int32)

    own[...] = jnp.broadcast_to(line_ref[pl.ds(slab, 1), :], own.shape)
    sent = in_part(own[...], lax.broadcasted_iota(jnp.int32, own.shape, 0))
    total = running(sent.astype(jnp.int32))
    send_len[...] = jnp.broadcast_to(total[:, number - 1 :], send_len.shape)
    rank = total - sent.astype(jnp.int32)
    row_ids = split_index(lax.broadcasted_iota(jnp.int32, (1, number), 1))
    for q in range(n_img):
        out = compacted(sent[q : q + 1], rank[q : q + 1], row_ids, lead)
        src_ref[q * lead : (q + 1) * lead, :] = (32.0 * out[0] + out[1]).astype(jnp.int32)

    member = in_part(lines, group)
    place = running(member.astype(jnp.int32)) - member.astype(jnp.int32)
    place = jnp.minimum(place, cap - 1)
    local = plane_ref[...] - slab * planes_here
    here = member & (local >= 0) & (local < planes_here)
    total = running(here.astype(jnp.int32))
    recv_len[...] = jnp.broadcast_to(total[:, number - 1 :], recv_len.shape)
    rank = total - here.astype(jnp.int32)
    target = local * line_stride(lines_here) + lines - group * lines_here + HEAD
    target = jnp.where(here, target, 0)
    for v in range(blocks):
        row = slice(v, v + 1)
        values = split_index(place[row]) + split_index(target[row]) + split_weight(wgt_ref[row, :])
        out = compacted(here[row], rank[row], values, lead)
        at = slice(v * lead, (v + 1) * lead)
        code_ref[at, :] = (
            32768.0 * out[2] + 1024.0 * out[3] + 32.0 * out[0] + out[1]
        ).astype(jnp.int32)
        w_ref[at, :] = out[4] + out[5] + out[6]


def lists(row_plane, row_line, row_weight, n_vol, n_img, planes_here, lines_here, cap):
    lead = 8
    assert cap <= lead * COLS
    number = ROWS // n_vol * K

    def order(x):
        return x.T.reshape(n_vol, number)

    def table(blocks, dtype=jnp.int32):
        return jax.ShapeDtypeStruct((blocks * lead, COLS), dtype)

    return pl.pallas_call(
        partial(lists_kernel, n_img, planes_here, lines_here, cap),
        out_shape=[
            table(n_img),
            table(n_vol),
            table(n_vol, F32),
            jax.ShapeDtypeStruct((8, COLS), jnp.int32),
            jax.ShapeDtypeStruct((n_vol, COLS), jnp.int32),
            jax.ShapeDtypeStruct((8, COLS), jnp.int32),
        ],
        in_specs=[vmem()] * 3,
        out_specs=[vmem()] * 6,
        scratch_shapes=[pltpu.VMEM((8, number), jnp.int32)],
        compiler_params=pltpu.CompilerParams(vmem_limit_bytes=VMEM_LIMIT),
        cost_estimate=cost(6),
        name="lists",
    )(order(row_plane), order(row_line), order(row_weight))


def insert_into(carry, piece, planes_all, lines_all, weights_all, slab_id, planes_here):
    local_plane = planes_all - slab_id * planes_here
    in_slab = (local_plane >= 0) & (local_plane < planes_here)
    dump_row = planes_here * ROWS
    lower_index = jnp.where(in_slab, local_plane * ROWS + lines_all, dump_row).reshape(-1)
    upper_index = jnp.where(in_slab, lower_index.reshape(in_slab.shape) + 1, dump_row).reshape(-1)
    values = piece.reshape(-1, 3 * COLS)
    weight = weights_all.reshape(-1, 1)
    carry = carry.at[lower_index].add(weight * values)
    return carry.at[upper_index].add((1.0 - weight) * values)


def dense_path(
    logits, cand, counts, weighted, squared, cosine, sine,
    plane_share, line_share, weight_share, regularizer, slab_id,
):
    prob = posterior_rows(logits, counts).reshape(TRANS, LMAX, -1)
    hot = (cand[:, None, :] == jnp.arange(K)[None, :, None]).astype(F32)
    post = jnp.einsum("tlb,lkb->tkb", prob, hot).astype(BF16)
    y = jnp.einsum("tkb,rbz->tkrz", post, weighted, preferred_element_type=F32)
    d = jnp.einsum("tkb,rbc->krc", post, squared, preferred_element_type=F32)
    y_re = y[..., :COLS]
    y_im = y[..., COLS:]
    num_re = jnp.sum(cosine[:, None] * y_re + sine[:, None] * y_im, axis=0)
    num_im = jnp.sum(cosine[:, None] * y_im - sine[:, None] * y_re, axis=0)
    partial_value = lax.psum_scatter(
        jnp.stack([num_re, num_im, d], axis=2), "img", scatter_dimension=0, tiled=True
    )
    planes_here = regularizer.shape[0]
    inserted = insert_into(
        jnp.zeros((planes_here * ROWS + 1, 3 * COLS), F32),
        lax.all_gather(partial_value, "vol", axis=1, tiled=True),
        plane_share,
        line_share,
        weight_share,
        slab_id,
        planes_here,
    )
    slab = inserted[: planes_here * ROWS].reshape(planes_here, ROWS, 3, COLS)
    summed = lax.psum_scatter(slab, "img", scatter_dimension=1, tiled=True)
    denom = summed[:, :, 2] + regularizer
    return jnp.stack([summed[:, :, 0] / denom, summed[:, :, 1] / denom], axis=0)


def body(
    images, defocus, candidates, counts, noise_weight, volume,
    row_plane, row_line, row_weight, regularizer,
):
    rows = noise_weight.shape[0]
    planes_here = volume.shape[1]
    lines_here = regularizer.shape[1]
    slab_id = lax.axis_index("vol")
    group_id = lax.axis_index("img")
    n_vol = lax.axis_size("vol")
    n_img = lax.axis_size("img")
    global_rows = slab_id * rows + jnp.arange(rows)
    row_freq = (global_rows.astype(F32) - ROWS // 2) / ROWS
    col_freq = jnp.arange(COLS).astype(F32) / (2 * COLS)
    share = K // n_img
    first = group_id * share
    plane_share = lax.dynamic_slice_in_dim(row_plane, first, share, 0)
    line_share = lax.dynamic_slice_in_dim(row_line, first, share, 0)
    weight_share = lax.dynamic_slice_in_dim(row_weight, first, share, 0)

    aligned = max(1, 16 // rows)
    share_a = share * 11 // 16 // aligned * aligned
    messages = extract(volume, row_plane, row_line, row_weight, n_vol, share, share_a)
    cosine, sine = shift_phases(row_freq, col_freq, TRANS)
    weighted, squared = weigh(images, defocus, noise_weight, row_freq, col_freq)
    mean = rows * K // n_img
    cap = -(-int(mean + 4.2 * math.sqrt(mean)) // 32) * 32
    src, code, wgt, send_len, recv_len, longest = lists(
        row_plane, row_line, row_weight, n_vol, n_img, planes_here, lines_here, cap
    )
    own_a, own_b = to_pixel_rows(messages, n_vol, weighted)
    slices_b = from_partners(own_b, n_img)
    slices_a = from_partners(own_a, n_img)
    slices = [x for both in zip(slices_a, slices_b) for x in both]
    cand = candidates.T
    count_row = counts[None, :]
    partial_logits = candidate_logits(code, slices, weighted, squared, cosine, sine, cand)
    pair_logits = partial_logits + lax.ppermute(partial_logits, "vol", flip(n_vol, 1))
    logits = [pair_logits] + [
        lax.ppermute(pair_logits, "vol", along_z(n_vol, d)) for d in range(1, n_vol // 2)
    ]

    keep, send = project(
        src.reshape(-1), send_len, n_img, logits, cand, count_row, weighted, squared, cosine, sine, cap
    )
    low, high = to_member(keep, send, n_img)
    pieces = ring_gather(low, high, n_vol)

    def listed():
        return insert(recv_len, code.reshape(-1), wgt.reshape(-1), pieces, regularizer)

    def dense():
        return dense_path(
            sum(logits[1:], logits[0]), cand, count_row, weighted, squared, cosine, sine,
            plane_share, line_share, weight_share, regularizer, slab_id,
        )

    return lax.cond(longest[0, 0] <= cap, listed, dense)


def solution(mesh):
    return jax.shard_map(
        body,
        mesh=mesh,
        in_specs=(
            P(None, "img", "vol", None),
            P("img"),
            P("img", None),
            P("img"),
            P("vol", None),
            P(None, "vol", None, None),
            P(),
            P(),
            P(),
            P("vol", "img", None),
        ),
        out_specs=P(None, "vol", "img", None),
        check_vma=False,
    )
```
